128 devices in a mesh: tm: 32 (over y_hi, z, x), chan: 4 (over y_lo, core).
Axes of the slice: x: 4, y: 4 (y_hi: 2, y_lo: 2; y = y_hi * 2 + y_lo), z: 4, core: 2. Of those that a mesh axis runs over, the one named last changes fastest.
Arguments:
- signal: bfloat16 [128, 131072], P('chan', 'tm'), may hold values from -6 to 6
- cotangent: bfloat16 [128, 131072], P('chan', 'tm'), may hold values from -6 to 6
- log_step: float32 [128], P('chan'), may hold values from -5.8 to -3.5
- damping: float32 [128, 32], P('chan'), may hold values from 0.001 to 3
- frequency: float32 [128, 32], P('chan'), may hold values from 0.05 to 0.5
- coef_re: float32 [128, 32], P('chan'), may hold values from -0.9 to 0.9
- coef_im: float32 [128, 32], P('chan'), may hold values from -0.9 to 0.9
- skip_gain: float32 [128], P('chan'), may hold values from -3 to 3
- mix_weight: bfloat16 [128, 128], P('chan'), may hold values from -0.5 to 0.5
- embed_table: float32 [200, 128], P(None, 'chan'), may hold values from -1.8 to 1.8
- diffusion_step: int32 [1], replicated, may hold values from 0 to 199
Outputs:
- grad_signal: bfloat16 [128, 131072], P('chan', 'tm')
- grad_kernel: float32 [128, 131072], P('chan', 'tm')
- grad_log_step: float32 [128], P('chan')
- grad_damping: float32 [128, 32], P('chan')
- grad_frequency: float32 [128, 32], P('chan')
- grad_coef_re: float32 [128, 32], P('chan')
- grad_coef_im: float32 [128, 32], P('chan')
- grad_skip: float32 [128], P('chan')
- grad_mix: float32 [128, 128], P('chan')
- grad_table: float32 [200, 128], P(None, 'chan')
The draws below stay inside these ranges and needn't reach their ends.
All inputs are finite; a program needn't handle non-finite values.
Results may differ from the reference program's by a relative error of at most 0.0034.
Values may be sent and summed in bfloat16 or wider, within the bound.
No kernel may reach another device: no remote copies, remote signals or barrier semaphores. Data moves between devices by JAX's collectives and lax.ppermute only.
A program may use at most 128 MiB of HBM per device.

```python
import math
import jax
import jax.numpy as jnp
from jax import lax

CHANNELS = 128
NUM_MODES = 32
DIFF_STEPS = 200
SAMPLES = 131072


def level_of(stream_key, dims, cuts, least, largest):
    factor_of = 1.0
    for position, shards_of in cuts:
        steps = jax.random.uniform(jax.random.fold_in(jax.random.fold_in(stream_key, 6), position), (shards_of,), jnp.float32, least / len(cuts), largest / len(cuts))
        factor_of = factor_of * jnp.repeat(jnp.exp(steps), dims[position] // shards_of).reshape((-1,) + (1,) * (len(dims) - 1 - position))
    return factor_of


def bell_draw(key, shape, scale, limit, cuts=(), held_as=jnp.bfloat16):
    result = jax.random.normal(key, shape, jnp.float32) * scale
    if len(cuts) > 0:
        result = level_of(key, shape, cuts, -0.22, 0.18) * result
    return jnp.clip(result, min=-limit, max=limit).astype(held_as)


def setup_inputs(seed: int = 0) -> dict:
    arg_keys = jax.random.split(jax.random.key(seed), 12)
    return {
        "signal": bell_draw(arg_keys[0], (CHANNELS, SAMPLES), 1.0, 6.0, ((0, 4), (1, 32))),
        "cotangent": bell_draw(arg_keys[1], (CHANNELS, SAMPLES), 1.0, 6.0, ((0, 4), (1, 32))),
        "log_step": jnp.clip(-5.8 + 2.3000002 * jax.random.uniform(arg_keys[2], (CHANNELS,), jnp.float32) ** level_of(arg_keys[2], (CHANNELS,), ((0, 4),), -0.2, 0.2), -5.8, -3.5),
        "damping": jnp.clip(jnp.exp(math.log(3.0) - 8.006368 * jax.random.uniform(arg_keys[3], (CHANNELS, NUM_MODES), jnp.float32) ** level_of(arg_keys[3], (CHANNELS, NUM_MODES), ((0, 4),), -0.2, 0.2)), 0.001, 3.0),
        "frequency": jnp.clip(jnp.exp(math.log(0.5) - 2.3025851 * jax.random.uniform(arg_keys[4], (CHANNELS, NUM_MODES), jnp.float32) ** level_of(arg_keys[4], (CHANNELS, NUM_MODES), ((0, 4),), -0.2, 0.2)), 0.05, 0.5),
        "coef_re": bell_draw(arg_keys[5], (CHANNELS, NUM_MODES), 0.15, 0.9, ((0, 4),), jnp.float32),
        "coef_im": bell_draw(arg_keys[6], (CHANNELS, NUM_MODES), 0.15, 0.9, ((0, 4),), jnp.float32),
        "skip_gain": bell_draw(arg_keys[7], (CHANNELS,), 0.5, 3.0, ((0, 4),), jnp.float32),
        "mix_weight": bell_draw(arg_keys[8], (CHANNELS, CHANNELS), CHANNELS ** -0.5, 0.5, ((0, 4),)),
        "embed_table": bell_draw(arg_keys[9], (DIFF_STEPS, CHANNELS), 0.3, 1.8, ((1, 4),), jnp.float32),
        "diffusion_step": jax.random.randint(arg_keys[10], (1,), 0, DIFF_STEPS).astype(jnp.int32),
    }


def mode_terms(log_step, damping, frequency, coef_re, coef_im):
    step_size = jnp.exp(log_step)[:, None]
    decay_rate = step_size * damping
    turn_rate = step_size * frequency
    half_sine = jnp.sin(0.5 * turn_rate)
    grow_real = jnp.expm1(-decay_rate) * jnp.cos(turn_rate) - 2.0 * half_sine * half_sine
    grow_imag = jnp.exp(-decay_rate) * jnp.sin(turn_rate)
    spread = damping * damping + frequency * frequency
    hold_real = (frequency * grow_imag - damping * grow_real) / spread
    hold_imag = -(frequency * grow_real + damping * grow_imag) / spread
    weight_real = coef_re * hold_real - coef_im * hold_imag
    weight_imag = coef_re * hold_imag + coef_im * hold_real
    return (decay_rate, turn_rate, weight_real, weight_imag)

def channel_kernel(log_step, damping, frequency, coef_re, coef_im):
    decay_rate, turn_rate, weight_real, weight_imag = mode_terms(log_step[None], damping[None], frequency[None], coef_re[None], coef_im[None])
    positions = jnp.arange(SAMPLES, dtype=jnp.float32)
    decayed = jnp.exp(-decay_rate[0][:, None] * positions)
    turned = turn_rate[0][:, None] * positions
    pieces = decayed * (weight_real[0][:, None] * jnp.cos(turned) - weight_imag[0][:, None] * jnp.sin(turned))
    return 2.0 * lax.optimization_barrier(jnp.sum(pieces, axis=0))

def reference(signal, cotangent, log_step, damping, frequency, coef_re, coef_im, skip_gain, mix_weight, embed_table, diffusion_step):
    padded = 2 * SAMPLES
    embed_row = lax.dynamic_slice_in_dim(embed_table, diffusion_step[0], 1, 0)[0]
    inputs = signal.astype(jnp.float32) + embed_row[:, None]
    kernel = lax.map(lambda params: channel_kernel(*params), (log_step, damping, frequency, coef_re, coef_im))
    input_spec = jnp.fft.rfft(inputs, n=padded, axis=1)
    kernel_spec = jnp.fft.rfft(kernel, n=padded, axis=1)
    output = jnp.fft.irfft(input_spec * kernel_spec, n=padded, axis=1)[:, :SAMPLES]
    mixed_in = output + skip_gain[:, None] * inputs
    act_full, gelu_pull = jax.vjp(jax.nn.gelu, mixed_in)
    activation = act_full.astype(jnp.bfloat16)
    grad_act = jnp.dot(mix_weight.T, cotangent, preferred_element_type=jnp.float32)
    grad_mixed = gelu_pull(grad_act)[0]
    grad_spec = jnp.fft.rfft(grad_mixed, n=padded, axis=1)
    conv_back = jnp.fft.irfft(jnp.conj(kernel_spec) * grad_spec, n=padded, axis=1)[:, :SAMPLES]
    grad_kernel = jnp.fft.irfft(jnp.conj(input_spec) * grad_spec, n=padded, axis=1)[:, :SAMPLES]
    grad_input = conv_back + skip_gain[:, None] * grad_mixed
    grad_signal = (cotangent.astype(jnp.float32) + grad_input).astype(jnp.bfloat16)
    grad_skip = lax.optimization_barrier(jnp.sum(grad_mixed * inputs, axis=1))
    chosen = (jnp.arange(DIFF_STEPS, dtype=jnp.int32) == diffusion_step[0]).astype(jnp.float32)
    grad_table = chosen[:, None] * lax.optimization_barrier(jnp.sum(grad_input, axis=1))[None, :]
    grad_mix = jnp.dot(cotangent, activation.T, preferred_element_type=jnp.float32)

    def channel_grads(packed):
        params, cotan_row = packed
        unused_value, pullback = jax.vjp(channel_kernel, *params)
        return pullback(cotan_row)
    gradients = lax.map(channel_grads, ((log_step, damping, frequency, coef_re, coef_im), grad_kernel))
    return (grad_signal, grad_kernel, gradients[0], gradients[1], gradients[2], gradients[3], gradients[4], grad_skip, grad_mix, grad_table)
```

```python
import math

import jax
import jax.numpy as jnp
import numpy as np
from jax import lax
from jax.sharding import PartitionSpec as P

HIGHEST = lax.Precision.HIGHEST
F32 = jnp.float32
BF16 = jnp.bfloat16
CHUNK = 128
COLS = 512


def mode_terms(log_step, damping, frequency, coef_re, coef_im):
    step_size = jnp.exp(log_step)[:, None]
    decay_rate = step_size * damping
    turn_rate = step_size * frequency
    half_sine = jnp.sin(0.5 * turn_rate)
    grow_real = jnp.expm1(-decay_rate) * jnp.cos(turn_rate) - 2.0 * half_sine * half_sine
    grow_imag = jnp.exp(-decay_rate) * jnp.sin(turn_rate)
    spread = damping * damping + frequency * frequency
    hold_real = (frequency * grow_imag - damping * grow_real) / spread
    hold_imag = -(frequency * grow_real + damping * grow_imag) / spread
    weight_real = coef_re * hold_real - coef_im * hold_imag
    weight_imag = coef_re * hold_imag + coef_im * hold_real
    return (decay_rate, turn_rate, weight_real, weight_imag)


def product(form, left_side, right_side):
    return jnp.einsum(
        form, left_side, right_side, precision=HIGHEST, preferred_element_type=F32
    )


def mode_powers(decay_rate, turn_rate, positions):
    size = jnp.exp(-decay_rate[..., None] * positions)
    turned = turn_rate[..., None] * positions
    return size * jnp.cos(turned), size * jnp.sin(turned)


def cmul(ar, ai, br, bi):
    return ar * br - ai * bi, ar * bi + ai * br


def dft_tables(tm_ranks, block_len):
    full_len = tm_ranks * block_len
    pieces = block_len // COLS
    row_total = full_len // COLS
    row = np.arange(row_total)
    time_row = (row % tm_ranks) * pieces + row // tm_ranks
    first = np.arange(row_total)
    column = np.arange(COLS)
    angle1 = 2.0 * np.pi * (((4 * first[:, None] + 1) * time_row[None, :]) % (4 * row_total)) / (4 * row_total)
    angle_t = 2.0 * np.pi * ((4 * first[:, None] + 1) * column[None, :]) / (4 * full_len)
    angle2 = 2.0 * np.pi * ((column[:, None] * column[None, :]) % COLS) / COLS
    return tuple(
        (np.cos(a).astype(np.float32), np.sin(a).astype(np.float32))
        for a in (angle1, angle_t, angle2)
    )


def to_rows(block):
    ranks, block_len = block.shape
    return jnp.concatenate(
        [block[:, p * COLS : (p + 1) * COLS] for p in range(block_len // COLS)], 0
    )


def from_rows(rows, ranks):
    return jnp.concatenate(
        [rows[p * ranks : (p + 1) * ranks] for p in range(rows.shape[0] // ranks)], 1
    )


def to_spectrum(rows, tables):
    (c1, s1), (ct, st), (c2, s2) = tables
    ar = product("kt,tc->kc", c1, rows)
    ai = -product("kt,tc->kc", s1, rows)
    ar, ai = cmul(ar, ai, ct, -st)
    xr = product("kc,cl->kl", ar, c2) + product("kc,cl->kl", ai, s2)
    xi = product("kc,cl->kl", ai, c2) - product("kc,cl->kl", ar, s2)
    return xr, xi


def from_spectrum(pr, pi, tables):
    (c1, s1), (ct, st), (c2, s2) = tables
    br = product("kl,lc->kc", pr, c2) - product("kl,lc->kc", pi, s2)
    bi = product("kl,lc->kc", pi, c2) + product("kl,lc->kc", pr, s2)
    br, bi = cmul(br, bi, ct, st)
    out = product("kt,kc->tc", c1, br) - product("kt,kc->tc", s1, bi)
    return out * (1.0 / pr.size)


def exchange(values):
    return lax.all_to_all(values, "tm", split_axis=0, concat_axis=0, tiled=True)


def carried(powers, pieces, initial, reverse):
    zr, zi = powers
    hr, hi = initial
    count = pieces[0].shape[1]
    before_r, before_i = [None] * count, [None] * count
    for i in reversed(range(count)) if reverse else range(count):
        before_r[i], before_i[i] = hr, hi
        nr, ni = cmul(zr, zi, hr, hi)
        hr, hi = nr + pieces[0][:, i], ni + pieces[1][:, i]
    return (jnp.stack(before_r, 1), jnp.stack(before_i, 1)), (hr, hi)


def shards(
    signal,
    cotangent,
    log_step,
    damping,
    frequency,
    coef_re,
    coef_im,
    skip_gain,
    mix_weight,
    embed_table,
    diffusion_step,
):
    channels, block_len = signal.shape
    modes = damping.shape[1]
    ranks = lax.axis_size("tm")
    groups = lax.axis_size("chan")
    me = lax.axis_index("tm")
    group = lax.axis_index("chan")
    chunks = block_len // CHUNK
    tables = dft_tables(ranks, block_len)

    chosen = (lax.iota(jnp.int32, embed_table.shape[0]) == diffusion_step[0]).astype(F32)
    embed_row = jnp.dot(chosen, embed_table, precision=HIGHEST, preferred_element_type=F32)
    decay, turn, wr, wi = mode_terms(log_step, damping, frequency, coef_re, coef_im)

    def swap(values, mask):
        return lax.ppermute(values, "chan", [(i, i ^ mask) for i in range(4)])

    across = swap(cotangent, 2)
    pair = jnp.stack([cotangent, across])
    pair_near = swap(pair, 1)
    by_xor = [cotangent, pair_near[0], across, pair_near[1]]

    def from_group(parts, wanted):
        result = parts[0]
        for mask in range(1, 4):
            result = jnp.where((group ^ mask) == wanted, parts[mask], result)
        return result

    cot_all = jnp.concatenate([from_group(by_xor, o) for o in range(groups)], 0)
    mix_mine = lax.all_to_all(
        mix_weight.reshape(channels, groups, channels).transpose(1, 0, 2),
        "chan",
        split_axis=0,
        concat_axis=0,
        tiled=True,
    ).reshape(groups * channels, channels)
    grad_act = jnp.einsum("oc,ot->ct", mix_mine, cot_all, preferred_element_type=F32)

    steps = jnp.arange(CHUNK, dtype=F32)
    er, ei = mode_powers(decay, turn, steps)
    fr, fi = er[..., ::-1], ei[..., ::-1]
    one_r, one_i = mode_powers(decay, turn, jnp.ones((1,), F32))
    vr, vi = cmul(2.0 * wr[..., None], 2.0 * wi[..., None], er, ei)
    taps = jnp.sum(vr, axis=1)
    ur, ui = cmul(vr, vi, one_r, one_i)
    lag = np.arange(CHUNK)[None, :] - np.arange(CHUNK)[:, None]
    toeplitz = jnp.where(lag >= 0, taps[:, np.maximum(lag, 0)], 0.0)
    chunk_power = tuple(
        p[..., 0] for p in mode_powers(decay, turn, jnp.full((1,), CHUNK, F32))
    )

    inputs = signal.astype(F32) + embed_row[:, None]
    x = inputs.reshape(channels, chunks, CHUNK)
    pieces = (product("cij,cnj->cin", x, fr), product("cij,cnj->cin", x, fi))
    zero = jnp.zeros((channels, modes), F32)
    unused, last = carried(chunk_power, pieces, (zero, zero), False)
    sent = jnp.stack(last).reshape(1, -1)
    sent = jnp.concatenate(
        [inputs, jnp.broadcast_to(sent, (ranks, sent.shape[1]))], 1
    )
    got = exchange(sent)
    x_rows = to_rows(got[:, :block_len])
    others = got[:, block_len:].reshape(ranks, 2, channels, modes)

    def gathered(distance):
        size_r, size_i = mode_powers(
            decay, turn, (jnp.maximum(distance, 0) * block_len).astype(F32)
        )
        keep = (distance >= 0).astype(F32)
        pr, pi = size_r * keep, size_i * keep

        def combine(states):
            sr, si = states[:, 0].transpose(1, 2, 0), states[:, 1].transpose(1, 2, 0)
            hr, hi = cmul(pr, pi, sr, si)
            return jnp.sum(hr, -1), jnp.sum(hi, -1)

        return combine

    rank_ids = lax.iota(jnp.int32, ranks)
    start = gathered(me - 1 - rank_ids)(others)
    before, unused = carried(chunk_power, pieces, start, False)
    output = product("cij,cjk->cik", x, toeplitz)
    output += product("cin,cnk->cik", before[0], ur) - product("cin,cnk->cik", before[1], ui)
    output = output.reshape(channels, block_len)

    mixed_in = output + skip_gain[:, None] * inputs
    act_full, gelu_pull = jax.vjp(jax.nn.gelu, mixed_in)
    activation = act_full.astype(BF16)
    grad_mixed = gelu_pull(grad_act)[0]
    mix_part = jnp.einsum("ot,ct->oc", cot_all, activation, preferred_element_type=F32)

    g = grad_mixed.reshape(channels, chunks, CHUNK)
    pieces = (product("cij,cnj->cin", g, er), product("cij,cnj->cin", g, ei))
    unused, last = carried(chunk_power, pieces, (zero, zero), True)
    sent = jnp.stack(last).reshape(1, -1)
    state_len = sent.shape[1]
    sent = jnp.concatenate(
        [grad_mixed, jnp.broadcast_to(sent, (ranks, state_len)), mix_part.reshape(ranks, -1)], 1
    )
    got = exchange(sent)
    g_rows = to_rows(got[:, :block_len])
    others = got[:, block_len : block_len + state_len].reshape(ranks, 2, channels, modes)
    mix_sum = jnp.sum(got[:, block_len + state_len :], axis=0)

    start = gathered(rank_ids - me - 1)(others)
    after, unused = carried(chunk_power, pieces, start, True)
    back = product("cij,ckj->cik", g, toeplitz)
    back += product("cin,cnk->cik", after[0], ur[..., ::-1]) - product(
        "cin,cnk->cik", after[1], ui[..., ::-1]
    )
    grad_input = back.reshape(channels, block_len) + skip_gain[:, None] * grad_mixed
    grad_signal = (cotangent.astype(F32) + grad_input).astype(BF16)
    table_part = jnp.sum(grad_input, axis=1)

    x_spec = to_spectrum(x_rows, tables)
    g_spec = to_spectrum(g_rows, tables)
    pr, pi = cmul(x_spec[0], -x_spec[1], g_spec[0], g_spec[1])
    kernel_rows = from_spectrum(pr, pi, tables)

    def mine(values):
        return lax.dynamic_slice_in_dim(values, me, 1, 0)

    my_terms, terms_pull = jax.vjp(
        mode_terms, mine(log_step), mine(damping), mine(frequency), mine(coef_re), mine(coef_im)
    )
    d, th, mr, mi = my_terms
    col = jnp.arange(COLS, dtype=F32)
    cr, ci = (v[0] for v in mode_powers(d, th, col))
    row_ids = np.arange(kernel_rows.shape[0])
    row_start = ((row_ids % ranks) * (block_len // COLS) + row_ids // ranks) * COLS
    rr, ri = (v[0].T for v in mode_powers(d, th, jnp.asarray(row_start, F32)))
    inner = product(
        "rc,nc->rn", kernel_rows, jnp.concatenate([cr, ci, cr * col, ci * col], 0)
    )
    i0r, i0i, i1r, i1i = (inner[:, k * modes : (k + 1) * modes] for k in range(4))
    starts = jnp.asarray(row_start, F32)[:, None]
    i1r, i1i = i1r + starts * i0r, i1i + starts * i0i
    cos_sum, sin_sum = (jnp.sum(v, 0)[None] for v in cmul(rr, ri, i0r, i0i))
    cos_moment, sin_moment = (jnp.sum(v, 0)[None] for v in cmul(rr, ri, i1r, i1i))
    grad_terms = (
        -2.0 * (mr * cos_moment - mi * sin_moment),
        -2.0 * (mr * sin_moment + mi * cos_moment),
        2.0 * cos_sum,
        -2.0 * sin_sum,
    )
    grads = terms_pull(grad_terms)
    skip_sum = jnp.sum(x_rows * g_rows).reshape(1)
    mix_rows = lax.all_gather(mix_sum, "chan")
    small = jnp.concatenate(
        [
            grads[0],
            skip_sum,
            grads[1][0],
            grads[2][0],
            grads[3][0],
            grads[4][0],
            mix_rows.reshape(-1),
            table_part,
        ]
    )
    pad = -small.shape[0] % 128
    small = jnp.pad(small, (0, pad))
    sent = jnp.concatenate(
        [from_rows(kernel_rows, ranks), jnp.broadcast_to(small, (ranks, small.shape[0]))], 1
    )
    got = exchange(sent)
    grad_kernel = got[:, :block_len]
    rest = got[:, block_len:]
    base = 2 + 4 * modes
    mix_len = mix_rows.size
    per_rank = groups * channels // ranks
    mix_all = rest[:, base : base + mix_len].reshape(ranks, groups, per_rank, channels)
    mix_all = lax.dynamic_slice_in_dim(mix_all, group * (ranks // groups), ranks // groups, 0)
    grad_mix = mix_all.transpose(0, 2, 1, 3).reshape(channels, groups * channels)
    table_row = jnp.sum(rest[:, base + mix_len : base + mix_len + channels], 0)
    grad_table = chosen[:, None] * table_row[None, :]
    parts = [rest[:, 2 + k * modes : 2 + (k + 1) * modes] for k in range(4)]
    return (
        grad_signal,
        grad_kernel,
        rest[:, 0],
        parts[0],
        parts[1],
        parts[2],
        parts[3],
        rest[:, 1],
        grad_mix,
        grad_table,
    )


def solution(mesh):
    placed = (
        P("chan", "tm"),
        P("chan", "tm"),
        P("chan"),
        P("chan", None),
        P("chan", None),
        P("chan", None),
        P("chan", None),
        P("chan"),
        P("chan", None),
        P(None, "chan"),
        P(),
    )
    return jax.shard_map(
        shards,
        mesh=mesh,
        in_specs=placed,
        out_specs=(
            P("chan", "tm"),
            P("chan", "tm"),
            P("chan"),
            P("chan", None),
            P("chan", None),
            P("chan", None),
            P("chan", None),
            P("chan"),
            P("chan", None),
            P(None, "chan"),
        ),
        check_vma=False,
    )
```

```python
import functools

import jax
import jax.numpy as jnp
import numpy as np
from jax import lax
from jax.experimental import pallas as pl
from jax.experimental.pallas import tpu as pltpu
from jax.sharding import PartitionSpec as P

HIGHEST = lax.Precision.HIGHEST
F32 = jnp.float32
BF16 = jnp.bfloat16

CH = 32
MODES = 32
BLOCK = 4096
LN = 128
CK = BLOCK // LN
LANE_CH = LN // MODES
GROUPS = CH // LANE_CH
RANKS = 32
COLS = 512
PER = COLS // LN
ROWS = RANKS * BLOCK // COLS
SEND1 = 64
SEND2 = 56
SEND3 = 40
NT = (((1,), (1,)), ((), ()))
NN = (((1,), (0,)), ((), ()))
PARAMS = pltpu.CompilerParams(vmem_limit_bytes=40 * 1024 * 1024)


def mode_terms(log_step, damping, frequency, coef_re, coef_im):
    step_size = jnp.exp(log_step)
    decay_rate = step_size * damping
    turn_rate = step_size * frequency
    half_sine = jnp.sin(0.5 * turn_rate)
    grow_real = jnp.expm1(-decay_rate) * jnp.cos(turn_rate) - 2.0 * half_sine * half_sine
    grow_imag = jnp.exp(-decay_rate) * jnp.sin(turn_rate)
    spread = damping * damping + frequency * frequency
    hold_real = (frequency * grow_imag - damping * grow_real) / spread
    hold_imag = -(frequency * grow_real + damping * grow_imag) / spread
    weight_real = coef_re * hold_real - coef_im * hold_imag
    weight_imag = coef_re * hold_imag + coef_im * hold_real
    return (decay_rate, turn_rate, weight_real, weight_imag)


def cmul(ar, ai, br, bi):
    return ar * br - ai * bi, ar * bi + ai * br


def split(values):
    high = values.astype(BF16)
    return high, (values - high.astype(F32)).astype(BF16)


def dot(left, right, dims=NN):
    return lax.dot_general(left, right, dims, preferred_element_type=F32)


def dot3(left, right, dims=NN):
    lh, ll = left
    rh, rl = right
    return dot(lh, rh, dims) + dot(ll, rh, dims) + dot(lh, rl, dims)


def sin_cos(x):
    y = x * x
    s = 1.0
    for k in (210.0, 156.0, 110.0, 72.0, 42.0, 20.0, 6.0):
        s = 1.0 - y * s * (1.0 / k)
    c = 1.0
    for k in (240.0, 182.0, 132.0, 90.0, 56.0, 30.0, 12.0, 2.0):
        c = 1.0 - y * c * (1.0 / k)
    return x * s, c


def power(decay, turn, steps):
    size = jnp.exp(-decay * steps)
    s, c = sin_cos(turn * steps)
    return size * c, size * s


def doublings(decay, turn):
    return [power(decay, turn, float(k)) for k in (8, 16, 32, 64)]


def rising(decay, turn, doubles, g):
    rows = lax.broadcasted_iota(jnp.int32, (8, LN), 0).astype(F32)
    tr, ti = power(decay[g : g + 1], turn[g : g + 1], rows)
    for zr, zi in doubles:
        nr, ni = cmul(tr, ti, zr[g : g + 1], zi[g : g + 1])
        tr, ti = jnp.concatenate([tr, nr], 0), jnp.concatenate([ti, ni], 0)
    return tr, ti


def falling(decay, turn, doubles, g):
    rows = 7.0 - lax.broadcasted_iota(jnp.int32, (8, LN), 0).astype(F32)
    tr, ti = power(decay[g : g + 1], turn[g : g + 1], rows)
    for zr, zi in doubles:
        nr, ni = cmul(tr, ti, zr[g : g + 1], zi[g : g + 1])
        tr, ti = jnp.concatenate([nr, tr], 0), jnp.concatenate([ni, ti], 0)
    return tr, ti


def lane_channel(shape):
    return lax.broadcasted_iota(jnp.int32, shape, 1) // MODES


def gather_group(products):
    owner = lane_channel((CK, LN))
    real, imag = products[:, :LN], products[:, LN:]
    out_r, out_i = real[:CK], imag[:CK]
    for k in range(1, LANE_CH):
        mine = owner == k
        out_r = jnp.where(mine, real[k * CK : (k + 1) * CK], out_r)
        out_i = jnp.where(mine, imag[k * CK : (k + 1) * CK], out_i)
    return out_r, out_i


def spread_group(state_r, state_i, table):
    owner = lane_channel((CK, LN))
    zero = jnp.zeros((CK, LN), F32)
    left = jnp.concatenate(
        [
            jnp.concatenate(
                [jnp.where(owner == k, state_r, zero), jnp.where(owner == k, -state_i, zero)], 1
            )
            for k in range(LANE_CH)
        ],
        0,
    )
    return dot3(split(left), split(table), NT)


def scan_states(sr_ref, si_ref, power_r, power_i, start_r, start_i, order, keep):
    hr, hi = start_r, start_i
    for i in order:
        rows = pl.ds(i * GROUPS, GROUPS)
        own_r, own_i = sr_ref[rows, :], si_ref[rows, :]
        if keep:
            sr_ref[rows, :] = hr
            si_ref[rows, :] = hi
        nr, ni = cmul(power_r, power_i, hr, hi)
        hr, hi = nr + own_r, ni + own_i
    return hr, hi


def toeplitz(taps_row):
    rows = jnp.broadcast_to(taps_row, (LN, LN))
    turned = pltpu.roll(rows, 0, 1, stride=1, stride_axis=0)
    lag = lax.broadcasted_iota(jnp.int32, (LN, LN), 1) - lax.broadcasted_iota(
        jnp.int32, (LN, LN), 0
    )
    return jnp.where(lag >= 0, turned, 0.0)


def group_taps(terms, table, g):
    real = 2.0 * (terms[2][g : g + 1] * table[0] - terms[3][g : g + 1] * table[1])
    owner = (
        lane_channel((8, LN)) == lax.broadcasted_iota(jnp.int32, (8, LN), 0)
    ).astype(BF16)
    high, low = split(real)
    return dot(owner, high, NT) + dot(owner, low, NT)


def first_kernel(signal_ref, terms_ref, embed_ref, send_ref, sr_ref, si_ref, rows_ref):
    for i in range(CK):
        rows_ref[pl.ds(i, CH, stride=CK), :] = signal_ref[:, i * LN : (i + 1) * LN].astype(F32)
    decay, turn = terms_ref[0], terms_ref[1]
    doubles = doublings(decay, turn)
    for g in range(GROUPS):
        x = rows_ref[g * LN : (g + 1) * LN, :].astype(BF16)
        fr, fi = falling(decay, turn, doubles, g)
        table = jnp.concatenate([fr, fi], 1)
        th, tl = split(table)
        pr, pi = gather_group(dot(x, th) + dot(x, tl))
        level = embed_ref[g : g + 1]
        sr_ref[pl.ds(g, CK, stride=GROUPS), :] = pr + level * jnp.sum(fr, 0, keepdims=True)
        si_ref[pl.ds(g, CK, stride=GROUPS), :] = pi + level * jnp.sum(fi, 0, keepdims=True)
        for k in range(LANE_CH):
            send_ref[g * LANE_CH + k, :CK, :] = x[k * CK : (k + 1) * CK]
    zr, zi = power(decay, turn, float(LN))
    zero = jnp.zeros((GROUPS, LN), F32)
    hr, hi = scan_states(sr_ref, si_ref, zr, zi, zero, zero, range(CK), False)
    high, low = split(jnp.concatenate([hr, hi], 0))
    packed = jnp.concatenate([high, low], 0)
    for d in range(RANKS):
        send_ref[d, CK:SEND1, :] = packed


def first(signal, terms, embed_lanes):
    return pl.pallas_call(
        first_kernel,
        out_shape=(
            jax.ShapeDtypeStruct((RANKS, SEND1, LN), BF16),
            jax.ShapeDtypeStruct((CK * GROUPS, LN), F32),
            jax.ShapeDtypeStruct((CK * GROUPS, LN), F32),
        ),
        scratch_shapes=[pltpu.VMEM((CH * CK, LN), F32)],
        compiler_params=PARAMS,
        name="block_states",
    )(signal, terms, embed_lanes)


def within_kernel(x_ref, terms_ref, embed_ref, c0, c1, c2, c3, pick_ref, out_ref, act_ref):
    terms = terms_ref[0], terms_ref[1], terms_ref[2], terms_ref[3]
    doubles = doublings(terms[0], terms[1])
    for g in range(GROUPS):
        taps = group_taps(terms, rising(terms[0], terms[1], doubles, g), g)
        for k in range(LANE_CH):
            c = g * LANE_CH + k
            matrix = toeplitz(taps[k : k + 1])
            high, low = split(matrix)
            x = x_ref[c, :CK, :]
            level = embed_ref[c : c + 1, :]
            out_ref[c * CK : (c + 1) * CK, :] = (
                dot(x, high) + dot(x, low) + level * jnp.sum(matrix, 0, keepdims=True)
            )
    weights = jnp.concatenate([c[:, BLOCK:] for c in (c0, c1, c2, c3)], 0)
    weights = dot(pick_ref[...], weights, NT).astype(BF16)
    for i in range(CK):
        cols = slice(i * LN, (i + 1) * LN)
        cot = jnp.concatenate([c[:, cols] for c in (c0, c1, c2, c3)], 0)
        act_ref[pl.ds(i, CH, stride=CK), :] = dot(weights, cot)


def within(send, terms, embed_rows, parts, pick):
    return pl.pallas_call(
        within_kernel,
        out_shape=(
            jax.ShapeDtypeStruct((CH * CK, LN), F32),
            jax.ShapeDtypeStruct((CH * CK, LN), F32),
        ),
        compiler_params=PARAMS,
        name="within_chunks",
    )(send, terms, embed_rows, *parts, pick)


def gelu_both(x):
    scale = np.float32(np.sqrt(2.0 / np.pi))
    square = x * x
    t = jnp.tanh(scale * (x + 0.044715 * (square * x)))
    half = 0.5 * (1.0 + t)
    slope = half + 0.5 * x * (1.0 - t * t) * (scale * (1.0 + (3.0 * 0.044715) * square))
    return x * half, slope


def entering(states, table_r, table_i):
    hr = jnp.zeros((GROUPS, LN), F32)
    hi = jnp.zeros((GROUPS, LN), F32)
    for d in range(RANKS):
        sr, si = states(d)
        nr, ni = cmul(table_r[d], table_i[d], sr, si)
        hr, hi = hr + nr, hi + ni
    return hr, hi


def second_kernel(
    got_ref, x_ref, terms_ref, embed_ref, skip_ref, far_r, far_i, sr_in, si_in, out_ref, act_ref,
    c0, c1, c2, c3, send_ref, sr_ref, si_ref, activation_ref, flat_ref,
):
    terms = terms_ref[0], terms_ref[1], terms_ref[2], terms_ref[3]
    decay, turn = terms[0], terms[1]
    doubles = doublings(decay, turn)
    zr, zi = power(decay, turn, float(LN))
    one_r, one_i = power(decay, turn, 1.0)
    ur, ui = cmul(2.0 * terms[2], 2.0 * terms[3], one_r, one_i)

    def states(d):
        packed = got_ref[d, CK:SEND1, :].astype(F32)
        values = packed[: 2 * GROUPS] + packed[2 * GROUPS :]
        return values[:GROUPS], values[GROUPS:]

    start = entering(states, far_r, far_i)
    sr_ref[...] = sr_in[...]
    si_ref[...] = si_in[...]
    scan_states(sr_ref, si_ref, zr, zi, start[0], start[1], range(CK), True)
    for g in range(GROUPS):
        every = pl.ds(g, CK, stride=GROUPS)
        er, ei = rising(decay, turn, doubles, g)
        wr, wi = cmul(er, ei, ur[g : g + 1], ui[g : g + 1])
        inter = spread_group(sr_ref[every, :], si_ref[every, :], jnp.concatenate([wr, wi], 1))
        left = []
        for k in range(LANE_CH):
            c = g * LANE_CH + k
            rows = slice(c * CK, (c + 1) * CK)
            x = x_ref[c, :CK, :].astype(F32) + embed_ref[c : c + 1, :]
            mixed = out_ref[rows, :] + inter[k * CK : (k + 1) * CK] + skip_ref[c : c + 1, :] * x
            act, slope = gelu_both(mixed)
            activation_ref[rows, :] = act
            grad = act_ref[rows, :] * slope
            send_ref[c, :CK, :] = grad
            left.append(grad)
        products = dot3(split(jnp.concatenate(left, 0)), split(jnp.concatenate([er, ei], 1)))
        pr, pi = gather_group(products)
        sr_ref[every, :] = pr
        si_ref[every, :] = pi
    zero = jnp.zeros((GROUPS, LN), F32)
    hr, hi = scan_states(sr_ref, si_ref, zr, zi, zero, zero, range(CK - 1, -1, -1), False)
    for i in range(CK):
        flat_ref[:, i * LN : (i + 1) * LN] = activation_ref[pl.ds(i, CH, stride=CK), :].astype(BF16)
    flat = flat_ref[...]
    mix = jnp.concatenate([dot(flat, c[:, :BLOCK], NT) for c in (c0, c1, c2, c3)], 1)
    for d in range(RANKS):
        send_ref[d, CK : CK + GROUPS, :] = hr
        send_ref[d, CK + GROUPS : CK + 2 * GROUPS, :] = hi
        send_ref[d, CK + 2 * GROUPS :, :] = jnp.broadcast_to(mix[d : d + 1], (8, LN))


def second(got, send, terms, embed_rows, skip_rows, far, sr, si, out, grad_act, parts):
    return pl.pallas_call(
        second_kernel,
        out_shape=(
            jax.ShapeDtypeStruct((RANKS, SEND2, LN), F32),
            jax.ShapeDtypeStruct((CK * GROUPS, LN), F32),
            jax.ShapeDtypeStruct((CK * GROUPS, LN), F32),
        ),
        scratch_shapes=[pltpu.VMEM((CH * CK, LN), F32), pltpu.VMEM((CH, BLOCK), BF16)],
        compiler_params=PARAMS,
        name="activation_and_states",
    )(got, send, terms, embed_rows, skip_rows, far[0], far[1], sr, si, out, grad_act, *parts)


def back_kernel(send_ref, terms_ref, out_ref):
    terms = terms_ref[0], terms_ref[1], terms_ref[2], terms_ref[3]
    doubles = doublings(terms[0], terms[1])
    for g in range(GROUPS):
        taps = group_taps(terms, rising(terms[0], terms[1], doubles, g), g)
        for k in range(LANE_CH):
            c = g * LANE_CH + k
            out_ref[c * CK : (c + 1) * CK, :] = dot3(
                split(send_ref[c, :CK, :]), split(toeplitz(taps[k : k + 1])), NT
            )


def back(send, terms):
    return pl.pallas_call(
        back_kernel,
        out_shape=jax.ShapeDtypeStruct((CH * CK, LN), F32),
        compiler_params=PARAMS,
        name="back_within_chunks",
    )(send, terms)


def signal_kernel(
    got_ref, send_ref, terms_ref, skip_ref, far_r, far_i, sr_in, si_in, back_ref, cot_ref,
    out_ref, part_ref, sr_ref, si_ref, rows_ref,
):
    terms = terms_ref[0], terms_ref[1], terms_ref[2], terms_ref[3]
    decay, turn = terms[0], terms[1]
    doubles = doublings(decay, turn)
    zr, zi = power(decay, turn, float(LN))
    one_r, one_i = power(decay, turn, 1.0)
    ur, ui = cmul(2.0 * terms[2], 2.0 * terms[3], one_r, one_i)

    def states(d):
        return got_ref[d, CK : CK + GROUPS, :], got_ref[d, CK + GROUPS : CK + 2 * GROUPS, :]

    start = entering(states, far_r, far_i)
    sr_ref[...] = sr_in[...]
    si_ref[...] = si_in[...]
    scan_states(sr_ref, si_ref, zr, zi, start[0], start[1], range(CK - 1, -1, -1), True)
    for g in range(GROUPS):
        every = pl.ds(g, CK, stride=GROUPS)
        fr, fi = falling(decay, turn, doubles, g)
        wr, wi = cmul(fr, fi, ur[g : g + 1], ui[g : g + 1])
        inter = spread_group(sr_ref[every, :], si_ref[every, :], jnp.concatenate([wr, wi], 1))
        for k in range(LANE_CH):
            c = g * LANE_CH + k
            rows = slice(c * CK, (c + 1) * CK)
            grad = (
                back_ref[rows, :]
                + inter[k * CK : (k + 1) * CK]
                + skip_ref[c : c + 1, :] * send_ref[c, :CK, :]
            )
            rows_ref[rows, :] = grad
    total = jnp.zeros((CH, LN), F32)
    for i in range(CK):
        cols = slice(i * LN, (i + 1) * LN)
        grad = rows_ref[pl.ds(i, CH, stride=CK), :]
        total = total + grad
        out_ref[:, cols] = (cot_ref[:, cols].astype(F32) + grad).astype(BF16)
    part_ref[...] = total


def signal_grad(got, send, terms, skip_rows, far, sr, si, back_out, cotangent):
    return pl.pallas_call(
        signal_kernel,
        out_shape=(
            jax.ShapeDtypeStruct((CH, BLOCK), BF16),
            jax.ShapeDtypeStruct((CH, LN), F32),
        ),
        scratch_shapes=[
            pltpu.VMEM((CK * GROUPS, LN), F32),
            pltpu.VMEM((CK * GROUPS, LN), F32),
            pltpu.VMEM((CH * CK, LN), F32),
        ],
        compiler_params=PARAMS,
        name="signal_gradient",
    )(got, send, terms, skip_rows, far[0], far[1], sr, si, back_out, cotangent)


def dft_tables():
    full_len = RANKS * BLOCK
    row = np.arange(ROWS)
    time_row = (row % RANKS) * (BLOCK // COLS) + row // RANKS
    first_ids = np.arange(ROWS)
    column = np.arange(COLS)
    angle1 = (
        2.0 * np.pi * (((4 * first_ids[:, None] + 1) * time_row[None, :]) % (4 * ROWS)) / (4 * ROWS)
    )
    angle_t = 2.0 * np.pi * ((4 * first_ids[:, None] + 1) * column[None, :]) / (4 * full_len)
    angle2 = 2.0 * np.pi * ((column[:, None] * column[None, :]) % COLS) / COLS

    def halves(values):
        values = values.astype(np.float32)
        high = values.astype(BF16)
        return high, (values - high.astype(np.float32)).astype(BF16)

    stage1 = np.concatenate([np.cos(angle1), -np.sin(angle1)], 0)
    stage2 = np.concatenate([np.cos(angle2), np.sin(angle2)], 1)
    twiddle = np.stack([np.cos(angle_t), np.sin(angle_t)]).astype(np.float32)
    return halves(stage1), halves(stage1.T / full_len), halves(stage2), twiddle


def gather_rows(ref, stride, base):
    return jnp.concatenate(
        [
            jnp.concatenate(
                [
                    ref[pl.ds(base + piece * PER + q, RANKS, stride=stride), :]
                    for q in range(PER)
                ],
                1,
            )
            for piece in range(BLOCK // COLS)
        ],
        0,
    )


def forward_dft(rows, d1h, d1l, d2h, d2l, twiddle):
    xh, xl = split(rows)
    a = dot(d1h[...], xh) + dot(d1h[...], xl) + dot(d1l[...], xh)
    ar, ai = cmul(a[:ROWS], a[ROWS:], twiddle[0], -twiddle[1])
    p = dot3(split(jnp.concatenate([ar, ai], 0)), (d2h[...], d2l[...]))
    return p[:ROWS, :COLS] + p[ROWS:, COLS:], p[ROWS:, :COLS] - p[:ROWS, COLS:]


def inverse_dft(pr, pi, d1th, d1tl, d2h, d2l, twiddle):
    p = dot3(split(jnp.concatenate([pr, pi], 0)), (d2h[...], d2l[...]))
    br, bi = p[:ROWS, :COLS] - p[ROWS:, COLS:], p[ROWS:, :COLS] + p[:ROWS, COLS:]
    br, bi = cmul(br, bi, twiddle[0], twiddle[1])
    bh, bl = split(jnp.concatenate([br, bi], 0))
    return dot(d1th[...], bh) + dot(d1th[...], bl) + dot(d1tl[...], bh)


def spectrum_kernel(got_ref, embed_ref, d1h, d1l, d2h, d2l, twiddle, spec_ref, rows_ref, flat_ref):
    for d in range(RANKS):
        flat_ref[d * CK : (d + 1) * CK, :] = got_ref[d, :CK, :].astype(F32) + embed_ref[...]
    rows = gather_rows(flat_ref, CK, 0)
    rows_ref[...] = rows
    xr, xi = forward_dft(rows, d1h, d1l, d2h, d2l, twiddle)
    spec_ref[0] = xr
    spec_ref[1] = xi


def spectrum(got, embed_mine, tables):
    (d1h, d1l), unused, (d2h, d2l), twiddle = tables
    return pl.pallas_call(
        spectrum_kernel,
        out_shape=(
            jax.ShapeDtypeStruct((2, ROWS, COLS), F32),
            jax.ShapeDtypeStruct((ROWS, COLS), F32),
        ),
        scratch_shapes=[pltpu.VMEM((RANKS * CK, LN), F32)],
        compiler_params=PARAMS,
        name="input_spectrum",
    )(got, embed_mine, d1h, d1l, d2h, d2l, twiddle)


def correlate_kernel(
    got_ref, spec_ref, rows_ref, d1h, d1l, d1th, d1tl, d2h, d2l, twiddle, column_ref, turn_ref,
    pull_ref, send_ref, small_ref,
):
    g_rows = gather_rows(got_ref, SEND2, 0)
    gr, gi = forward_dft(g_rows, d1h, d1l, d2h, d2l, twiddle)
    xr, xi = spec_ref[0], spec_ref[1]
    pr = xr * gr + xi * gi
    pi = xr * gi - xi * gr
    kernel_rows = inverse_dft(pr, pi, d1th, d1tl, d2h, d2l, twiddle)
    for piece in range(BLOCK // COLS):
        for q in range(PER):
            send_ref[pl.ds(piece * PER + q, RANKS, stride=SEND3), :] = kernel_rows[
                piece * RANKS : (piece + 1) * RANKS, q * LN : (q + 1) * LN
            ]
    inner = dot3(split(kernel_rows), split(column_ref[...]))
    rr, ri = turn_ref[0], turn_ref[1]
    ids = lax.broadcasted_iota(jnp.int32, (ROWS, LN), 0)
    starts = ((ids % RANKS) * BLOCK + (ids // RANKS) * COLS).astype(F32)

    def total(values):
        return jnp.sum(values, 0, keepdims=True)

    by_r, by_i = rr * inner, ri * inner
    u, v = total(by_r), total(by_i)
    su, sv = total(starts * by_r), total(starts * by_i)

    def block(row, k):
        lanes = lax.broadcasted_iota(jnp.int32, (1, LN), 1)
        moved = pltpu.roll(row, (LN - k * MODES) % LN, 1) if k else row
        return jnp.where(lanes < MODES, moved, 0.0)

    cos_sum = block(u, 0) - block(v, 1)
    sin_sum = block(u, 1) + block(v, 0)
    cos_moment = block(u, 2) - block(v, 3) + block(su, 0) - block(sv, 1)
    sin_moment = block(u, 3) + block(v, 2) + block(su, 1) + block(sv, 0)
    grads = jnp.zeros((1, LN), F32)
    step = jnp.zeros((1, LN), F32)
    for k, value in enumerate((cos_sum, sin_sum, cos_moment, sin_moment)):
        wide = value
        for m in range(1, LANE_CH):
            wide = wide + pltpu.roll(value, m * MODES, 1)
        grads = grads + pull_ref[k : k + 1, :] * wide
        step = step + pull_ref[4 + k : 5 + k, :] * value
    step_sum = jnp.sum(step, 1, keepdims=True)
    skip_sum = jnp.sum(total(rows_ref[...] * g_rows), 1, keepdims=True)
    lanes = lax.broadcasted_iota(jnp.int32, (1, LN), 1)
    scalars = jnp.where(lanes == 0, step_sum, 0.0) + jnp.where(lanes == 1, skip_sum, 0.0)
    small_ref[...] = jnp.concatenate([grads, scalars, jnp.zeros((6, LN), F32)], 0)
    for d in range(RANKS):
        send_ref[d * SEND3 + CK : (d + 1) * SEND3, :] = small_ref[...]


def correlate(got, spec, rows, tables, column, turns, pull):
    (d1h, d1l), (d1th, d1tl), (d2h, d2l), twiddle = tables
    return pl.pallas_call(
        correlate_kernel,
        out_shape=(
            jax.ShapeDtypeStruct((RANKS * SEND3, LN), F32),
            jax.ShapeDtypeStruct((8, LN), F32),
        ),
        compiler_params=PARAMS,
        name="correlation",
    )(
        got.reshape(RANKS * SEND2, LN), spec, rows, d1h, d1l, d1th, d1tl, d2h, d2l, twiddle,
        column, turns, pull,
    )


def exchange(values):
    return lax.all_to_all(values, "tm", split_axis=0, concat_axis=0, tiled=True)


def mode_powers(decay_rate, turn_rate, positions):
    size = jnp.exp(-decay_rate * positions)
    turned = turn_rate * positions
    return size * jnp.cos(turned), size * jnp.sin(turned)


def shards(
    signal,
    cotangent,
    log_step,
    damping,
    frequency,
    coef_re,
    coef_im,
    skip_gain,
    mix_weight,
    embed_table,
    diffusion_step,
):
    me = lax.axis_index("tm")
    group = lax.axis_index("chan")
    tables = dft_tables()

    def swap(values, mask):
        return lax.ppermute(values, "chan", [(i, i ^ mask) for i in range(4)])

    own = jnp.concatenate([cotangent, mix_weight], 1)
    across = swap(own, 2)
    near = swap(own, 1)
    diagonal = swap(across, 1)
    parts = (own, near, across, diagonal)

    embed_row = lax.dynamic_slice_in_dim(embed_table, diffusion_step[0], 1, 0)[0]

    def on_lanes(values):
        return values.reshape(GROUPS, LN)

    def widened(values):
        return on_lanes(jnp.broadcast_to(values[:, None], (CH, MODES)))

    terms = jnp.stack(
        mode_terms(
            widened(log_step), on_lanes(damping), on_lanes(frequency), on_lanes(coef_re),
            on_lanes(coef_im),
        )
    )
    embed_lanes = widened(embed_row)
    embed_rows = jnp.broadcast_to(embed_row[:, None], (CH, LN))
    skip_rows = jnp.broadcast_to(skip_gain[:, None], (CH, LN))

    send1, sr, si = first(signal, terms, embed_lanes)
    got1 = exchange(send1)

    pick = (
        lax.broadcasted_iota(jnp.int32, (CH, 4 * CH), 1)
        == group * CH + lax.broadcasted_iota(jnp.int32, (CH, 4 * CH), 0)
    ).astype(BF16)
    out, grad_act = within(send1, terms, embed_rows, parts, pick)

    rank_ids = lax.iota(jnp.int32, RANKS)

    def far_powers(distance):
        keep = (distance >= 0).astype(F32)[:, None, None]
        steps = (jnp.maximum(distance, 0) * BLOCK).astype(F32)[:, None, None]
        pr, pi = mode_powers(terms[0][None], terms[1][None], steps)
        return pr * keep, pi * keep

    send2, br, bi = second(
        got1, send1, terms, embed_rows, skip_rows, far_powers(me - 1 - rank_ids), sr, si, out,
        grad_act, parts,
    )
    got2 = exchange(send2)
    back_out = back(send2, terms)

    def mine(values):
        return lax.dynamic_slice_in_dim(values, me, 1, 0)

    spec, x_rows = spectrum(
        got1, jnp.broadcast_to(mine(embed_row)[:, None], (CK, LN)), tables
    )

    raw = (
        jnp.broadcast_to(mine(log_step)[:, None], (1, MODES)),
        mine(damping), mine(frequency), mine(coef_re), mine(coef_im),
    )
    (d, th, mr, mi), pull = jax.vjp(mode_terms, *raw)
    zero = jnp.zeros_like(d)
    pulled = [
        pull((zero, zero, zero + 2.0, zero)),
        pull((zero, zero, zero, zero - 2.0)),
        pull((-2.0 * mr, -2.0 * mi, zero, zero)),
        pull((2.0 * mi, -2.0 * mr, zero, zero)),
    ]
    pull_table = jnp.concatenate(
        [jnp.concatenate(p[1:], 1) for p in pulled]
        + [jnp.pad(p[0], ((0, 0), (0, LN - MODES))) for p in pulled],
        0,
    )
    col = lax.broadcasted_iota(jnp.int32, (COLS, 1), 0).astype(F32)
    cr, ci = mode_powers(d, th, col)
    column = jnp.concatenate([cr, ci, cr * col, ci * col], 1)
    row_ids = lax.broadcasted_iota(jnp.int32, (ROWS, 1), 0)
    row_start = ((row_ids % RANKS) * BLOCK + (row_ids // RANKS) * COLS).astype(F32)
    rr, ri = mode_powers(jnp.tile(d, (1, 4)), jnp.tile(th, (1, 4)), row_start)
    send3, small = correlate(got2, spec, x_rows, tables, column, jnp.stack([rr, ri]), pull_table)

    grad_signal, part = signal_grad(
        got2, send2, terms, skip_rows, far_powers(rank_ids - me - 1), br, bi, back_out, cotangent
    )
    mix_sum = jnp.sum(got2[:, CK + 2 * GROUPS, :], axis=0).reshape(4, CH)
    mix_row = jnp.concatenate([mix_sum[:1]] + [swap(mix_sum[m : m + 1], m) for m in range(1, 4)], 1)
    extra = jnp.concatenate(
        [mix_row, jnp.pad(jnp.sum(part, 1)[None], ((0, 0), (0, LN - CH)))], 0
    )
    send3 = send3.reshape(RANKS, SEND3, LN)
    send3 = send3.at[:, CK + 2 : CK + 4, :].set(jnp.broadcast_to(extra, (RANKS, 2, LN)))
    got3 = exchange(send3)

    grad_kernel = got3[:, :CK, :].reshape(CH, BLOCK)
    grads = got3[:, CK, :]
    scalars = got3[:, CK + 1, :]
    mixes = got3[:, CK + 2, :].reshape(CH, 4, CH)
    grad_mix = jnp.concatenate(
        [
            lax.dynamic_index_in_dim(mixes, group ^ cg, 1, keepdims=False).T
            for cg in range(4)
        ],
        1,
    )
    table_row = jnp.sum(got3[:, CK + 3, :CH], 0)
    chosen = (lax.iota(jnp.int32, embed_table.shape[0]) == diffusion_step[0]).astype(F32)
    grad_table = chosen[:, None] * table_row[None, :]
    pieces = [grads[:, k * MODES : (k + 1) * MODES] for k in range(4)]
    return (
        grad_signal,
        grad_kernel,
        scalars[:, 0],
        pieces[0],
        pieces[1],
        pieces[2],
        pieces[3],
        scalars[:, 1],
        grad_mix,
        grad_table,
    )


def solution(mesh):
    placed = (
        P("chan", "tm"),
        P("chan", "tm"),
        P("chan"),
        P("chan", None),
        P("chan", None),
        P("chan", None),
        P("chan", None),
        P("chan"),
        P("chan", None),
        P(None, "chan"),
        P(),
    )
    return jax.shard_map(
        shards,
        mesh=mesh,
        in_specs=placed,
        out_specs=(
            P("chan", "tm"),
            P("chan", "tm"),
            P("chan"),
            P("chan", None),
            P("chan", None),
            P("chan", None),
            P("chan", None),
            P("chan"),
            P("chan", None),
            P(None, "chan"),
        ),
        check_vma=False,
    )
```

```python
import functools

import jax
import jax.numpy as jnp
import numpy as np
from jax import lax
from jax.experimental import pallas as pl
from jax.experimental.pallas import tpu as pltpu
from jax.sharding import PartitionSpec as P

HIGHEST = lax.Precision.HIGHEST
F32 = jnp.float32
BF16 = jnp.bfloat16

CH = 32
MODES = 32
BLOCK = 4096
LN = 128
CK = BLOCK // LN
LANE_CH = LN // MODES
GROUPS = CH // LANE_CH
RANKS = 32
COLS = 512
PER = COLS // LN
ROWS = RANKS * BLOCK // COLS
SEND1 = 64
SEND2 = 64
SEND3 = 80
NT = (((1,), (1,)), ((), ()))
NN = (((1,), (0,)), ((), ()))
PARAMS = pltpu.CompilerParams(vmem_limit_bytes=56 * 1024 * 1024)
SMEM = pl.BlockSpec(memory_space=pltpu.SMEM)
VMEM = pl.BlockSpec(memory_space=pltpu.VMEM)
ANY = pl.BlockSpec(memory_space=pl.ANY)


def expm1_small(x):
    r = 1.0
    for k in (7.0, 6.0, 5.0, 4.0, 3.0, 2.0):
        r = 1.0 + x * r * (1.0 / k)
    return x * r


def mode_terms(step_size, damping, frequency, coef_re, coef_im):
    decay_rate = step_size * damping
    turn_rate = step_size * frequency
    half_sine = jnp.sin(0.5 * turn_rate)
    grow_real = expm1_small(-decay_rate) * jnp.cos(turn_rate) - 2.0 * half_sine * half_sine
    grow_imag = jnp.exp(-decay_rate) * jnp.sin(turn_rate)
    inverse = 1.0 / (damping * damping + frequency * frequency)
    hold_real = (frequency * grow_imag - damping * grow_real) * inverse
    hold_imag = -(frequency * grow_real + damping * grow_imag) * inverse
    weight_real = coef_re * hold_real - coef_im * hold_imag
    weight_imag = coef_re * hold_imag + coef_im * hold_real
    return (decay_rate, turn_rate, weight_real, weight_imag)


def cmul(ar, ai, br, bi):
    return ar * br - ai * bi, ar * bi + ai * br


def split(values):
    high = values.astype(BF16)
    return high, (values - high.astype(F32)).astype(BF16)


def dot(left, right, dims=NN):
    return lax.dot_general(left, right, dims, preferred_element_type=F32)


def dot3(left, right, dims=NN):
    lh, ll = left
    rh, rl = right
    return dot(lh, rh, dims) + dot(ll, rh, dims) + dot(lh, rl, dims)


def started(sems, *pairs):
    copies = [pltpu.make_async_copy(a, b, sems.at[k]) for k, (a, b) in enumerate(pairs)]
    for copy in copies:
        copy.start()
    return copies


def sin_cos(x):
    y = x * x
    s = 1.0
    for k in (210.0, 156.0, 110.0, 72.0, 42.0, 20.0, 6.0):
        s = 1.0 - y * s * (1.0 / k)
    c = 1.0
    for k in (240.0, 182.0, 132.0, 90.0, 56.0, 30.0, 12.0, 2.0):
        c = 1.0 - y * c * (1.0 / k)
    return x * s, c


def power(decay, turn, steps):
    size = jnp.exp(-decay * steps)
    s, c = sin_cos(turn * steps)
    return size * c, size * s


def doublings(decay, turn):
    return [power(decay, turn, float(k)) for k in (8, 16, 32, 64)]


def rising(decay, turn, doubles, g):
    rows = lax.broadcasted_iota(jnp.int32, (8, LN), 0).astype(F32)
    tr, ti = power(decay[g : g + 1], turn[g : g + 1], rows)
    for zr, zi in doubles:
        nr, ni = cmul(tr, ti, zr[g : g + 1], zi[g : g + 1])
        tr, ti = jnp.concatenate([tr, nr], 0), jnp.concatenate([ti, ni], 0)
    return tr, ti


def falling(decay, turn, doubles, g):
    rows = 7.0 - lax.broadcasted_iota(jnp.int32, (8, LN), 0).astype(F32)
    tr, ti = power(decay[g : g + 1], turn[g : g + 1], rows)
    for zr, zi in doubles:
        nr, ni = cmul(tr, ti, zr[g : g + 1], zi[g : g + 1])
        tr, ti = jnp.concatenate([nr, tr], 0), jnp.concatenate([ni, ti], 0)
    return tr, ti


def lane_channel(shape):
    return lax.broadcasted_iota(jnp.int32, shape, 1) // MODES


def gather_group(products):
    owner = lane_channel((CK, LN))
    real, imag = products[:, :LN], products[:, LN:]
    out_r, out_i = real[:CK], imag[:CK]
    for k in range(1, LANE_CH):
        mine = owner == k
        out_r = jnp.where(mine, real[k * CK : (k + 1) * CK], out_r)
        out_i = jnp.where(mine, imag[k * CK : (k + 1) * CK], out_i)
    return out_r, out_i


def spread_group(state_r, state_i, table):
    owner = lane_channel((CK, LN))
    zero = jnp.zeros((CK, LN), F32)
    left = jnp.concatenate(
        [
            jnp.concatenate(
                [jnp.where(owner == k, state_r, zero), jnp.where(owner == k, -state_i, zero)], 1
            )
            for k in range(LANE_CH)
        ],
        0,
    )
    return dot3(split(left), split(table), NT)


def scan_states(sr_ref, si_ref, power_r, power_i, start_r, start_i, order, keep):
    hr, hi = start_r, start_i
    for i in order:
        rows = pl.ds(i * GROUPS, GROUPS)
        own_r, own_i = sr_ref[rows, :], si_ref[rows, :]
        if keep:
            sr_ref[rows, :] = hr
            si_ref[rows, :] = hi
        nr, ni = cmul(power_r, power_i, hr, hi)
        hr, hi = nr + own_r, ni + own_i
    return hr, hi


def toeplitz(taps_row):
    rows = jnp.broadcast_to(taps_row, (LN, LN))
    turned = pltpu.roll(rows, 0, 1, stride=1, stride_axis=0)
    lag = lax.broadcasted_iota(jnp.int32, (LN, LN), 1) - lax.broadcasted_iota(
        jnp.int32, (LN, LN), 0
    )
    return jnp.where(lag >= 0, turned, 0.0)


def group_taps(terms, table, g):
    real = 2.0 * (terms[2][g : g + 1] * table[0] - terms[3][g : g + 1] * table[1])
    owner = (
        lane_channel((8, LN)) == lax.broadcasted_iota(jnp.int32, (8, LN), 0)
    ).astype(BF16)
    high, low = split(real)
    return dot(owner, high, NT) + dot(owner, low, NT)


def packed_lanes(ref):
    return jnp.concatenate([ref[pl.ds(k, GROUPS, stride=LANE_CH), :] for k in range(LANE_CH)], 1)


def as_column(row):
    shape = (CH, CH)
    same = lax.broadcasted_iota(jnp.int32, shape, 0) == lax.broadcasted_iota(jnp.int32, shape, 1)
    return jnp.sum(jnp.where(same, row, 0.0), 1, keepdims=True)


def first_kernel(
    step_ref, signal_hbm, cot_hbm, mix_hbm, size_ref, damping_ref, frequency_ref, re_ref, im_ref,
    skip_ref, table_ref, send_hbm, own_hbm, sr_ref, si_ref, terms_ref, raw_ref, wide_ref,
    signal_ref, own_ref, send_ref, rows_ref, pack_ref, sems, out_sems,
):
    loads = started(
        sems,
        (signal_hbm, signal_ref),
        (cot_hbm, own_ref.at[:, pl.ds(0, BLOCK)]),
        (mix_hbm, own_ref.at[:, pl.ds(BLOCK, LN)]),
    )
    picked = lax.broadcasted_iota(jnp.int32, table_ref.shape, 1) == step_ref[0]
    embed = jnp.sum(jnp.where(picked, table_ref[...], 0.0), 1, keepdims=True)
    wide_ref[0] = jnp.broadcast_to(embed, (CH, LN))
    wide_ref[1] = jnp.broadcast_to(as_column(skip_ref[...]), (CH, LN))
    pack_ref[...] = jnp.broadcast_to(embed, (CH, MODES))
    embed_lanes = packed_lanes(pack_ref)
    pack_ref[...] = jnp.broadcast_to(as_column(jnp.exp(size_ref[...])), (CH, MODES))
    raw = [packed_lanes(r) for r in (pack_ref, damping_ref, frequency_ref, re_ref, im_ref)]
    for k in range(5):
        raw_ref[k] = raw[k]
    terms = mode_terms(*raw)
    for k in range(4):
        terms_ref[k] = terms[k]
    decay, turn = terms[0], terms[1]
    doubles = doublings(decay, turn)
    loads[0].wait()
    for i in range(CK):
        rows_ref[pl.ds(i, CH, stride=CK), :] = signal_ref[:, i * LN : (i + 1) * LN].astype(F32)
    for c in range(CH):
        send_ref[c, :CK, :] = rows_ref[c * CK : (c + 1) * CK, :].astype(BF16)
    loads[1].wait()
    loads[2].wait()
    stores = started(
        out_sems,
        (send_ref.at[:, pl.ds(0, CK), :], send_hbm.at[:, pl.ds(0, CK), :]),
        (own_ref, own_hbm),
    )
    for g in range(GROUPS):
        x = rows_ref[g * LN : (g + 1) * LN, :].astype(BF16)
        fr, fi = falling(decay, turn, doubles, g)
        table = jnp.concatenate([fr, fi], 1)
        th, tl = split(table)
        pr, pi = gather_group(dot(x, th) + dot(x, tl))
        level = embed_lanes[g : g + 1]
        sr_ref[pl.ds(g, CK, stride=GROUPS), :] = pr + level * jnp.sum(fr, 0, keepdims=True)
        si_ref[pl.ds(g, CK, stride=GROUPS), :] = pi + level * jnp.sum(fi, 0, keepdims=True)
    zr, zi = power(decay, turn, float(LN))
    zero = jnp.zeros((GROUPS, LN), F32)
    hr, hi = scan_states(sr_ref, si_ref, zr, zi, zero, zero, range(CK), False)
    packed = packed_states(hr, hi)
    for d in range(RANKS):
        send_ref[d, CK:, :] = packed
    last = pltpu.make_async_copy(
        send_ref.at[:, pl.ds(CK, CK), :], send_hbm.at[:, pl.ds(CK, CK), :], out_sems.at[2]
    )
    last.start()
    for copy in stores + [last]:
        copy.wait()


def packed_states(hr, hi):
    high, low = split(jnp.concatenate([hr, hi], 0))
    return jnp.concatenate([high, low], 0)


def unpacked_states(packed):
    packed = packed.astype(F32)
    values = packed[: 2 * GROUPS] + packed[2 * GROUPS :]
    return values[:GROUPS], values[GROUPS:]


def first(step, signal, cotangent, mix_weight, sizes, params, skip, table):
    return pl.pallas_call(
        first_kernel,
        in_specs=[SMEM] + [ANY] * 3 + [VMEM] * 7,
        out_specs=[ANY] * 2 + [VMEM] * 5,
        out_shape=(
            jax.ShapeDtypeStruct((RANKS, SEND1, LN), BF16),
            jax.ShapeDtypeStruct((CH, BLOCK + LN), BF16),
            jax.ShapeDtypeStruct((CK * GROUPS, LN), F32),
            jax.ShapeDtypeStruct((CK * GROUPS, LN), F32),
            jax.ShapeDtypeStruct((4, GROUPS, LN), F32),
            jax.ShapeDtypeStruct((5, GROUPS, LN), F32),
            jax.ShapeDtypeStruct((2, CH, LN), F32),
        ),
        scratch_shapes=[
            pltpu.VMEM((CH, BLOCK), BF16),
            pltpu.VMEM((CH, BLOCK + LN), BF16),
            pltpu.VMEM((RANKS, SEND1, LN), BF16),
            pltpu.VMEM((CH * CK, LN), F32),
            pltpu.VMEM((CH, MODES), F32),
            pltpu.SemaphoreType.DMA((3,)),
            pltpu.SemaphoreType.DMA((3,)),
        ],
        compiler_params=PARAMS,
        name="block_states",
    )(step, signal, cotangent, mix_weight, sizes, *params, skip, table)


def far_power(decay, turn, blocks):
    size = jnp.exp(-decay * (BLOCK * blocks))
    angle = turn * (BLOCK * blocks)
    return size * jnp.cos(angle), size * jnp.sin(angle)


def within_kernel(x_hbm, terms_ref, wide_ref, out_ref, far_r, far_i, x_ref, sems):
    loads = started(sems, (x_hbm.at[:, pl.ds(0, CK), :], x_ref))
    terms = terms_ref[0], terms_ref[1], terms_ref[2], terms_ref[3]
    decay, turn = terms[0], terms[1]
    near = [far_power(decay, turn, float(b)) for b in range(4)]
    for a in range(RANKS // 4):
        base = far_power(decay, turn, float(4 * a))
        for b in range(4):
            pr, pi = cmul(base[0], base[1], near[b][0], near[b][1]) if a and b else (
                base if a else near[b]
            )
            far_r[4 * a + b] = pr
            far_i[4 * a + b] = pi
    doubles = doublings(decay, turn)
    loads[0].wait()
    for g in range(GROUPS):
        taps = group_taps(terms, rising(decay, turn, doubles, g), g)
        for k in range(LANE_CH):
            c = g * LANE_CH + k
            matrix = toeplitz(taps[k : k + 1])
            high, low = split(matrix)
            x = x_ref[c]
            level = wide_ref[0, c : c + 1, :]
            out_ref[c * CK : (c + 1) * CK, :] = (
                dot(x, high) + dot(x, low) + level * jnp.sum(matrix, 0, keepdims=True)
            )


def within(send, terms, wide):
    return pl.pallas_call(
        within_kernel,
        in_specs=[ANY, VMEM, VMEM],
        out_shape=(
            jax.ShapeDtypeStruct((CH * CK, LN), F32),
            jax.ShapeDtypeStruct((RANKS, GROUPS, LN), F32),
            jax.ShapeDtypeStruct((RANKS, GROUPS, LN), F32),
        ),
        scratch_shapes=[pltpu.VMEM((CH, CK, LN), BF16), pltpu.SemaphoreType.DMA((1,))],
        compiler_params=PARAMS,
        name="within_chunks",
    )(send, terms, wide)


def mixed_back(group, parts, act_ref):
    mine = lax.broadcasted_iota(jnp.int32, (CH, LN), 1) == group * CH + lax.broadcasted_iota(
        jnp.int32, (CH, LN), 0
    )
    weights = jnp.concatenate([c[:, BLOCK:] for c in parts], 0)
    weights = dot(mine.astype(BF16), weights, NT).astype(BF16)
    for i in range(CK):
        cols = slice(i * LN, (i + 1) * LN)
        cot = jnp.concatenate([c[:, cols] for c in parts], 0)
        act_ref[pl.ds(i, CH, stride=CK), :] = dot(weights, cot)


def gelu_both(x):
    scale = np.float32(np.sqrt(2.0 / np.pi))
    square = x * x
    t = jnp.tanh(scale * (x + 0.044715 * (square * x)))
    half = 0.5 * (1.0 + t)
    slope = half + 0.5 * x * (1.0 - t * t) * (scale * (1.0 + (3.0 * 0.044715) * square))
    return x * half, slope


def entering(states, table_r, table_i, distance):
    hr = jnp.zeros((GROUPS, LN), F32)
    hi = jnp.zeros((GROUPS, LN), F32)
    for d in range(RANKS):
        steps = distance(d)
        sr, si = states(d)
        at = jnp.maximum(steps, 0)
        nr, ni = cmul(table_r[at], table_i[at], sr, si)
        hr = jnp.where(steps >= 0, hr + nr, hr)
        hi = jnp.where(steps >= 0, hi + ni, hi)
    return hr, hi


def second_kernel(
    me_ref, group_ref, c0h, c1h, c2h, c3h, out_hbm, got_hbm, x_hbm, terms_ref, wide_ref, far_r,
    far_i, sr_in, si_in, send_hbm, grad_hbm, mix_ref, sr_ref, si_ref,
    c0, c1, c2, c3, flat_ref, out_ref, got_ref, x_ref, act_ref, activation_ref, send_ref, grad_ref, sems, out_sems,
):
    loads = started(
        sems,
        (got_hbm.at[:, pl.ds(CK, CK), :], got_ref),
        (c0h, c0), (c1h, c1), (c2h, c2), (c3h, c3),
        (x_hbm.at[:, pl.ds(0, CK), :], x_ref),
        (out_hbm, out_ref),
    )
    me = me_ref[0]
    terms = terms_ref[0], terms_ref[1], terms_ref[2], terms_ref[3]
    decay, turn = terms[0], terms[1]
    doubles = doublings(decay, turn)
    zr, zi = power(decay, turn, float(LN))
    one_r, one_i = power(decay, turn, 1.0)
    ur, ui = cmul(2.0 * terms[2], 2.0 * terms[3], one_r, one_i)
    sr_ref[...] = sr_in[...]
    si_ref[...] = si_in[...]
    loads[0].wait()
    start = entering(lambda d: unpacked_states(got_ref[d]), far_r, far_i, lambda d: me - 1 - d)
    scan_states(sr_ref, si_ref, zr, zi, start[0], start[1], range(CK), True)
    for copy in loads[1:5]:
        copy.wait()
    mixed_back(group_ref[0], (c0, c1, c2, c3), act_ref)
    for copy in loads[5:]:
        copy.wait()
    stores = []
    for g in range(GROUPS):
        every = pl.ds(g, CK, stride=GROUPS)
        er, ei = rising(decay, turn, doubles, g)
        wr, wi = cmul(er, ei, ur[g : g + 1], ui[g : g + 1])
        inter = spread_group(sr_ref[every, :], si_ref[every, :], jnp.concatenate([wr, wi], 1))
        left = []
        for k in range(LANE_CH):
            c = g * LANE_CH + k
            rows = slice(c * CK, (c + 1) * CK)
            x = x_ref[c].astype(F32) + wide_ref[0, c : c + 1, :]
            mixed = out_ref[rows, :] + inter[k * CK : (k + 1) * CK] + wide_ref[1, c : c + 1, :] * x
            act, slope = gelu_both(mixed)
            activation_ref[rows, :] = act
            grad = act_ref[rows, :] * slope
            grad_ref[rows, :] = grad
            send_ref[c, :CK, :] = grad.astype(BF16)
            left.append(grad)
        stores.append(
            pltpu.make_async_copy(
                send_ref.at[pl.ds(g * LANE_CH, LANE_CH), pl.ds(0, CK), :],
                send_hbm.at[pl.ds(g * LANE_CH, LANE_CH), pl.ds(0, CK), :],
                out_sems.at[g],
            )
        )
        stores[-1].start()
        products = dot3(split(jnp.concatenate(left, 0)), split(jnp.concatenate([er, ei], 1)))
        pr, pi = gather_group(products)
        sr_ref[every, :] = pr
        si_ref[every, :] = pi
    zero = jnp.zeros((GROUPS, LN), F32)
    hr, hi = scan_states(sr_ref, si_ref, zr, zi, zero, zero, range(CK - 1, -1, -1), False)
    packed = packed_states(hr, hi)
    for d in range(RANKS):
        send_ref[d, CK:, :] = packed
    stores.append(
        pltpu.make_async_copy(
            send_ref.at[:, pl.ds(CK, CK), :], send_hbm.at[:, pl.ds(CK, CK), :],
            out_sems.at[GROUPS],
        )
    )
    stores[-1].start()
    stores.append(pltpu.make_async_copy(grad_ref, grad_hbm, out_sems.at[GROUPS + 1]))
    stores[-1].start()
    for i in range(CK):
        flat_ref[:, i * LN : (i + 1) * LN] = activation_ref[pl.ds(i, CH, stride=CK), :].astype(BF16)
    flat = flat_ref[...]
    mix_ref[...] = jnp.concatenate([dot(flat, c[:, :BLOCK], NT) for c in (c0, c1, c2, c3)], 1)
    for copy in stores:
        copy.wait()


def second(me, group, parts, out, got, send, terms, wide, far, sr, si):
    return pl.pallas_call(
        second_kernel,
        in_specs=[SMEM] * 2 + [ANY] * 7 + [VMEM] * 6,
        out_specs=[ANY] * 2 + [VMEM] * 3,
        out_shape=(
            jax.ShapeDtypeStruct((RANKS, SEND2, LN), BF16),
            jax.ShapeDtypeStruct((CH * CK, LN), F32),
            jax.ShapeDtypeStruct((CH, LN), F32),
            jax.ShapeDtypeStruct((CK * GROUPS, LN), F32),
            jax.ShapeDtypeStruct((CK * GROUPS, LN), F32),
        ),
        scratch_shapes=[pltpu.VMEM((CH, BLOCK + LN), BF16)] * 4
        + [
            pltpu.VMEM((CH, BLOCK), BF16),
            pltpu.VMEM((CH * CK, LN), F32),
            pltpu.VMEM((RANKS, CK, LN), BF16),
            pltpu.VMEM((CH, CK, LN), BF16),
            pltpu.VMEM((CH * CK, LN), F32),
            pltpu.VMEM((CH * CK, LN), F32),
            pltpu.VMEM((RANKS, SEND2, LN), BF16),
            pltpu.VMEM((CH * CK, LN), F32),
            pltpu.SemaphoreType.DMA((7,)),
            pltpu.SemaphoreType.DMA((GROUPS + 2,)),
        ],
        compiler_params=PARAMS,
        name="activation_and_states",
    )(me, group, *parts, out, got, send, terms, wide, far[0], far[1], sr, si)


def signal_kernel(
    me_ref, got_hbm, send_hbm, cot_hbm, after_hbm, terms_ref, wide_ref, far_r, far_i, sr_in, si_in,
    out_ref, sr_ref, si_ref, rows_ref, got_ref, send_ref, cot_ref, sems,
):
    loads = started(
        sems,
        (got_hbm.at[:, pl.ds(CK, CK), :], got_ref),
        (send_hbm, send_ref),
        (cot_hbm, cot_ref),
    )
    me = me_ref[0]
    terms = terms_ref[0], terms_ref[1], terms_ref[2], terms_ref[3]
    decay, turn = terms[0], terms[1]
    doubles = doublings(decay, turn)
    zr, zi = power(decay, turn, float(LN))
    one_r, one_i = power(decay, turn, 1.0)
    ur, ui = cmul(2.0 * terms[2], 2.0 * terms[3], one_r, one_i)

    sr_ref[...] = sr_in[...]
    si_ref[...] = si_in[...]
    loads[0].wait()
    start = entering(lambda d: unpacked_states(got_ref[d]), far_r, far_i, lambda d: d - me - 1)
    scan_states(sr_ref, si_ref, zr, zi, start[0], start[1], range(CK - 1, -1, -1), True)
    for copy in loads[1:]:
        copy.wait()
    for g in range(GROUPS):
        every = pl.ds(g, CK, stride=GROUPS)
        fr, fi = falling(decay, turn, doubles, g)
        wr, wi = cmul(fr, fi, ur[g : g + 1], ui[g : g + 1])
        inter = spread_group(sr_ref[every, :], si_ref[every, :], jnp.concatenate([wr, wi], 1))
        taps = group_taps(terms, rising(decay, turn, doubles, g), g)
        for k in range(LANE_CH):
            c = g * LANE_CH + k
            grad = send_ref[c * CK : (c + 1) * CK, :]
            rows_ref[c * CK : (c + 1) * CK, :] = (
                dot3(split(grad), split(toeplitz(taps[k : k + 1])), NT)
                + inter[k * CK : (k + 1) * CK]
                + wide_ref[1, c : c + 1, :] * grad
            )
    for i in range(CK):
        cols = slice(i * LN, (i + 1) * LN)
        out_ref[:, cols] = (
            cot_ref[:, cols].astype(F32) + rows_ref[pl.ds(i, CH, stride=CK), :]
        ).astype(BF16)


def signal_grad(me, got, send, terms, wide, far, sr, si, cotangent, after):
    return pl.pallas_call(
        signal_kernel,
        in_specs=[SMEM] + [ANY] * 4 + [VMEM] * 6,
        out_shape=jax.ShapeDtypeStruct((CH, BLOCK), BF16),
        scratch_shapes=[
            pltpu.VMEM((CK * GROUPS, LN), F32),
            pltpu.VMEM((CK * GROUPS, LN), F32),
            pltpu.VMEM((CH * CK, LN), F32),
            pltpu.VMEM((RANKS, CK, LN), BF16),
            pltpu.VMEM((CH * CK, LN), F32),
            pltpu.VMEM((CH, BLOCK), BF16),
            pltpu.SemaphoreType.DMA((3,)),
        ],
        compiler_params=PARAMS,
        name="signal_gradient",
    )(me, got, send, cotangent, after, terms, wide, far[0], far[1], sr, si)


def dft_tables():
    full_len = RANKS * BLOCK
    row = np.arange(ROWS)
    time_row = (row % RANKS) * (BLOCK // COLS) + row // RANKS
    first_ids = np.arange(ROWS)
    column = np.arange(COLS)
    angle1 = (
        2.0 * np.pi * (((4 * first_ids[:, None] + 1) * time_row[None, :]) % (4 * ROWS)) / (4 * ROWS)
    )
    angle_t = 2.0 * np.pi * ((4 * first_ids[:, None] + 1) * column[None, :]) / (4 * full_len)
    lane = np.arange(LN)
    angle2 = 2.0 * np.pi * ((lane[:, None] * lane[None, :]) % LN) / LN
    angle_p = 2.0 * np.pi * np.arange(PER)[:, None] * lane[None, :] / COLS

    def halves(values):
        values = values.astype(np.float32)
        high = values.astype(BF16)
        return high, (values - high.astype(np.float32)).astype(BF16)

    stage1 = np.concatenate([np.cos(angle1), -np.sin(angle1)], 0)
    cos2, sin2 = np.cos(angle2), np.sin(angle2)
    stage2 = np.concatenate(
        [np.concatenate([cos2, -sin2], 1), np.concatenate([sin2, cos2], 1)], 0
    )
    twiddle = np.stack([np.cos(angle_t), np.sin(angle_t)]).astype(np.float32)
    steps = np.concatenate([np.cos(angle_p), np.sin(angle_p)], 0).astype(np.float32)
    return halves(stage1), halves(stage1.T / full_len), halves(stage2), twiddle, steps


def gather_rows(ref, stride, base):
    return jnp.concatenate(
        [
            jnp.concatenate(
                [
                    ref[pl.ds(base + piece * PER + q, RANKS, stride=stride), :]
                    for q in range(PER)
                ],
                1,
            )
            for piece in range(BLOCK // COLS)
        ],
        0,
    )


def butterfly(parts, sign):
    (r0, i0), (r1, i1), (r2, i2), (r3, i3) = parts
    sr, si, dr, di = r0 + r2, i0 + i2, r0 - r2, i0 - i2
    tr, ti, er, ei = r1 + r3, i1 + i3, r1 - r3, i1 - i3
    if sign > 0:
        er, ei = -er, -ei
    return (sr + tr, si + ti), (dr + ei, di - er), (sr - tr, si - ti), (dr - ei, di + er)


def forward_dft(rows, exact, d1h, d1l, d2h, d2l, twiddle, steps, wait1, wait2):
    xh, xl = split(rows)
    wait1()
    a = dot(d1h[...], xh) + dot(d1l[...], xh)
    if not exact:
        a = a + dot(d1h[...], xl)
    wait2()
    parts = []
    for q in range(PER):
        cols = slice(q * LN, (q + 1) * LN)
        parts.append(cmul(a[:ROWS, cols], a[ROWS:, cols], twiddle[0, :, cols], -twiddle[1, :, cols]))
    out = []
    for p, (ur, ui) in enumerate(butterfly(parts, -1)):
        if p:
            ur, ui = cmul(ur, ui, steps[p : p + 1, :], -steps[PER + p : PER + p + 1, :])
        out.append(jnp.concatenate([ur, ui], 1))
    return dot3(split(jnp.concatenate(out, 0)), (d2h[...], d2l[...]))


def inverse_dft(spec, d1th, d1tl, d2h, d2l, twiddle, steps):
    v = dot3(split(spec), (d2h[...], d2l[...]), NT)
    parts = []
    for p in range(PER):
        vr, vi = v[p * ROWS : (p + 1) * ROWS, :LN], v[p * ROWS : (p + 1) * ROWS, LN:]
        if p:
            vr, vi = cmul(vr, vi, steps[p : p + 1, :], steps[PER + p : PER + p + 1, :])
        parts.append((vr, vi))
    real, imag = [], []
    for q, (br, bi) in enumerate(butterfly(parts, 1)):
        cols = slice(q * LN, (q + 1) * LN)
        br, bi = cmul(br, bi, twiddle[0, :, cols], twiddle[1, :, cols])
        real.append(br)
        imag.append(bi)
    bh, bl = split(
        jnp.concatenate([jnp.concatenate(real, 1), jnp.concatenate(imag, 1)], 0)
    )
    return dot(d1th[...], bh) + dot(d1th[...], bl) + dot(d1tl[...], bh)


def lane_block(row):
    return lax.broadcasted_iota(jnp.int32, row.shape, 1) // MODES


def repeated(row):
    row = jnp.where(lane_block(row) == 0, row, 0.0)
    total = row
    for m in range(1, LANE_CH):
        total = total + pltpu.roll(row, m * MODES, 1)
    return total


def by_block(rows):
    result = rows[0]
    for m in range(1, LANE_CH):
        result = jnp.where(lane_block(result) == m, rows[m], result)
    return result


def waiting(copies):
    def wait():
        for copy in copies:
            copy.wait()

    return wait


def spectrum_kernel(
    me_ref, got_hbm, d1h_hbm, d1l_hbm, twiddle_hbm, d2h_hbm, d2l_hbm, after_hbm,
    steps_ref, wide_ref, raw_ref, spec_ref, column_ref, turn_ref, pull_ref,
    got_ref, d1h, d1l, twiddle, d2h, d2l, rows_ref, sems,
):
    loads = started(
        sems,
        (got_hbm.at[:, pl.ds(0, CK), :], got_ref),
        (d1h_hbm, d1h), (d1l_hbm, d1l), (twiddle_hbm, twiddle), (d2h_hbm, d2h), (d2l_hbm, d2l),
    )
    me = me_ref[0]
    embed = wide_ref[0, pl.ds(me, 1), :]
    loads[0].wait()
    for d in range(RANKS):
        rows_ref[d * CK : (d + 1) * CK, :] = got_ref[d].astype(F32) + embed
    rows = gather_rows(rows_ref, CK, 0)
    spec_ref[...] = forward_dft(
        rows, False, d1h, d1l, d2h, d2l, twiddle, steps_ref, waiting(loads[1:3]),
        waiting(loads[3:6]),
    )

    at, shift = me // LANE_CH, (me % LANE_CH) * MODES

    def own(k):
        row = jnp.broadcast_to(raw_ref[k, pl.ds(at, 1), :], (8, LN))
        return repeated(pltpu.roll(row, (LN - shift) % LN, 1)[:1])

    raw = [own(k) for k in range(5)]
    (d, th, mr, mi), pull = jax.vjp(mode_terms, *raw)
    zero = jnp.zeros((1, LN), F32)
    pulled = [
        pull((zero, zero, zero + 2.0, zero)),
        pull((zero, zero, zero, zero - 2.0)),
        pull((-2.0 * mr, -2.0 * mi, zero, zero)),
        pull((2.0 * mi, -2.0 * mr, zero, zero)),
    ]
    inverse = 1.0 / (raw[1] * raw[1] + raw[2] * raw[2])
    qr, qi = cmul(raw[3], raw[4], raw[1] * inverse, raw[2] * inverse)
    one_r, one_i = power(d, th, 1.0)
    er, ei = cmul(qr, qi, one_r, one_i)
    first_lanes = lane_block(zero) == 0
    pull_ref[...] = jnp.concatenate(
        [by_block(p[1:]) for p in pulled]
        + [jnp.where(first_lanes, p[0] * raw[0], 0.0) for p in pulled]
        + [jnp.where(first_lanes, v, 0.0) for v in (2.0 * qr, -2.0 * er, 2.0 * ei)]
        + [wide_ref[1, pl.ds(me, 1), :]]
        + [jnp.zeros((4, LN), F32)],
        0,
    )
    steps = lax.broadcasted_iota(jnp.int32, (8, LN), 0).astype(F32)
    cr, ci = power(d, th, steps)
    for k in (8, 16, 32, 64, 128, 256):
        zr, zi = far_power(d, th, float(k) / BLOCK)
        nr, ni = cmul(cr, ci, zr, zi)
        cr, ci = jnp.concatenate([cr, nr], 0), jnp.concatenate([ci, ni], 0)
    col = lax.broadcasted_iota(jnp.int32, (COLS, LN), 0).astype(F32)
    block = lane_block(col)
    table = jnp.where(block % 2 == 0, cr, ci)
    column_ref[...] = jnp.where(block < 2, table, table * col)
    ranks = lax.broadcasted_iota(jnp.int32, (RANKS, LN), 0).astype(F32)
    br, bi = far_power(d, th, ranks)
    for piece in range(BLOCK // COLS):
        zr, zi = far_power(d, th, float(piece * COLS) / BLOCK)
        nr, ni = cmul(br, bi, zr, zi) if piece else (br, bi)
        turn_ref[0, piece * RANKS : (piece + 1) * RANKS, :] = nr
        turn_ref[1, piece * RANKS : (piece + 1) * RANKS, :] = ni


def spectrum(me, got, after, wide, raw, tables):
    (d1h, d1l), unused, (d2h, d2l), twiddle, steps = tables
    return pl.pallas_call(
        spectrum_kernel,
        in_specs=[SMEM] + [ANY] * 7 + [VMEM] * 3,
        out_shape=(
            jax.ShapeDtypeStruct((PER * ROWS, 2 * LN), F32),
            jax.ShapeDtypeStruct((COLS, LN), F32),
            jax.ShapeDtypeStruct((2, ROWS, LN), F32),
            jax.ShapeDtypeStruct((16, LN), F32),
        ),
        scratch_shapes=[
            pltpu.VMEM((RANKS, CK, LN), BF16),
            pltpu.VMEM((2 * ROWS, ROWS), BF16),
            pltpu.VMEM((2 * ROWS, ROWS), BF16),
            pltpu.VMEM((2, ROWS, COLS), F32),
            pltpu.VMEM((2 * LN, 2 * LN), BF16),
            pltpu.VMEM((2 * LN, 2 * LN), BF16),
            pltpu.VMEM((RANKS * CK, LN), F32),
            pltpu.SemaphoreType.DMA((6,)),
        ],
        compiler_params=PARAMS,
        name="input_spectrum",
    )(me, got, d1h, d1l, twiddle, d2h, d2l, after, steps, wide, raw)


def correlate_kernel(
    got_hbm, d1h_hbm, d1l_hbm, twiddle_hbm, d2h_hbm, d2l_hbm, spec_hbm, d1th_hbm, d1tl_hbm,
    column_hbm, turn_hbm, steps_ref, pull_ref, m0, m1, m2, m3, send_hbm, after_ref,
    got_ref, d1h, d1l, twiddle, d2h, d2l, spec_ref, d1th, d1tl, column_ref, turn_ref,
    rows_ref, send_ref, sems, out_sems,
):
    loads = started(
        sems,
        (got_hbm.at[:, pl.ds(0, CK), :], got_ref),
        (d1h_hbm, d1h), (d1l_hbm, d1l), (twiddle_hbm, twiddle), (d2h_hbm, d2h), (d2l_hbm, d2l),
        (spec_hbm, spec_ref), (d1th_hbm, d1th), (d1tl_hbm, d1tl), (column_hbm, column_ref),
        (turn_hbm, turn_ref),
    )
    mixes = by_block([m[...] for m in (m0, m1, m2, m3)]).astype(BF16)
    for d in range(RANKS):
        send_ref[d, CK : 2 * CK, :] = mixes
    middle = pl.ds(CK, CK)
    stores = started(out_sems, (send_ref.at[:, middle, :], send_hbm.at[:, middle, :]))
    loads[0].wait()
    for d in range(RANKS):
        rows_ref[d * CK : (d + 1) * CK, :] = got_ref[d].astype(F32)
    g_rows = gather_rows(rows_ref, CK, 0)
    g_spec = forward_dft(
        g_rows, True, d1h, d1l, d2h, d2l, twiddle, steps_ref, waiting(loads[1:3]),
        waiting(loads[3:6]),
    )
    waiting(loads[6:7])()
    gr, gi = g_spec[:, :LN], g_spec[:, LN:]
    xr, xi = spec_ref[:, :LN], spec_ref[:, LN:]
    both = jnp.concatenate([xr * gr + xi * gi, xr * gi - xi * gr], 1)
    waiting(loads[7:])()
    kernel_rows = inverse_dft(both, d1th, d1tl, d2h, d2l, twiddle, steps_ref)
    for piece in range(BLOCK // COLS):
        for q in range(PER):
            rows_ref[pl.ds(piece * PER + q, RANKS, stride=CK), :] = kernel_rows[
                piece * RANKS : (piece + 1) * RANKS, q * LN : (q + 1) * LN
            ]
    for d in range(RANKS):
        send_ref[d, :CK, :] = rows_ref[d * CK : (d + 1) * CK, :].astype(BF16)
    stores.append(
        pltpu.make_async_copy(
            send_ref.at[:, pl.ds(0, CK), :], send_hbm.at[:, pl.ds(0, CK), :], out_sems.at[1]
        )
    )
    stores[-1].start()
    both = dot3(split(jnp.concatenate([kernel_rows, g_rows], 0)), split(column_ref[...]))
    inner = both[:ROWS]
    rr, ri = turn_ref[0], turn_ref[1]
    ids = lax.broadcasted_iota(jnp.int32, (ROWS, LN), 0)
    starts = ((ids % RANKS) * BLOCK + (ids // RANKS) * COLS).astype(F32)

    def total(values):
        return jnp.sum(values, 0, keepdims=True)

    by_r, by_i = rr * inner, ri * inner
    u, v = total(by_r), total(by_i)
    su, sv = total(starts * by_r), total(starts * by_i)
    gu, gv = total(rr * both[ROWS:]), total(ri * both[ROWS:])

    def block(row, k):
        moved = pltpu.roll(row, (LN - k * MODES) % LN, 1) if k else row
        return jnp.where(lane_block(row) == 0, moved, 0.0)

    cos_sum = block(u, 0) - block(v, 1)
    sin_sum = block(u, 1) + block(v, 0)
    cos_moment = block(u, 2) - block(v, 3) + block(su, 0) - block(sv, 1)
    sin_moment = block(u, 3) + block(v, 2) + block(su, 1) + block(sv, 0)
    grads = jnp.zeros((1, LN), F32)
    step = jnp.zeros((1, LN), F32)
    for k, value in enumerate((cos_sum, sin_sum, cos_moment, sin_moment)):
        grads = grads + pull_ref[k : k + 1, :] * repeated(value)
        step = step + pull_ref[4 + k : 5 + k, :] * value
    step_sum = jnp.sum(step, 1, keepdims=True)
    skip_sum = kernel_rows[0:1, 0:1]
    g_sum = jnp.sum(total(g_rows), 1, keepdims=True)
    back_sum = jnp.sum(
        pull_ref[8:9, :] * g_sum
        + pull_ref[9:10, :] * (block(gu, 0) - block(gv, 1))
        + pull_ref[10:11, :] * (block(gu, 1) + block(gv, 0)),
        1,
        keepdims=True,
    )
    lanes = lax.broadcasted_iota(jnp.int32, (1, LN), 1)
    scalars = (
        jnp.where(lanes == 0, step_sum, 0.0)
        + jnp.where(lanes == 1, skip_sum, 0.0)
        + jnp.where(lanes == 2, back_sum + pull_ref[11:12, :] * g_sum, 0.0)
    )
    small = jnp.concatenate([grads, scalars, jnp.zeros((6, LN), F32)], 0)
    after_ref[...] = small
    high, low = split(jnp.concatenate([small, small], 0))
    upper = lax.broadcasted_iota(jnp.int32, (16, LN), 0) < 8
    packed = jnp.where(upper, high.astype(F32), low.astype(F32)).astype(BF16)
    for d in range(RANKS):
        send_ref[d, 2 * CK :, :] = packed
    stores.append(
        pltpu.make_async_copy(
            send_ref.at[:, pl.ds(2 * CK, 16), :], send_hbm.at[:, pl.ds(2 * CK, 16), :],
            out_sems.at[2],
        )
    )
    stores[-1].start()
    for copy in stores:
        copy.wait()


def correlate(got, spec, tables, column, turns, pull, mixes):
    (d1h, d1l), (d1th, d1tl), (d2h, d2l), twiddle, steps = tables
    return pl.pallas_call(
        correlate_kernel,
        in_specs=[ANY] * 11 + [VMEM] * 6,
        out_specs=[ANY, VMEM],
        out_shape=(
            jax.ShapeDtypeStruct((RANKS, SEND3, LN), BF16),
            jax.ShapeDtypeStruct((8, LN), F32),
        ),
        scratch_shapes=[
            pltpu.VMEM((RANKS, CK, LN), BF16),
            pltpu.VMEM((2 * ROWS, ROWS), BF16),
            pltpu.VMEM((2 * ROWS, ROWS), BF16),
            pltpu.VMEM((2, ROWS, COLS), F32),
            pltpu.VMEM((2 * LN, 2 * LN), BF16),
            pltpu.VMEM((2 * LN, 2 * LN), BF16),
            pltpu.VMEM((PER * ROWS, 2 * LN), F32),
            pltpu.VMEM((ROWS, 2 * ROWS), BF16),
            pltpu.VMEM((ROWS, 2 * ROWS), BF16),
            pltpu.VMEM((COLS, LN), F32),
            pltpu.VMEM((2, ROWS, LN), F32),
            pltpu.VMEM((RANKS * CK, LN), F32),
            pltpu.VMEM((RANKS, SEND3, LN), BF16),
            pltpu.SemaphoreType.DMA((11,)),
            pltpu.SemaphoreType.DMA((3,)),
        ],
        compiler_params=PARAMS,
        name="correlation",
    )(got, d1h, d1l, twiddle, d2h, d2l, spec, d1th, d1tl, column, turns, steps, pull, *mixes)


def outputs_kernel(
    step_ref, group_ref, got_ref, kernel_ref, damping_ref, frequency_ref, re_ref, im_ref,
    size_ref, skip_ref, mix_ref, table_ref, rows_ref, turned_ref,
):
    mixes = jnp.zeros((CH, LN), F32)
    for c in range(CH):
        rows_ref[c * CK : (c + 1) * CK, :] = got_ref[c, :CK, :].astype(F32)
        mixes = mixes + got_ref[c, CK : 2 * CK, :].astype(F32)
    for i in range(CK):
        kernel_ref[:, i * LN : (i + 1) * LN] = rows_ref[pl.ds(i, CH, stride=CK), :]
    for c in range(CH):
        small = got_ref[c, 2 * CK :, :].astype(F32)
        rows_ref[c * 8 : (c + 1) * 8, :] = small[:8] + small[8:]
    grads = rows_ref[pl.ds(0, CH, stride=8), :]
    for k, ref in enumerate((damping_ref, frequency_ref, re_ref, im_ref)):
        ref[...] = grads[:, k * MODES : (k + 1) * MODES]
    scalars = rows_ref[pl.ds(1, CH, stride=8), :]
    turned = jnp.concatenate([scalars, jnp.zeros((LN - CH, LN), F32)], 0).T
    size_ref[...] = turned[0:1, :CH]
    skip_ref[...] = turned[1:2, :CH]
    picked = lax.broadcasted_iota(jnp.int32, table_ref.shape, 1) == step_ref[0]
    table_ref[...] = jnp.where(picked, scalars[:, 2:3], 0.0)
    turned_ref[...] = jnp.concatenate([mixes, jnp.zeros((LN - CH, LN), F32)], 0).T
    mix_ref[...] = jnp.concatenate(
        [
            turned_ref[pl.ds(pl.multiple_of((group_ref[0] ^ c) * CH, CH), CH), :][:, :CH]
            for c in range(LN // CH)
        ],
        1,
    )


def outputs(step, group, got, table_len):
    wide = jax.ShapeDtypeStruct((CH, MODES), F32)
    row = jax.ShapeDtypeStruct((1, CH), F32)
    return pl.pallas_call(
        outputs_kernel,
        in_specs=[SMEM, SMEM, VMEM],
        out_shape=(
            jax.ShapeDtypeStruct((CH, BLOCK), F32),
            wide, wide, wide, wide, row, row,
            jax.ShapeDtypeStruct((CH, LN), F32),
            jax.ShapeDtypeStruct((CH, table_len), F32),
        ),
        scratch_shapes=[pltpu.VMEM((CH * CK, LN), F32), pltpu.VMEM((LN, LN), F32)],
        compiler_params=PARAMS,
        name="outputs",
    )(step, group, got)


def exchange(values):
    return lax.all_to_all(values, "tm", split_axis=0, concat_axis=0, tiled=True)


def shards(
    signal,
    cotangent,
    log_step,
    damping,
    frequency,
    coef_re,
    coef_im,
    skip_gain,
    mix_weight,
    embed_table,
    diffusion_step,
):
    me = lax.axis_index("tm").reshape(1)
    group = lax.axis_index("chan").reshape(1)
    tables = dft_tables()

    def swap(values, mask):
        return lax.ppermute(values, "chan", [(i, i ^ mask) for i in range(4)])

    send1, own, sr, si, terms, raw, wide = first(
        diffusion_step, signal, cotangent, mix_weight, log_step[None],
        (damping, frequency, coef_re, coef_im), skip_gain[None], embed_table.T,
    )
    got1 = exchange(send1)
    own, across = lax.optimization_barrier((own, swap(own, 2)))
    parts = (own, swap(own, 1), across, swap(across, 1))
    out, far_r, far_i = within(send1, terms, wide)
    far = (far_r, far_i)
    send2, grad, mix, br, bi = second(me, group, parts, out, got1, send1, terms, wide, far, sr, si)
    got2 = exchange(send2)
    mixes = [mix] + [swap(mix, m) for m in range(1, 4)]
    spec, column, turns, pull = spectrum(me, got1, mix, wide, raw, tables)
    send3, after = correlate(got2, spec, tables, column, turns, pull, mixes)
    got3 = exchange(send3)
    grad_signal = signal_grad(me, got2, grad, terms, wide, far, br, bi, cotangent, after)
    kernel, g_damping, g_frequency, g_re, g_im, g_size, g_skip, g_mix, g_table = outputs(
        diffusion_step, group, got3, embed_table.shape[0]
    )
    return (
        grad_signal,
        kernel,
        g_size[0],
        g_damping,
        g_frequency,
        g_re,
        g_im,
        g_skip[0],
        g_mix,
        g_table.T,
    )


def solution(mesh):
    placed = (
        P("chan", "tm"),
        P("chan", "tm"),
        P("chan"),
        P("chan", None),
        P("chan", None),
        P("chan", None),
        P("chan", None),
        P("chan"),
        P("chan", None),
        P(None, "chan"),
        P(),
    )
    return jax.shard_map(
        shards,
        mesh=mesh,
        in_specs=placed,
        out_specs=(
            P("chan", "tm"),
            P("chan", "tm"),
            P("chan"),
            P("chan", None),
            P("chan", None),
            P("chan", None),
            P("chan", None),
            P("chan"),
            P("chan", None),
            P(None, "chan"),
        ),
        check_vma=False,
    )
```

```python
import functools

import jax
import jax.numpy as jnp
import numpy as np
from jax import lax
from jax.experimental import pallas as pl
from jax.experimental.pallas import tpu as pltpu
from jax.sharding import PartitionSpec as P

HIGHEST = lax.Precision.HIGHEST
F32 = jnp.float32
BF16 = jnp.bfloat16

CH = 32
MODES = 32
BLOCK = 4096
LN = 128
CK = BLOCK // LN
LANE_CH = LN // MODES
GROUPS = CH // LANE_CH
RANKS = 32
COLS = 512
PER = COLS // LN
ROWS = RANKS * BLOCK // COLS
SEND1 = 64
SEND2 = 64
SEND3 = 80
NT = (((1,), (1,)), ((), ()))
NN = (((1,), (0,)), ((), ()))
GRANT = 63.75
SMEM = pl.BlockSpec(memory_space=pltpu.SMEM)
VMEM = pl.BlockSpec(memory_space=pltpu.VMEM)
ANY = pl.BlockSpec(memory_space=pl.ANY)
HBM = pl.BlockSpec(memory_space=pltpu.HBM)


def expm1_small(x):
    r = 1.0
    for k in (7.0, 6.0, 5.0, 4.0, 3.0, 2.0):
        r = 1.0 + x * r * (1.0 / k)
    return x * r


def mode_terms(step_size, damping, frequency, coef_re, coef_im):
    decay_rate = step_size * damping
    turn_rate = step_size * frequency
    half_sine = jnp.sin(0.5 * turn_rate)
    grow_real = expm1_small(-decay_rate) * jnp.cos(turn_rate) - 2.0 * half_sine * half_sine
    grow_imag = jnp.exp(-decay_rate) * jnp.sin(turn_rate)
    inverse = 1.0 / (damping * damping + frequency * frequency)
    hold_real = (frequency * grow_imag - damping * grow_real) * inverse
    hold_imag = -(frequency * grow_real + damping * grow_imag) * inverse
    weight_real = coef_re * hold_real - coef_im * hold_imag
    weight_imag = coef_re * hold_imag + coef_im * hold_real
    return (decay_rate, turn_rate, weight_real, weight_imag)


def cmul(ar, ai, br, bi):
    return ar * br - ai * bi, ar * bi + ai * br


def split(values):
    high = values.astype(BF16)
    return high, (values - high.astype(F32)).astype(BF16)


def dot(left, right, dims=NN):
    return lax.dot_general(left, right, dims, preferred_element_type=F32)


def dot3(left, right, dims=NN):
    (lh, ll), (rh, rl) = left, right
    (axis,), (other,) = dims[0]
    return dot(
        jnp.concatenate([lh, ll, lh], axis), jnp.concatenate([rh, rh, rl], other), dims
    )


def dot2(left, right, dims=NN):
    (axis,), (other,) = dims[0]
    return dot(jnp.concatenate([left, left], axis), jnp.concatenate(right, other), dims)


def started(sems, *pairs):
    copies = [pltpu.make_async_copy(a, b, sems.at[k]) for k, (a, b) in enumerate(pairs)]
    for copy in copies:
        copy.start()
    return copies


def waiting(copies):
    def wait():
        for copy in copies:
            copy.wait()

    return wait


def staged(
    kernel, scalars, plain, small, *, out_specs, out_shape, scratch_shapes, name,
    plain_spec=HBM, limit=GRANT,
):
    heads, outs = len(scalars) + len(plain), len(out_shape)

    def body(*refs):
        given, rest = refs[:heads], refs[heads:]
        sources, rest = rest[: len(small)], rest[len(small) :]
        results, rest = rest[:outs], rest[outs:]
        held, sems, rest = rest[: len(small)], rest[len(small)], rest[len(small) + 1 :]
        copies = started(sems, *zip(sources, held))
        kernel(waiting(copies), *given, *held, *results, *rest)

    return pl.pallas_call(
        body,
        in_specs=[SMEM] * len(scalars) + [plain_spec] * len(plain) + [HBM] * len(small),
        out_specs=out_specs,
        out_shape=out_shape,
        scratch_shapes=[pltpu.VMEM(a.shape, a.dtype) for a in small]
        + [pltpu.SemaphoreType.DMA((len(small),))]
        + scratch_shapes,
        compiler_params=pltpu.CompilerParams(vmem_limit_bytes=int(limit * 1024 * 1024)),
        name=name,
    )(*scalars, *plain, *small)


def sin_cos(x):
    y = x * x
    s = 1.0
    for k in (210.0, 156.0, 110.0, 72.0, 42.0, 20.0, 6.0):
        s = 1.0 - y * s * (1.0 / k)
    c = 1.0
    for k in (240.0, 182.0, 132.0, 90.0, 56.0, 30.0, 12.0, 2.0):
        c = 1.0 - y * c * (1.0 / k)
    return x * s, c


def power(decay, turn, steps):
    size = jnp.exp(-decay * steps)
    s, c = sin_cos(turn * steps)
    return size * c, size * s


def doublings(decay, turn):
    return [power(decay, turn, float(k)) for k in (8, 16, 32, 64)]


def rising(decay, turn, doubles, g):
    rows = lax.broadcasted_iota(jnp.int32, (8, LN), 0).astype(F32)
    tr, ti = power(decay[g : g + 1], turn[g : g + 1], rows)
    for zr, zi in doubles:
        nr, ni = cmul(tr, ti, zr[g : g + 1], zi[g : g + 1])
        tr, ti = jnp.concatenate([tr, nr], 0), jnp.concatenate([ti, ni], 0)
    return tr, ti


def falling(decay, turn, doubles, g):
    rows = 7.0 - lax.broadcasted_iota(jnp.int32, (8, LN), 0).astype(F32)
    tr, ti = power(decay[g : g + 1], turn[g : g + 1], rows)
    for zr, zi in doubles:
        nr, ni = cmul(tr, ti, zr[g : g + 1], zi[g : g + 1])
        tr, ti = jnp.concatenate([nr, tr], 0), jnp.concatenate([ni, ti], 0)
    return tr, ti


def lane_channel(shape):
    return lax.broadcasted_iota(jnp.int32, shape, 1) // MODES


def gather_group(products):
    owner = lane_channel((CK, LN))
    real, imag = products[:, :LN], products[:, LN:]
    out_r, out_i = real[:CK], imag[:CK]
    for k in range(1, LANE_CH):
        mine = owner == k
        out_r = jnp.where(mine, real[k * CK : (k + 1) * CK], out_r)
        out_i = jnp.where(mine, imag[k * CK : (k + 1) * CK], out_i)
    return out_r, out_i


def spread_group(state_r, state_i, table):
    owner = lane_channel((CK, LN))
    zero = jnp.zeros((CK, LN), F32)
    left = jnp.concatenate(
        [
            jnp.concatenate(
                [jnp.where(owner == k, state_r, zero), jnp.where(owner == k, -state_i, zero)], 1
            )
            for k in range(LANE_CH)
        ],
        0,
    )
    return dot3(split(left), split(table), NT)


def scan_states(sr_ref, si_ref, power_r, power_i, order):
    hr = jnp.zeros((GROUPS, LN), F32)
    hi = jnp.zeros((GROUPS, LN), F32)
    for i in order:
        rows = pl.ds(i * GROUPS, GROUPS)
        own_r, own_i = sr_ref[rows, :], si_ref[rows, :]
        sr_ref[rows, :] = hr
        si_ref[rows, :] = hi
        nr, ni = cmul(power_r, power_i, hr, hi)
        hr, hi = nr + own_r, ni + own_i
    return hr, hi


def add_entering(sr_ref, si_ref, sr_in, si_in, step_r, step_i, start, order):
    for k, i in enumerate(order):
        rows = pl.ds(i * GROUPS, GROUPS)
        nr, ni = cmul(step_r[k], step_i[k], *start) if k else start
        sr_ref[rows, :] = sr_in[rows, :] + nr
        si_ref[rows, :] = si_in[rows, :] + ni


def toeplitz(taps_row):
    rows = jnp.broadcast_to(taps_row, (LN, LN))
    turned = pltpu.roll(rows, 0, 1, stride=1, stride_axis=0)
    lag = lax.broadcasted_iota(jnp.int32, (LN, LN), 1) - lax.broadcasted_iota(
        jnp.int32, (LN, LN), 0
    )
    return jnp.where(lag >= 0, turned, 0.0)


def group_taps(terms, table, g):
    real = 2.0 * (terms[2][g : g + 1] * table[0] - terms[3][g : g + 1] * table[1])
    owner = (
        lane_channel((8, LN)) == lax.broadcasted_iota(jnp.int32, (8, LN), 0)
    ).astype(BF16)
    high, low = split(real)
    return dot2(owner, (high, low), NT)


def packed_lanes(ref):
    return jnp.concatenate([ref[pl.ds(k, GROUPS, stride=LANE_CH), :] for k in range(LANE_CH)], 1)


def as_column(row):
    shape = (CH, CH)
    same = lax.broadcasted_iota(jnp.int32, shape, 0) == lax.broadcasted_iota(jnp.int32, shape, 1)
    return jnp.sum(jnp.where(same, row, 0.0), 1, keepdims=True)


def first_kernel(
    wait_small, step_ref, signal_hbm, cot_hbm, mix_hbm, size_ref, damping_ref, frequency_ref, re_ref, im_ref,
    skip_ref, table_ref, send_hbm, own_hbm, sr_ref, si_ref, terms_ref, wide_ref,
    signal_ref, own_ref, send_ref, rows_ref, pack_ref, sems, out_sems,
):
    loads = started(
        sems,
        (signal_hbm, signal_ref),
        (cot_hbm, own_ref.at[:, pl.ds(0, BLOCK)]),
        (mix_hbm, own_ref.at[:, pl.ds(BLOCK, LN)]),
    )
    wait_small()
    picked = lax.broadcasted_iota(jnp.int32, table_ref.shape, 1) == step_ref[0]
    embed = jnp.sum(jnp.where(picked, table_ref[...], 0.0), 1, keepdims=True)
    wide_ref[0] = jnp.broadcast_to(embed, (CH, LN))
    wide_ref[1] = jnp.broadcast_to(as_column(skip_ref[...]), (CH, LN))
    pack_ref[...] = jnp.broadcast_to(embed, (CH, MODES))
    embed_lanes = packed_lanes(pack_ref)
    pack_ref[...] = jnp.broadcast_to(as_column(jnp.exp(size_ref[...])), (CH, MODES))
    raw = [packed_lanes(r) for r in (pack_ref, damping_ref, frequency_ref, re_ref, im_ref)]
    terms = mode_terms(*raw)
    for k in range(4):
        terms_ref[k] = terms[k]
    decay, turn = terms[0], terms[1]
    doubles = doublings(decay, turn)
    loads[0].wait()
    for i in range(CK):
        rows_ref[pl.ds(i, CH, stride=CK), :] = signal_ref[:, i * LN : (i + 1) * LN].astype(F32)
    for c in range(CH):
        send_ref[c, :CK, :] = rows_ref[c * CK : (c + 1) * CK, :].astype(BF16)
    loads[1].wait()
    loads[2].wait()
    stores = started(
        out_sems,
        (send_ref.at[:, pl.ds(0, CK), :], send_hbm.at[:, pl.ds(0, CK), :]),
        (own_ref, own_hbm),
    )
    for g in range(GROUPS):
        x = rows_ref[g * LN : (g + 1) * LN, :].astype(BF16)
        fr, fi = falling(decay, turn, doubles, g)
        table = jnp.concatenate([fr, fi], 1)
        th, tl = split(table)
        pr, pi = gather_group(dot2(x, (th, tl)))
        level = embed_lanes[g : g + 1]
        sr_ref[pl.ds(g, CK, stride=GROUPS), :] = pr + level * jnp.sum(fr, 0, keepdims=True)
        si_ref[pl.ds(g, CK, stride=GROUPS), :] = pi + level * jnp.sum(fi, 0, keepdims=True)
    zr, zi = power(decay, turn, float(LN))
    hr, hi = scan_states(sr_ref, si_ref, zr, zi, range(CK))
    packed = packed_states(hr, hi)
    for d in range(RANKS):
        send_ref[d, CK:, :] = packed
    last = pltpu.make_async_copy(
        send_ref.at[:, pl.ds(CK, CK), :], send_hbm.at[:, pl.ds(CK, CK), :], out_sems.at[2]
    )
    last.start()
    for copy in stores + [last]:
        copy.wait()


def packed_states(hr, hi):
    high, low = split(jnp.concatenate([hr, hi], 0))
    return jnp.concatenate([high, low], 0)


def unpacked_states(packed):
    packed = packed.astype(F32)
    values = packed[: 2 * GROUPS] + packed[2 * GROUPS :]
    return values[:GROUPS], values[GROUPS:]


def first(step, signal, cotangent, mix_weight, sizes, params, skip, table):
    return staged(
        first_kernel,
        (step,),
        (signal, cotangent, mix_weight),
        (sizes, *params, skip, table),
        out_specs=[ANY] * 2 + [VMEM] * 4,
        out_shape=(
            jax.ShapeDtypeStruct((RANKS, SEND1, LN), BF16),
            jax.ShapeDtypeStruct((CH, BLOCK + LN), BF16),
            jax.ShapeDtypeStruct((CK * GROUPS, LN), F32),
            jax.ShapeDtypeStruct((CK * GROUPS, LN), F32),
            jax.ShapeDtypeStruct((4, GROUPS, LN), F32),
            jax.ShapeDtypeStruct((2, CH, LN), F32),
        ),
        scratch_shapes=[
            pltpu.VMEM((CH, BLOCK), BF16),
            pltpu.VMEM((CH, BLOCK + LN), BF16),
            pltpu.VMEM((RANKS, SEND1, LN), BF16),
            pltpu.VMEM((CH * CK, LN), F32),
            pltpu.VMEM((CH, MODES), F32),
            pltpu.SemaphoreType.DMA((3,)),
            pltpu.SemaphoreType.DMA((3,)),
        ],
        name="block_states",
    )


def wide_sin_cos(x):
    turns = jnp.floor(x * np.float32(1.0 / (2.0 * np.pi)) + 0.5)
    x = (x - turns * np.float32(6.28125)) - turns * np.float32(2.0 * np.pi - 6.28125)
    s, c = sin_cos(0.5 * x)
    return 2.0 * s * c, 1.0 - 2.0 * s * s


def far_power(decay, turn, blocks):
    size = jnp.exp(-decay * (BLOCK * blocks))
    s, c = wide_sin_cos(turn * (BLOCK * blocks))
    return size * c, size * s


def within_kernel(
    wait_small, x_hbm, terms_ref, wide_ref, out_ref, far_r, far_i, step_r, step_i, x_ref, sems
):
    loads = started(sems, (x_hbm.at[:, pl.ds(0, CK), :], x_ref))
    wait_small()
    terms = terms_ref[0], terms_ref[1], terms_ref[2], terms_ref[3]
    decay, turn = terms[0], terms[1]
    near = [far_power(decay, turn, float(b)) for b in range(4)]
    for a in range(RANKS // 4):
        base = far_power(decay, turn, float(4 * a))
        for b in range(4):
            pr, pi = cmul(base[0], base[1], near[b][0], near[b][1]) if a and b else (
                base if a else near[b]
            )
            far_r[4 * a + b] = pr
            far_i[4 * a + b] = pi
    near = [far_power(decay, turn, b * LN / BLOCK) for b in range(4)]
    for a in range(CK // 4):
        base = far_power(decay, turn, 4 * a * LN / BLOCK)
        for b in range(4):
            step_r[4 * a + b], step_i[4 * a + b] = cmul(*base, *near[b])
    doubles = doublings(decay, turn)
    loads[0].wait()
    for g in range(GROUPS):
        taps = group_taps(terms, rising(decay, turn, doubles, g), g)
        for k in range(LANE_CH):
            c = g * LANE_CH + k
            matrix = toeplitz(taps[k : k + 1])
            high, low = split(matrix)
            x = x_ref[c]
            level = wide_ref[0, c : c + 1, :]
            out_ref[c * CK : (c + 1) * CK, :] = (
                dot2(x, (high, low)) + level * jnp.sum(matrix, 0, keepdims=True)
            )


def within(send, terms, wide):
    return staged(
        within_kernel,
        (),
        (send,),
        (terms, wide),
        out_specs=[VMEM] * 5,
        out_shape=(
            jax.ShapeDtypeStruct((CH * CK, LN), F32),
            jax.ShapeDtypeStruct((RANKS, GROUPS, LN), F32),
            jax.ShapeDtypeStruct((RANKS, GROUPS, LN), F32),
            jax.ShapeDtypeStruct((CK, GROUPS, LN), F32),
            jax.ShapeDtypeStruct((CK, GROUPS, LN), F32),
        ),
        scratch_shapes=[pltpu.VMEM((CH, CK, LN), BF16), pltpu.SemaphoreType.DMA((1,))],
        name="within_chunks",
    )


def mixed_back(group, cot_ref, act_ref):
    mine = lax.broadcasted_iota(jnp.int32, (CH, LN), 1) == group * CH + lax.broadcasted_iota(
        jnp.int32, (CH, LN), 0
    )
    weights = dot(mine.astype(BF16), cot_ref[:, BLOCK:], NT).astype(BF16)
    for i in range(CK):
        act_ref[pl.ds(i, CH, stride=CK), :] = dot(weights, cot_ref[:, i * LN : (i + 1) * LN])


def gelu_both(x):
    scale = np.float32(np.sqrt(2.0 / np.pi))
    square = x * x
    t = jnp.tanh(scale * (x + 0.044715 * (square * x)))
    half = 0.5 * (1.0 + t)
    slope = half + 0.5 * x * (1.0 - t * t) * (scale * (1.0 + (3.0 * 0.044715) * square))
    return x * half, slope


def entering(states, table_r, table_i, distance):
    hr = jnp.zeros((GROUPS, LN), F32)
    hi = jnp.zeros((GROUPS, LN), F32)
    for d in range(RANKS):
        steps = distance(d)
        sr, si = states(d)
        at = jnp.maximum(steps, 0)
        nr, ni = cmul(table_r[at], table_i[at], sr, si)
        hr = jnp.where(steps >= 0, hr + nr, hr)
        hi = jnp.where(steps >= 0, hi + ni, hi)
    return hr, hi


def second_kernel(
    wait_small, me_ref, group_ref, c0h, c1h, c2h, c3h, out_hbm, got_hbm, x_hbm, terms_ref, wide_ref, far_r,
    far_i, step_r, step_i, sr_in, si_in, send_hbm, grad_hbm, mix_ref, sr_ref, si_ref,
    cot_ref, flat_ref, out_ref, got_ref, x_ref, act_ref, activation_ref, send_ref, grad_ref, sems, out_sems,
):
    loads = started(
        sems,
        (got_hbm.at[:, pl.ds(CK, CK), :], got_ref),
        (x_hbm.at[:, pl.ds(0, CK), :], x_ref),
        (out_hbm, out_ref),
        *[(c, cot_ref.at[pl.ds(m * CH, CH), :]) for m, c in enumerate((c0h, c1h, c2h, c3h))],
    )
    wait_small()
    me = me_ref[0]
    terms = terms_ref[0], terms_ref[1], terms_ref[2], terms_ref[3]
    decay, turn = terms[0], terms[1]
    doubles = doublings(decay, turn)
    zr, zi = power(decay, turn, float(LN))
    one_r, one_i = power(decay, turn, 1.0)
    ur, ui = cmul(2.0 * terms[2], 2.0 * terms[3], one_r, one_i)
    loads[0].wait()
    start = entering(lambda d: unpacked_states(got_ref[d]), far_r, far_i, lambda d: me - 1 - d)
    add_entering(sr_ref, si_ref, sr_in, si_in, step_r, step_i, start, range(CK))
    for copy in loads[3:]:
        copy.wait()
    mixed_back(group_ref[0], cot_ref, act_ref)
    for copy in loads[1:3]:
        copy.wait()
    stores = []
    for g in range(GROUPS):
        every = pl.ds(g, CK, stride=GROUPS)
        er, ei = rising(decay, turn, doubles, g)
        wr, wi = cmul(er, ei, ur[g : g + 1], ui[g : g + 1])
        inter = spread_group(sr_ref[every, :], si_ref[every, :], jnp.concatenate([wr, wi], 1))
        left = []
        for k in range(LANE_CH):
            c = g * LANE_CH + k
            rows = slice(c * CK, (c + 1) * CK)
            x = x_ref[c].astype(F32) + wide_ref[0, c : c + 1, :]
            mixed = out_ref[rows, :] + inter[k * CK : (k + 1) * CK] + wide_ref[1, c : c + 1, :] * x
            act, slope = gelu_both(mixed)
            activation_ref[rows, :] = act
            grad = act_ref[rows, :] * slope
            grad_ref[rows, :] = grad
            send_ref[c, :CK, :] = grad.astype(BF16)
            left.append(grad)
        stores.append(
            pltpu.make_async_copy(
                send_ref.at[pl.ds(g * LANE_CH, LANE_CH), pl.ds(0, CK), :],
                send_hbm.at[pl.ds(g * LANE_CH, LANE_CH), pl.ds(0, CK), :],
                out_sems.at[g],
            )
        )
        stores[-1].start()
        products = dot3(split(jnp.concatenate(left, 0)), split(jnp.concatenate([er, ei], 1)))
        pr, pi = gather_group(products)
        sr_ref[every, :] = pr
        si_ref[every, :] = pi
    hr, hi = scan_states(sr_ref, si_ref, zr, zi, range(CK - 1, -1, -1))
    packed = packed_states(hr, hi)
    for d in range(RANKS):
        send_ref[d, CK:, :] = packed
    stores.append(
        pltpu.make_async_copy(
            send_ref.at[:, pl.ds(CK, CK), :], send_hbm.at[:, pl.ds(CK, CK), :],
            out_sems.at[GROUPS],
        )
    )
    stores[-1].start()
    stores.append(pltpu.make_async_copy(grad_ref, grad_hbm, out_sems.at[GROUPS + 1]))
    stores[-1].start()
    for i in range(CK):
        flat_ref[:, i * LN : (i + 1) * LN] = activation_ref[pl.ds(i, CH, stride=CK), :].astype(BF16)
    mix_ref[...] = dot(flat_ref[...], cot_ref[:, :BLOCK], NT)
    for copy in stores:
        copy.wait()


def second(me, group, parts, out, got, send, terms, wide, far, steps, sr, si):
    return staged(
        second_kernel,
        (me, group),
        (*parts, out, got, send),
        (terms, wide, far[0], far[1], steps[0], steps[1], sr, si),
        out_specs=[ANY] * 2 + [VMEM] * 3,
        out_shape=(
            jax.ShapeDtypeStruct((RANKS, SEND2, LN), BF16),
            jax.ShapeDtypeStruct((CH * CK, LN), F32),
            jax.ShapeDtypeStruct((CH, LN), F32),
            jax.ShapeDtypeStruct((CK * GROUPS, LN), F32),
            jax.ShapeDtypeStruct((CK * GROUPS, LN), F32),
        ),
        scratch_shapes=[
            pltpu.VMEM((LN, BLOCK + LN), BF16),
            pltpu.VMEM((CH, BLOCK), BF16),
            pltpu.VMEM((CH * CK, LN), F32),
            pltpu.VMEM((RANKS, CK, LN), BF16),
            pltpu.VMEM((CH, CK, LN), BF16),
            pltpu.VMEM((CH * CK, LN), F32),
            pltpu.VMEM((CH * CK, LN), F32),
            pltpu.VMEM((RANKS, SEND2, LN), BF16),
            pltpu.VMEM((CH * CK, LN), F32),
            pltpu.SemaphoreType.DMA((7,)),
            pltpu.SemaphoreType.DMA((GROUPS + 2,)),
        ],
        name="activation_and_states",
    )


def pull_table(size_ref, damping_ref, frequency_ref, re_ref, im_ref, pull_ref):
    def tiled(values):
        return jnp.concatenate([values] * LANE_CH, 1)

    size = jnp.broadcast_to(as_column(jnp.exp(size_ref[...])), (CH, LN))
    raw = [size] + [tiled(r[...]) for r in (damping_ref, frequency_ref, re_ref, im_ref)]
    (d, th, mr, mi), pull = jax.vjp(mode_terms, *raw)
    zero = jnp.zeros((CH, LN), F32)
    pulled = [
        pull((zero, zero, zero + 2.0, zero)),
        pull((zero, zero, zero, zero - 2.0)),
        pull((-2.0 * mr, -2.0 * mi, zero, zero)),
        pull((2.0 * mi, -2.0 * mr, zero, zero)),
    ]
    inverse = 1.0 / (raw[1] * raw[1] + raw[2] * raw[2])
    qr, qi = cmul(raw[3], raw[4], raw[1] * inverse, raw[2] * inverse)
    one_r, one_i = power(d, th, 1.0)
    er, ei = cmul(qr, qi, one_r, one_i)
    first_lanes = lane_block(zero) == 0
    for k, p in enumerate(pulled):
        pull_ref[k] = by_block(p[1:])
        pull_ref[4 + k] = jnp.where(first_lanes, p[0] * raw[0], 0.0)
    for k, value in enumerate((2.0 * qr, -2.0 * er, 2.0 * ei)):
        pull_ref[8 + k] = jnp.where(first_lanes, value, 0.0)


def signal_kernel(
    wait_small, me_ref, got_hbm, send_hbm, cot_hbm, after_hbm, terms_ref, wide_ref, far_r, far_i,
    step_r, step_i, sr_in, si_in, size_ref, damping_ref, frequency_ref, re_ref, im_ref,
    out_ref, pull_ref, sr_ref, si_ref, rows_ref, got_ref, send_ref, cot_ref, sems,
):
    loads = started(
        sems,
        (got_hbm.at[:, pl.ds(CK, CK), :], got_ref),
        (send_hbm, send_ref),
        (cot_hbm, cot_ref),
    )
    wait_small()
    pull_table(size_ref, damping_ref, frequency_ref, re_ref, im_ref, pull_ref)
    me = me_ref[0]
    terms = terms_ref[0], terms_ref[1], terms_ref[2], terms_ref[3]
    decay, turn = terms[0], terms[1]
    doubles = doublings(decay, turn)
    one_r, one_i = power(decay, turn, 1.0)
    ur, ui = cmul(2.0 * terms[2], 2.0 * terms[3], one_r, one_i)
    loads[0].wait()
    start = entering(lambda d: unpacked_states(got_ref[d]), far_r, far_i, lambda d: d - me - 1)
    add_entering(sr_ref, si_ref, sr_in, si_in, step_r, step_i, start, range(CK - 1, -1, -1))
    for copy in loads[1:]:
        copy.wait()
    for g in range(GROUPS):
        every = pl.ds(g, CK, stride=GROUPS)
        fr, fi = falling(decay, turn, doubles, g)
        wr, wi = cmul(fr, fi, ur[g : g + 1], ui[g : g + 1])
        inter = spread_group(sr_ref[every, :], si_ref[every, :], jnp.concatenate([wr, wi], 1))
        taps = group_taps(terms, rising(decay, turn, doubles, g), g)
        for k in range(LANE_CH):
            c = g * LANE_CH + k
            grad = send_ref[c * CK : (c + 1) * CK, :]
            rows_ref[c * CK : (c + 1) * CK, :] = (
                dot3(split(grad), split(toeplitz(taps[k : k + 1])), NT)
                + inter[k * CK : (k + 1) * CK]
                + wide_ref[1, c : c + 1, :] * grad
            )
    for i in range(CK):
        cols = slice(i * LN, (i + 1) * LN)
        out_ref[:, cols] = (
            cot_ref[:, cols].astype(F32) + rows_ref[pl.ds(i, CH, stride=CK), :]
        ).astype(BF16)


def signal_grad(me, got, send, terms, wide, far, steps, sr, si, raw, cotangent, after):
    return staged(
        signal_kernel,
        (me,),
        (got, send, cotangent, after),
        (terms, wide, far[0], far[1], steps[0], steps[1], sr, si, *raw),
        out_specs=[VMEM] * 2,
        out_shape=(
            jax.ShapeDtypeStruct((CH, BLOCK), BF16),
            jax.ShapeDtypeStruct((11, CH, LN), F32),
        ),
        scratch_shapes=[
            pltpu.VMEM((CK * GROUPS, LN), F32),
            pltpu.VMEM((CK * GROUPS, LN), F32),
            pltpu.VMEM((CH * CK, LN), F32),
            pltpu.VMEM((RANKS, CK, LN), BF16),
            pltpu.VMEM((CH * CK, LN), F32),
            pltpu.VMEM((CH, BLOCK), BF16),
            pltpu.SemaphoreType.DMA((3,)),
        ],
        name="signal_gradient",
        limit=62.5,
    )


def dft_tables():
    full_len = RANKS * BLOCK
    row = np.arange(ROWS)
    time_row = (row % RANKS) * (BLOCK // COLS) + row // RANKS
    first_ids = np.arange(ROWS)
    column = np.arange(COLS)
    angle1 = (
        2.0 * np.pi * (((4 * first_ids[:, None] + 1) * time_row[None, :]) % (4 * ROWS)) / (4 * ROWS)
    )
    angle_t = 2.0 * np.pi * ((4 * first_ids[:, None] + 1) * column[None, :]) / (4 * full_len)
    lane = np.arange(LN)
    angle2 = 2.0 * np.pi * ((lane[:, None] * lane[None, :]) % LN) / LN
    angle_p = 2.0 * np.pi * np.arange(PER)[:, None] * lane[None, :] / COLS

    def halves(values):
        values = values.astype(np.float32)
        high = values.astype(BF16)
        return high, (values - high.astype(np.float32)).astype(BF16)

    stage1 = np.concatenate([np.cos(angle1), -np.sin(angle1)], 0)
    cos2, sin2 = np.cos(angle2), np.sin(angle2)
    stage2 = np.concatenate(
        [np.concatenate([cos2, -sin2], 1), np.concatenate([sin2, cos2], 1)], 0
    )
    twiddle = np.stack([np.cos(angle_t), np.sin(angle_t)]).astype(np.float32)
    steps = np.concatenate([np.cos(angle_p), np.sin(angle_p)], 0).astype(np.float32)
    return halves(stage1), halves(stage1.T / full_len), halves(stage2), twiddle, steps


def gather_rows(ref, stride, base):
    return jnp.concatenate(
        [
            jnp.concatenate(
                [
                    ref[pl.ds(base + piece * PER + q, RANKS, stride=stride), :]
                    for q in range(PER)
                ],
                1,
            )
            for piece in range(BLOCK // COLS)
        ],
        0,
    )


def butterfly(parts, sign):
    (r0, i0), (r1, i1), (r2, i2), (r3, i3) = parts
    sr, si, dr, di = r0 + r2, i0 + i2, r0 - r2, i0 - i2
    tr, ti, er, ei = r1 + r3, i1 + i3, r1 - r3, i1 - i3
    if sign > 0:
        er, ei = -er, -ei
    return (sr + tr, si + ti), (dr + ei, di - er), (sr - tr, si - ti), (dr - ei, di + er)


def forward_dft(rows, exact, d1h, d1l, d2h, d2l, twiddle, steps, wait1, wait2):
    xh, xl = split(rows)
    wait1()
    if exact:
        a = dot(jnp.concatenate([d1h[...], d1l[...]], 1), jnp.concatenate([xh, xh], 0))
    else:
        a = dot3((d1h[...], d1l[...]), (xh, xl))
    wait2()
    parts = []
    for q in range(PER):
        cols = slice(q * LN, (q + 1) * LN)
        parts.append(cmul(a[:ROWS, cols], a[ROWS:, cols], twiddle[0, :, cols], -twiddle[1, :, cols]))
    out = []
    for p, (ur, ui) in enumerate(butterfly(parts, -1)):
        if p:
            ur, ui = cmul(ur, ui, steps[p : p + 1, :], -steps[PER + p : PER + p + 1, :])
        out.append(jnp.concatenate([ur, ui], 1))
    return dot3(split(jnp.concatenate(out, 0)), (d2h[...], d2l[...]))


def inverse_dft(spec, d1th, d1tl, d2h, d2l, twiddle, steps):
    v = dot3(split(spec), (d2h[...], d2l[...]), NT)
    parts = []
    for p in range(PER):
        vr, vi = v[p * ROWS : (p + 1) * ROWS, :LN], v[p * ROWS : (p + 1) * ROWS, LN:]
        if p:
            vr, vi = cmul(vr, vi, steps[p : p + 1, :], steps[PER + p : PER + p + 1, :])
        parts.append((vr, vi))
    real, imag = [], []
    for q, (br, bi) in enumerate(butterfly(parts, 1)):
        cols = slice(q * LN, (q + 1) * LN)
        br, bi = cmul(br, bi, twiddle[0, :, cols], twiddle[1, :, cols])
        real.append(br)
        imag.append(bi)
    bh, bl = split(
        jnp.concatenate([jnp.concatenate(real, 1), jnp.concatenate(imag, 1)], 0)
    )
    return dot3((d1th[...], d1tl[...]), (bh, bl))


def lane_block(row):
    return lax.broadcasted_iota(jnp.int32, row.shape, 1) // MODES


def repeated(row):
    row = jnp.where(lane_block(row) == 0, row, 0.0)
    total = row
    for m in range(1, LANE_CH):
        total = total + pltpu.roll(row, m * MODES, 1)
    return total


def by_block(rows):
    result = rows[0]
    for m in range(1, LANE_CH):
        result = jnp.where(lane_block(result) == m, rows[m], result)
    return result


def spectrum_kernel(
    wait_small, me_ref, got_hbm, d1h_hbm, d1l_hbm, twiddle_hbm, d2h_hbm, d2l_hbm, after_hbm,
    steps_ref, wide_ref, terms_ref, spec_ref, column_ref, turn_ref,
    got_ref, d1h, d1l, twiddle, d2h, d2l, rows_ref, sems,
):
    loads = started(
        sems,
        (got_hbm.at[:, pl.ds(0, CK), :], got_ref),
        (d1h_hbm, d1h), (d1l_hbm, d1l), (twiddle_hbm, twiddle), (d2h_hbm, d2h), (d2l_hbm, d2l),
    )
    wait_small()
    me = me_ref[0]
    embed = wide_ref[0, pl.ds(me, 1), :]
    loads[0].wait()
    for d in range(RANKS):
        rows_ref[d * CK : (d + 1) * CK, :] = got_ref[d].astype(F32) + embed
    rows = gather_rows(rows_ref, CK, 0)
    spec_ref[...] = forward_dft(
        rows, False, d1h, d1l, d2h, d2l, twiddle, steps_ref, waiting(loads[1:3]),
        waiting(loads[3:6]),
    )

    at, shift = me // LANE_CH, (me % LANE_CH) * MODES

    def own(k):
        row = jnp.broadcast_to(terms_ref[k, pl.ds(at, 1), :], (8, LN))
        return repeated(pltpu.roll(row, (LN - shift) % LN, 1)[:1])

    d, th = own(0), own(1)
    steps = lax.broadcasted_iota(jnp.int32, (8, LN), 0).astype(F32)
    cr, ci = power(d, th, steps)
    for k in (8, 16, 32, 64, 128, 256):
        zr, zi = far_power(d, th, float(k) / BLOCK)
        nr, ni = cmul(cr, ci, zr, zi)
        cr, ci = jnp.concatenate([cr, nr], 0), jnp.concatenate([ci, ni], 0)
    col = lax.broadcasted_iota(jnp.int32, (COLS, LN), 0).astype(F32)
    block = lane_block(col)
    table = jnp.where(block % 2 == 0, cr, ci)
    column_ref[...] = jnp.where(block < 2, table, table * col)
    ranks = lax.broadcasted_iota(jnp.int32, (RANKS, LN), 0).astype(F32)
    br, bi = far_power(d, th, ranks)
    for piece in range(BLOCK // COLS):
        zr, zi = far_power(d, th, float(piece * COLS) / BLOCK)
        nr, ni = cmul(br, bi, zr, zi) if piece else (br, bi)
        turn_ref[0, piece * RANKS : (piece + 1) * RANKS, :] = nr
        turn_ref[1, piece * RANKS : (piece + 1) * RANKS, :] = ni


def spectrum(me, got, after, wide, terms, tables):
    (d1h, d1l), unused, (d2h, d2l), twiddle, steps = tables
    return staged(
        spectrum_kernel,
        (me,),
        (got, d1h, d1l, twiddle, d2h, d2l, after),
        (steps, wide, terms),
        out_specs=[VMEM] * 3,
        out_shape=(
            jax.ShapeDtypeStruct((PER * ROWS, 2 * LN), F32),
            jax.ShapeDtypeStruct((COLS, LN), F32),
            jax.ShapeDtypeStruct((2, ROWS, LN), F32),
        ),
        scratch_shapes=[
            pltpu.VMEM((RANKS, CK, LN), BF16),
            pltpu.VMEM((2 * ROWS, ROWS), BF16),
            pltpu.VMEM((2 * ROWS, ROWS), BF16),
            pltpu.VMEM((2, ROWS, COLS), F32),
            pltpu.VMEM((2 * LN, 2 * LN), BF16),
            pltpu.VMEM((2 * LN, 2 * LN), BF16),
            pltpu.VMEM((RANKS * CK, LN), F32),
            pltpu.SemaphoreType.DMA((6,)),
        ],
        name="input_spectrum",
    )


def correlate_kernel(
    wait_small, got_hbm, d1h_hbm, d1l_hbm, twiddle_hbm, d2h_hbm, d2l_hbm, spec_hbm, d1th_hbm, d1tl_hbm,
    column_hbm, turn_hbm, steps_ref, m0, m1, m2, m3, send_hbm, after_ref,
    got_ref, d1h, d1l, twiddle, d2h, d2l, spec_ref, d1th, d1tl, column_ref, turn_ref,
    rows_ref, send_ref, sems, out_sems,
):
    loads = started(
        sems,
        (got_hbm.at[:, pl.ds(0, CK), :], got_ref),
        (d1h_hbm, d1h), (d1l_hbm, d1l), (twiddle_hbm, twiddle), (d2h_hbm, d2h), (d2l_hbm, d2l),
        (spec_hbm, spec_ref), (d1th_hbm, d1th), (d1tl_hbm, d1tl), (column_hbm, column_ref),
        (turn_hbm, turn_ref),
    )
    wait_small()
    mixes = by_block([m[...] for m in (m0, m1, m2, m3)]).astype(BF16)
    for d in range(RANKS):
        send_ref[d, CK : 2 * CK, :] = mixes
    middle = pl.ds(CK, CK)
    stores = started(out_sems, (send_ref.at[:, middle, :], send_hbm.at[:, middle, :]))
    loads[0].wait()
    for d in range(RANKS):
        rows_ref[d * CK : (d + 1) * CK, :] = got_ref[d].astype(F32)
    g_rows = gather_rows(rows_ref, CK, 0)
    g_spec = forward_dft(
        g_rows, True, d1h, d1l, d2h, d2l, twiddle, steps_ref, waiting(loads[1:3]),
        waiting(loads[3:6]),
    )
    waiting(loads[6:7])()
    gr, gi = g_spec[:, :LN], g_spec[:, LN:]
    xr, xi = spec_ref[:, :LN], spec_ref[:, LN:]
    both = jnp.concatenate([xr * gr + xi * gi, xr * gi - xi * gr], 1)
    waiting(loads[7:])()
    kernel_rows = inverse_dft(both, d1th, d1tl, d2h, d2l, twiddle, steps_ref)
    for piece in range(BLOCK // COLS):
        for q in range(PER):
            rows_ref[pl.ds(piece * PER + q, RANKS, stride=CK), :] = kernel_rows[
                piece * RANKS : (piece + 1) * RANKS, q * LN : (q + 1) * LN
            ]
    for d in range(RANKS):
        send_ref[d, :CK, :] = rows_ref[d * CK : (d + 1) * CK, :].astype(BF16)
    stores.append(
        pltpu.make_async_copy(
            send_ref.at[:, pl.ds(0, CK), :], send_hbm.at[:, pl.ds(0, CK), :], out_sems.at[1]
        )
    )
    stores[-1].start()
    column = split(column_ref[...])
    inner = dot3(split(kernel_rows), column)
    g_inner = dot2(g_rows.astype(BF16), column)
    rr, ri = turn_ref[0], turn_ref[1]
    ids = lax.broadcasted_iota(jnp.int32, (ROWS, LN), 0)
    starts = ((ids % RANKS) * BLOCK + (ids // RANKS) * COLS).astype(F32)

    def total(values):
        return jnp.sum(values, 0, keepdims=True)

    by_r, by_i = rr * inner, ri * inner
    u, v = total(by_r), total(by_i)
    su, sv = total(starts * by_r), total(starts * by_i)
    gu, gv = total(rr * g_inner), total(ri * g_inner)

    lanes = lax.broadcasted_iota(jnp.int32, (1, LN), 1)
    scalars = jnp.where(lanes == 0, kernel_rows[0:1, 0:1], 0.0) + jnp.where(
        lanes == 1, jnp.sum(total(g_rows), 1, keepdims=True), 0.0
    )
    small = jnp.concatenate([u, v, su, sv, gu, gv, scalars, jnp.zeros((1, LN), F32)], 0)
    after_ref[...] = small
    high, low = split(jnp.concatenate([small, small], 0))
    upper = lax.broadcasted_iota(jnp.int32, (16, LN), 0) < 8
    packed = jnp.where(upper, high.astype(F32), low.astype(F32)).astype(BF16)
    for d in range(RANKS):
        send_ref[d, 2 * CK :, :] = packed
    stores.append(
        pltpu.make_async_copy(
            send_ref.at[:, pl.ds(2 * CK, 16), :], send_hbm.at[:, pl.ds(2 * CK, 16), :],
            out_sems.at[2],
        )
    )
    stores[-1].start()
    for copy in stores:
        copy.wait()


def correlate(got, spec, tables, column, turns, mixes):
    (d1h, d1l), (d1th, d1tl), (d2h, d2l), twiddle, steps = tables
    return staged(
        correlate_kernel,
        (),
        (got, d1h, d1l, twiddle, d2h, d2l, spec, d1th, d1tl, column, turns),
        (steps, *mixes),
        out_specs=[ANY, VMEM],
        out_shape=(
            jax.ShapeDtypeStruct((RANKS, SEND3, LN), BF16),
            jax.ShapeDtypeStruct((8, LN), F32),
        ),
        scratch_shapes=[
            pltpu.VMEM((RANKS, CK, LN), BF16),
            pltpu.VMEM((2 * ROWS, ROWS), BF16),
            pltpu.VMEM((2 * ROWS, ROWS), BF16),
            pltpu.VMEM((2, ROWS, COLS), F32),
            pltpu.VMEM((2 * LN, 2 * LN), BF16),
            pltpu.VMEM((2 * LN, 2 * LN), BF16),
            pltpu.VMEM((PER * ROWS, 2 * LN), F32),
            pltpu.VMEM((ROWS, 2 * ROWS), BF16),
            pltpu.VMEM((ROWS, 2 * ROWS), BF16),
            pltpu.VMEM((COLS, LN), F32),
            pltpu.VMEM((2, ROWS, LN), F32),
            pltpu.VMEM((RANKS * CK, LN), F32),
            pltpu.VMEM((RANKS, SEND3, LN), BF16),
            pltpu.SemaphoreType.DMA((11,)),
            pltpu.SemaphoreType.DMA((3,)),
        ],
        name="correlation",
    )


def outputs_kernel(
    wait_small, step_ref, group_ref, got_ref, pull_ref, wide_ref, kernel_ref, damping_ref, frequency_ref, re_ref, im_ref,
    size_ref, skip_ref, mix_ref, table_ref, rows_ref, turned_ref,
):
    mixes = jnp.zeros((CH, LN), F32)
    for c in range(CH):
        rows_ref[c * CK : (c + 1) * CK, :] = got_ref[c, :CK, :].astype(F32)
        mixes = mixes + got_ref[c, CK : 2 * CK, :].astype(F32)
    for i in range(CK):
        kernel_ref[:, i * LN : (i + 1) * LN] = rows_ref[pl.ds(i, CH, stride=CK), :]
    for c in range(CH):
        small = got_ref[c, 2 * CK :, :].astype(F32)
        rows_ref[c * 8 : (c + 1) * 8, :] = small[:8] + small[8:]
    wait_small()
    u, v, su, sv, gu, gv, scalars = (rows_ref[pl.ds(k, CH, stride=8), :] for k in range(7))

    def block(row, k):
        moved = pltpu.roll(row, (LN - k * MODES) % LN, 1) if k else row
        return jnp.where(lane_block(row) == 0, moved, 0.0)

    sums = (
        block(u, 0) - block(v, 1),
        block(u, 1) + block(v, 0),
        block(u, 2) - block(v, 3) + block(su, 0) - block(sv, 1),
        block(u, 3) + block(v, 2) + block(su, 1) + block(sv, 0),
    )
    grads = jnp.zeros((CH, LN), F32)
    size = jnp.zeros((CH, LN), F32)
    for k, value in enumerate(sums):
        grads = grads + pull_ref[k] * repeated(value)
        size = size + pull_ref[4 + k] * value
    for k, ref in enumerate((damping_ref, frequency_ref, re_ref, im_ref)):
        ref[...] = grads[:, k * MODES : (k + 1) * MODES]
    g_sum = scalars[:, 1:2]
    back = (
        pull_ref[8] * g_sum
        + pull_ref[9] * (block(gu, 0) - block(gv, 1))
        + pull_ref[10] * (block(gu, 1) + block(gv, 0))
    )
    back_sum = jnp.sum(back, 1, keepdims=True) + wide_ref[1][:, :1] * g_sum
    lanes = lax.broadcasted_iota(jnp.int32, (CH, LN), 1)
    scalars = jnp.where(lanes == 0, jnp.sum(size, 1, keepdims=True), scalars[:, 0:1])
    turned = jnp.concatenate([scalars, jnp.zeros((LN - CH, LN), F32)], 0).T
    size_ref[...] = turned[0:1, :CH]
    skip_ref[...] = turned[1:2, :CH]
    picked = lax.broadcasted_iota(jnp.int32, table_ref.shape, 1) == step_ref[0]
    table_ref[...] = jnp.where(picked, back_sum, 0.0)
    turned_ref[...] = jnp.concatenate([mixes, jnp.zeros((LN - CH, LN), F32)], 0).T
    mix_ref[...] = jnp.concatenate(
        [
            turned_ref[pl.ds(pl.multiple_of((group_ref[0] ^ c) * CH, CH), CH), :][:, :CH]
            for c in range(LN // CH)
        ],
        1,
    )


def outputs(step, group, got, pull, levels, table_len):
    wide = jax.ShapeDtypeStruct((CH, MODES), F32)
    row = jax.ShapeDtypeStruct((1, CH), F32)
    return staged(
        outputs_kernel,
        (step, group),
        (got,),
        (pull, levels),
        out_specs=[VMEM] * 9,
        out_shape=(
            jax.ShapeDtypeStruct((CH, BLOCK), F32),
            wide, wide, wide, wide, row, row,
            jax.ShapeDtypeStruct((CH, LN), F32),
            jax.ShapeDtypeStruct((CH, table_len), F32),
        ),
        scratch_shapes=[pltpu.VMEM((CH * CK, LN), F32), pltpu.VMEM((LN, LN), F32)],
        name="outputs",
        plain_spec=VMEM,
        limit=8,
    )


def exchange(values):
    return lax.all_to_all(values, "tm", split_axis=0, concat_axis=0, tiled=True)


def shards(
    signal,
    cotangent,
    log_step,
    damping,
    frequency,
    coef_re,
    coef_im,
    skip_gain,
    mix_weight,
    embed_table,
    diffusion_step,
):
    me = lax.axis_index("tm").reshape(1)
    group = lax.axis_index("chan").reshape(1)
    tables = dft_tables()

    def swap(values, mask):
        return lax.ppermute(values, "chan", [(i, i ^ mask) for i in range(4)])

    send1, own, sr, si, terms, wide = first(
        diffusion_step, signal, cotangent, mix_weight, log_step[None], (damping, frequency, coef_re, coef_im),
        skip_gain[None], embed_table.T,
    )
    got1 = exchange(send1)
    own, across = lax.optimization_barrier((own, swap(own, 2)))
    parts = (own, swap(own, 1), across, swap(across, 1))
    out, far_r, far_i, step_r, step_i = within(send1, terms, wide)
    far = (far_r, far_i)
    steps = (step_r, step_i)
    send2, grad, mix, br, bi = second(
        me, group, parts, out, got1, send1, terms, wide, far, steps, sr, si
    )
    got2 = exchange(send2)
    mixes = [mix] + [swap(mix, m) for m in range(1, 4)]
    spec, column, turns = spectrum(me, got1, mix, wide, terms, tables)
    send3, after = correlate(got2, spec, tables, column, turns, mixes)
    got3 = exchange(send3)
    grad_signal, pull = signal_grad(
        me, got2, grad, terms, wide, far, steps, br, bi,
        (log_step[None], damping, frequency, coef_re, coef_im), cotangent, after,
    )
    kernel, g_damping, g_frequency, g_re, g_im, g_size, g_skip, g_mix, g_table = outputs(
        diffusion_step, group, got3, pull, wide, embed_table.shape[0]
    )
    return (
        grad_signal,
        kernel,
        g_size[0],
        g_damping,
        g_frequency,
        g_re,
        g_im,
        g_skip[0],
        g_mix,
        g_table.T,
    )


def solution(mesh):
    placed = (
        P("chan", "tm"),
        P("chan", "tm"),
        P("chan"),
        P("chan", None),
        P("chan", None),
        P("chan", None),
        P("chan", None),
        P("chan"),
        P("chan", None),
        P(None, "chan"),
        P(),
    )
    return jax.shard_map(
        shards,
        mesh=mesh,
        in_specs=placed,
        out_specs=(
            P("chan", "tm"),
            P("chan", "tm"),
            P("chan"),
            P("chan", None),
            P("chan", None),
            P("chan", None),
            P("chan", None),
            P("chan"),
            P("chan", None),
            P(None, "chan"),
        ),
        check_vma=False,
    )
```

```python
import functools

import jax
import jax.numpy as jnp
import numpy as np
from jax import lax
from jax.experimental import pallas as pl
from jax.experimental.pallas import tpu as pltpu
from jax.sharding import PartitionSpec as P

HIGHEST = lax.Precision.HIGHEST
F32 = jnp.float32
BF16 = jnp.bfloat16

CH = 32
MODES = 32
BLOCK = 4096
LN = 128
CK = BLOCK // LN
LANE_CH = LN // MODES
GROUPS = CH // LANE_CH
RANKS = 32
COLS = 512
PER = COLS // LN
ROWS = RANKS * BLOCK // COLS
SEND1 = 64
SEND2 = 64
SEND3 = 80
NT = (((1,), (1,)), ((), ()))
NN = (((1,), (0,)), ((), ()))
GRANT = 63.75
SMEM = pl.BlockSpec(memory_space=pltpu.SMEM)
VMEM = pl.BlockSpec(memory_space=pltpu.VMEM)
ANY = pl.BlockSpec(memory_space=pl.ANY)
HBM = pl.BlockSpec(memory_space=pltpu.HBM)


def expm1_small(x):
    r = 1.0
    for k in (7.0, 6.0, 5.0, 4.0, 3.0, 2.0):
        r = 1.0 + x * r * (1.0 / k)
    return x * r


def mode_terms(step_size, damping, frequency, coef_re, coef_im):
    decay_rate = step_size * damping
    turn_rate = step_size * frequency
    half_sine = jnp.sin(0.5 * turn_rate)
    grow_real = expm1_small(-decay_rate) * jnp.cos(turn_rate) - 2.0 * half_sine * half_sine
    grow_imag = jnp.exp(-decay_rate) * jnp.sin(turn_rate)
    inverse = 1.0 / (damping * damping + frequency * frequency)
    hold_real = (frequency * grow_imag - damping * grow_real) * inverse
    hold_imag = -(frequency * grow_real + damping * grow_imag) * inverse
    weight_real = coef_re * hold_real - coef_im * hold_imag
    weight_imag = coef_re * hold_imag + coef_im * hold_real
    return (decay_rate, turn_rate, weight_real, weight_imag)


def cmul(ar, ai, br, bi):
    return ar * br - ai * bi, ar * bi + ai * br


def split(values):
    high = values.astype(BF16)
    return high, (values - high.astype(F32)).astype(BF16)


def dot(left, right, dims=NN):
    return lax.dot_general(left, right, dims, preferred_element_type=F32)


def dot3(left, right, dims=NN):
    (lh, ll), (rh, rl) = left, right
    (axis,), (other,) = dims[0]
    return dot(
        jnp.concatenate([lh, ll, lh], axis), jnp.concatenate([rh, rh, rl], other), dims
    )


def dot2(left, right, dims=NN):
    (axis,), (other,) = dims[0]
    return dot(jnp.concatenate([left, left], axis), jnp.concatenate(right, other), dims)


def started(sems, *pairs):
    copies = [pltpu.make_async_copy(a, b, sems.at[k]) for k, (a, b) in enumerate(pairs)]
    for copy in copies:
        copy.start()
    return copies


def waiting(copies):
    def wait(first=0, last=None):
        for copy in copies[first:last]:
            copy.wait()

    return wait


def staged(
    kernel, scalars, plain, small, *, out_specs, out_shape, scratch_shapes, name,
    plain_spec=HBM, limit=GRANT, eager=None, early=(),
):
    heads, outs = len(scalars) + len(plain), len(out_shape)

    def body(*refs):
        given, rest = refs[:heads], refs[heads:]
        sources, rest = rest[: len(small)], rest[len(small) :]
        results, rest = list(rest[:outs]), rest[outs:]
        held, sems, rest = rest[: len(small)], rest[len(small)], rest[len(small) + 1 :]
        written, out_sems, rest = rest[: len(early)], rest[len(early)], rest[len(early) + 1 :]
        copies = [
            pltpu.make_async_copy(a, b, sems.at[k]) for k, (a, b) in enumerate(zip(sources, held))
        ]
        leaving = {
            k: pltpu.make_async_copy(written[n], results[k], out_sems.at[n])
            for n, k in enumerate(early)
        }
        for n, k in enumerate(early):
            results[k] = written[n]
        gone = set()

        def start(first=0, last=None):
            for copy in copies[first:last]:
                copy.start()

        def store(*which):
            for k in which:
                leaving[k].start()
                gone.add(k)

        wait = waiting(copies)
        wait.start, wait.store = start, store
        start(0, eager)
        kernel(wait, *given, *held, *results, *rest)
        store(*[k for k in early if k not in gone])
        for copy in leaving.values():
            copy.wait()

    return pl.pallas_call(
        body,
        in_specs=[SMEM] * len(scalars) + [plain_spec] * len(plain) + [HBM] * len(small),
        out_specs=[HBM if k in early else spec for k, spec in enumerate(out_specs)],
        out_shape=out_shape,
        scratch_shapes=[pltpu.VMEM(a.shape, a.dtype) for a in small]
        + [pltpu.SemaphoreType.DMA((len(small),))]
        + [pltpu.VMEM(out_shape[k].shape, out_shape[k].dtype) for k in early]
        + [pltpu.SemaphoreType.DMA((max(len(early), 1),))]
        + scratch_shapes,
        compiler_params=pltpu.CompilerParams(vmem_limit_bytes=int(limit * 1024 * 1024)),
        name=name,
    )(*scalars, *plain, *small)


def sin_cos(x):
    y = x * x
    s = 1.0
    for k in (210.0, 156.0, 110.0, 72.0, 42.0, 20.0, 6.0):
        s = 1.0 - y * s * (1.0 / k)
    c = 1.0
    for k in (240.0, 182.0, 132.0, 90.0, 56.0, 30.0, 12.0, 2.0):
        c = 1.0 - y * c * (1.0 / k)
    return x * s, c


def power(decay, turn, steps):
    size = jnp.exp(-decay * steps)
    s, c = sin_cos(turn * steps)
    return size * c, size * s


def doublings(decay, turn):
    return [power(decay, turn, float(k)) for k in (8, 16, 32, 64)]


def rising(decay, turn, doubles, g):
    rows = lax.broadcasted_iota(jnp.int32, (8, LN), 0).astype(F32)
    tr, ti = power(decay[g : g + 1], turn[g : g + 1], rows)
    for zr, zi in doubles:
        nr, ni = cmul(tr, ti, zr[g : g + 1], zi[g : g + 1])
        tr, ti = jnp.concatenate([tr, nr], 0), jnp.concatenate([ti, ni], 0)
    return tr, ti


def falling(decay, turn, doubles, g):
    rows = 7.0 - lax.broadcasted_iota(jnp.int32, (8, LN), 0).astype(F32)
    tr, ti = power(decay[g : g + 1], turn[g : g + 1], rows)
    for zr, zi in doubles:
        nr, ni = cmul(tr, ti, zr[g : g + 1], zi[g : g + 1])
        tr, ti = jnp.concatenate([nr, tr], 0), jnp.concatenate([ni, ti], 0)
    return tr, ti


def lane_channel(shape):
    return lax.broadcasted_iota(jnp.int32, shape, 1) // MODES


def gather_group(products):
    owner = lane_channel((CK, LN))
    real, imag = products[:, :LN], products[:, LN:]
    out_r, out_i = real[:CK], imag[:CK]
    for k in range(1, LANE_CH):
        mine = owner == k
        out_r = jnp.where(mine, real[k * CK : (k + 1) * CK], out_r)
        out_i = jnp.where(mine, imag[k * CK : (k + 1) * CK], out_i)
    return out_r, out_i


def spread_group(state_r, state_i, table):
    owner = lane_channel((CK, LN))
    zero = jnp.zeros((CK, LN), F32)
    left = jnp.concatenate(
        [
            jnp.concatenate(
                [jnp.where(owner == k, state_r, zero), jnp.where(owner == k, -state_i, zero)], 1
            )
            for k in range(LANE_CH)
        ],
        0,
    )
    return dot3(split(left), table, NT)


def scan_states(sr_ref, si_ref, power_r, power_i, order):
    hr = jnp.zeros((GROUPS, LN), F32)
    hi = jnp.zeros((GROUPS, LN), F32)
    for i in order:
        rows = pl.ds(i * GROUPS, GROUPS)
        own_r, own_i = sr_ref[rows, :], si_ref[rows, :]
        sr_ref[rows, :] = hr
        si_ref[rows, :] = hi
        nr, ni = cmul(power_r, power_i, hr, hi)
        hr, hi = nr + own_r, ni + own_i
    return hr, hi


def add_entering(sr_ref, si_ref, sr_in, si_in, step_r, step_i, start, order):
    for k, i in enumerate(order):
        rows = pl.ds(i * GROUPS, GROUPS)
        nr, ni = cmul(step_r[k], step_i[k], *start) if k else start
        sr_ref[rows, :] = sr_in[rows, :] + nr
        si_ref[rows, :] = si_in[rows, :] + ni


def toeplitz(taps_row):
    rows = jnp.broadcast_to(taps_row, (LN, LN))
    turned = pltpu.roll(rows, 0, 1, stride=1, stride_axis=0)
    lag = lax.broadcasted_iota(jnp.int32, (LN, LN), 1) - lax.broadcasted_iota(
        jnp.int32, (LN, LN), 0
    )
    return jnp.where(lag >= 0, turned, 0.0)


def group_taps(terms, table, g):
    real = 2.0 * (terms[2][g : g + 1] * table[0] - terms[3][g : g + 1] * table[1])
    owner = (
        lane_channel((8, LN)) == lax.broadcasted_iota(jnp.int32, (8, LN), 0)
    ).astype(BF16)
    high, low = split(real)
    return dot2(owner, (high, low), NT)


def packed_lanes(ref):
    return jnp.concatenate([ref[pl.ds(k, GROUPS, stride=LANE_CH), :] for k in range(LANE_CH)], 1)


def as_column(row):
    shape = (CH, CH)
    same = lax.broadcasted_iota(jnp.int32, shape, 0) == lax.broadcasted_iota(jnp.int32, shape, 1)
    return jnp.sum(jnp.where(same, row, 0.0), 1, keepdims=True)


def first_kernel(
    wait_small, step_ref, signal_hbm, cot_hbm, mix_hbm, size_ref, damping_ref, frequency_ref, re_ref, im_ref,
    skip_ref, table_ref, send_hbm, own_hbm, sr_ref, si_ref, terms_ref, wide_ref,
    signal_ref, own_ref, send_ref, rows_ref, pack_ref, sems, out_sems,
):
    loads = started(
        sems,
        (signal_hbm, signal_ref),
        (cot_hbm, own_ref.at[:, pl.ds(0, BLOCK)]),
        (mix_hbm, own_ref.at[:, pl.ds(BLOCK, LN)]),
    )
    wait_small()
    picked = lax.broadcasted_iota(jnp.int32, table_ref.shape, 1) == step_ref[0]
    embed = jnp.sum(jnp.where(picked, table_ref[...], 0.0), 1, keepdims=True)
    wide_ref[0] = jnp.broadcast_to(embed, (CH, LN))
    wide_ref[1] = jnp.broadcast_to(as_column(skip_ref[...]), (CH, LN))
    pack_ref[...] = jnp.broadcast_to(embed, (CH, MODES))
    embed_lanes = packed_lanes(pack_ref)
    pack_ref[...] = jnp.broadcast_to(as_column(jnp.exp(size_ref[...])), (CH, MODES))
    raw = [packed_lanes(r) for r in (pack_ref, damping_ref, frequency_ref, re_ref, im_ref)]
    terms = mode_terms(*raw)
    for k in range(4):
        terms_ref[k] = terms[k]
    wait_small.store(4, 5)
    decay, turn = terms[0], terms[1]
    doubles = doublings(decay, turn)
    loads[0].wait()
    for i in range(CK):
        rows_ref[pl.ds(i, CH, stride=CK), :] = signal_ref[:, i * LN : (i + 1) * LN].astype(F32)
    for c in range(CH):
        send_ref[c, :CK, :] = rows_ref[c * CK : (c + 1) * CK, :].astype(BF16)
    loads[1].wait()
    loads[2].wait()
    stores = started(
        out_sems,
        (send_ref.at[:, pl.ds(0, CK), :], send_hbm.at[:, pl.ds(0, CK), :]),
        (own_ref, own_hbm),
    )
    for g in range(GROUPS):
        x = rows_ref[g * LN : (g + 1) * LN, :].astype(BF16)
        fr, fi = falling(decay, turn, doubles, g)
        table = jnp.concatenate([fr, fi], 1)
        th, tl = split(table)
        pr, pi = gather_group(dot2(x, (th, tl)))
        level = embed_lanes[g : g + 1]
        sr_ref[pl.ds(g, CK, stride=GROUPS), :] = pr + level * jnp.sum(fr, 0, keepdims=True)
        si_ref[pl.ds(g, CK, stride=GROUPS), :] = pi + level * jnp.sum(fi, 0, keepdims=True)
    zr, zi = power(decay, turn, float(LN))
    hr, hi = scan_states(sr_ref, si_ref, zr, zi, range(CK))
    wait_small.store(2, 3)
    packed = packed_states(hr, hi)
    for d in range(RANKS):
        send_ref[d, CK:, :] = packed
    last = pltpu.make_async_copy(
        send_ref.at[:, pl.ds(CK, CK), :], send_hbm.at[:, pl.ds(CK, CK), :], out_sems.at[2]
    )
    last.start()
    for copy in stores + [last]:
        copy.wait()


def packed_states(hr, hi):
    high, low = split(jnp.concatenate([hr, hi], 0))
    return jnp.concatenate([high, low], 0)


def unpacked_states(packed):
    packed = packed.astype(F32)
    values = packed[: 2 * GROUPS] + packed[2 * GROUPS :]
    return values[:GROUPS], values[GROUPS:]


def first(step, signal, cotangent, mix_weight, sizes, params, skip, table):
    return staged(
        first_kernel,
        (step,),
        (signal, cotangent, mix_weight),
        (sizes, *params, skip, table),
        out_specs=[ANY] * 2 + [VMEM] * 4,
        out_shape=(
            jax.ShapeDtypeStruct((RANKS, SEND1, LN), BF16),
            jax.ShapeDtypeStruct((CH, BLOCK + LN), BF16),
            jax.ShapeDtypeStruct((CK * GROUPS, LN), F32),
            jax.ShapeDtypeStruct((CK * GROUPS, LN), F32),
            jax.ShapeDtypeStruct((4, GROUPS, LN), F32),
            jax.ShapeDtypeStruct((2, CH, LN), F32),
        ),
        scratch_shapes=[
            pltpu.VMEM((CH, BLOCK), BF16),
            pltpu.VMEM((CH, BLOCK + LN), BF16),
            pltpu.VMEM((RANKS, SEND1, LN), BF16),
            pltpu.VMEM((CH * CK, LN), F32),
            pltpu.VMEM((CH, MODES), F32),
            pltpu.SemaphoreType.DMA((3,)),
            pltpu.SemaphoreType.DMA((3,)),
        ],
        name="block_states",
        early=(2, 3, 4, 5),
    )


def wide_sin_cos(x):
    turns = jnp.floor(x * np.float32(1.0 / (2.0 * np.pi)) + 0.5)
    x = (x - turns * np.float32(6.28125)) - turns * np.float32(2.0 * np.pi - 6.28125)
    s, c = sin_cos(0.5 * x)
    return 2.0 * s * c, 1.0 - 2.0 * s * s


def far_power(decay, turn, blocks):
    size = jnp.exp(-decay * (BLOCK * blocks))
    s, c = wide_sin_cos(turn * (BLOCK * blocks))
    return size * c, size * s


def pull_table(size_ref, damping_ref, frequency_ref, re_ref, im_ref, pull_ref):
    def tiled(values):
        return jnp.concatenate([values] * LANE_CH, 1)

    size = jnp.broadcast_to(as_column(jnp.exp(size_ref[...])), (CH, LN))
    raw = [size] + [tiled(r[...]) for r in (damping_ref, frequency_ref, re_ref, im_ref)]
    (d, th, mr, mi), pull = jax.vjp(mode_terms, *raw)
    zero = jnp.zeros((CH, LN), F32)
    pulled = [
        pull((zero, zero, zero + 2.0, zero)),
        pull((zero, zero, zero, zero - 2.0)),
        pull((-2.0 * mr, -2.0 * mi, zero, zero)),
        pull((2.0 * mi, -2.0 * mr, zero, zero)),
    ]
    inverse = 1.0 / (raw[1] * raw[1] + raw[2] * raw[2])
    qr, qi = cmul(raw[3], raw[4], raw[1] * inverse, raw[2] * inverse)
    one_r, one_i = power(d, th, 1.0)
    er, ei = cmul(qr, qi, one_r, one_i)
    first_lanes = lane_block(zero) == 0
    for k, p in enumerate(pulled):
        pull_ref[k] = by_block(p[1:])
        pull_ref[4 + k] = jnp.where(first_lanes, p[0] * raw[0], 0.0)
    for k, value in enumerate((2.0 * qr, -2.0 * er, 2.0 * ei)):
        pull_ref[8 + k] = jnp.where(first_lanes, value, 0.0)


def within_kernel(
    wait_small, x_hbm, terms_ref, wide_ref, size_ref, damping_ref, frequency_ref, re_ref, im_ref,
    out_ref, far_r, far_i, step_r, step_i, pull_ref, x_ref, sems,
):
    loads = started(sems, (x_hbm.at[:, pl.ds(0, CK), :], x_ref))
    wait_small()
    pull_table(size_ref, damping_ref, frequency_ref, re_ref, im_ref, pull_ref)
    terms = terms_ref[0], terms_ref[1], terms_ref[2], terms_ref[3]
    decay, turn = terms[0], terms[1]
    near = [far_power(decay, turn, float(b)) for b in range(4)]
    for a in range(RANKS // 4):
        base = far_power(decay, turn, float(4 * a))
        for b in range(4):
            pr, pi = cmul(base[0], base[1], near[b][0], near[b][1]) if a and b else (
                base if a else near[b]
            )
            far_r[4 * a + b] = pr
            far_i[4 * a + b] = pi
    near = [far_power(decay, turn, b * LN / BLOCK) for b in range(4)]
    for a in range(CK // 4):
        base = far_power(decay, turn, 4 * a * LN / BLOCK)
        for b in range(4):
            step_r[4 * a + b], step_i[4 * a + b] = cmul(*base, *near[b])
    doubles = doublings(decay, turn)
    loads[0].wait()
    for g in range(GROUPS):
        taps = group_taps(terms, rising(decay, turn, doubles, g), g)
        for k in range(LANE_CH):
            c = g * LANE_CH + k
            matrix = toeplitz(taps[k : k + 1])
            high, low = split(matrix)
            x = x_ref[c]
            level = wide_ref[0, c : c + 1, :]
            out_ref[c * CK : (c + 1) * CK, :] = (
                dot2(x, (high, low)) + level * jnp.sum(matrix, 0, keepdims=True)
            )


def within(send, terms, wide, raw):
    return staged(
        within_kernel,
        (),
        (send,),
        (terms, wide, *raw),
        out_specs=[VMEM] * 6,
        out_shape=(
            jax.ShapeDtypeStruct((CH * CK, LN), F32),
            jax.ShapeDtypeStruct((RANKS, GROUPS, LN), F32),
            jax.ShapeDtypeStruct((RANKS, GROUPS, LN), F32),
            jax.ShapeDtypeStruct((CK, GROUPS, LN), F32),
            jax.ShapeDtypeStruct((CK, GROUPS, LN), F32),
            jax.ShapeDtypeStruct((11, CH, LN), F32),
        ),
        scratch_shapes=[pltpu.VMEM((CH, CK, LN), BF16), pltpu.SemaphoreType.DMA((1,))],
        name="within_chunks",
    )


def mixed_back(group, cot_ref, act_ref):
    mine = lax.broadcasted_iota(jnp.int32, (CH, LN), 1) == group * CH + lax.broadcasted_iota(
        jnp.int32, (CH, LN), 0
    )
    weights = dot(mine.astype(BF16), cot_ref[:, BLOCK:], NT).astype(BF16)
    for i in range(CK):
        act_ref[pl.ds(i, CH, stride=CK), :] = dot(weights, cot_ref[:, i * LN : (i + 1) * LN])


def gelu_both(x):
    scale = np.float32(np.sqrt(2.0 / np.pi))
    square = x * x
    t = jnp.tanh(scale * (x + 0.044715 * (square * x)))
    half = 0.5 * (1.0 + t)
    slope = half + 0.5 * x * (1.0 - t * t) * (scale * (1.0 + (3.0 * 0.044715) * square))
    return x * half, slope


def entering(states, table_r, table_i, distance):
    hr = jnp.zeros((GROUPS, LN), F32)
    hi = jnp.zeros((GROUPS, LN), F32)
    for d in range(RANKS):
        steps = distance(d)
        sr, si = states(d)
        at = jnp.maximum(steps, 0)
        nr, ni = cmul(table_r[at], table_i[at], sr, si)
        hr = jnp.where(steps >= 0, hr + nr, hr)
        hi = jnp.where(steps >= 0, hi + ni, hi)
    return hr, hi


def second_kernel(
    wait_small, me_ref, group_ref, c0h, c1h, c2h, c3h, out_hbm, got_hbm, x_hbm, terms_ref, wide_ref, far_r,
    far_i, step_r, step_i, sr_in, si_in, send_hbm, grad_hbm, mix_ref, sr_ref, si_ref,
    cot_ref, flat_ref, out_ref, got_ref, x_ref, act_ref, activation_ref, send_ref, grad_ref, table_ref, sems, out_sems,
):
    loads = started(
        sems,
        *[(c, cot_ref.at[pl.ds(m * CH, CH), :]) for m, c in enumerate((c0h, c1h, c2h, c3h))],
        (got_hbm.at[:, pl.ds(CK, CK), :], got_ref),
        (x_hbm.at[:, pl.ds(0, CK), :], x_ref),
        (out_hbm, out_ref),
    )
    wait_small.start(1)
    wait_small(0, 1)
    me = me_ref[0]
    terms = terms_ref[0], terms_ref[1], terms_ref[2], terms_ref[3]
    decay, turn = terms[0], terms[1]
    doubles = doublings(decay, turn)
    zr, zi = power(decay, turn, float(LN))
    one_r, one_i = power(decay, turn, 1.0)
    ur, ui = cmul(2.0 * terms[2], 2.0 * terms[3], one_r, one_i)
    for g in range(GROUPS):
        er, ei = rising(decay, turn, doubles, g)
        wr, wi = cmul(er, ei, ur[g : g + 1], ui[g : g + 1])
        table_ref[4 * g], table_ref[4 * g + 1] = split(jnp.concatenate([er, ei], 1))
        table_ref[4 * g + 2], table_ref[4 * g + 3] = split(jnp.concatenate([wr, wi], 1))
    for copy in loads[:4]:
        copy.wait()
    mixed_back(group_ref[0], cot_ref, act_ref)
    wait_small(1)
    loads[4].wait()
    start = entering(lambda d: unpacked_states(got_ref[d]), far_r, far_i, lambda d: me - 1 - d)
    add_entering(sr_ref, si_ref, sr_in, si_in, step_r, step_i, start, range(CK))
    for copy in loads[5:]:
        copy.wait()
    stores = []
    for g in range(GROUPS):
        every = pl.ds(g, CK, stride=GROUPS)
        inter = spread_group(
            sr_ref[every, :], si_ref[every, :], (table_ref[4 * g + 2], table_ref[4 * g + 3])
        )
        left = []
        for k in range(LANE_CH):
            c = g * LANE_CH + k
            rows = slice(c * CK, (c + 1) * CK)
            x = x_ref[c].astype(F32) + wide_ref[0, c : c + 1, :]
            mixed = out_ref[rows, :] + inter[k * CK : (k + 1) * CK] + wide_ref[1, c : c + 1, :] * x
            act, slope = gelu_both(mixed)
            activation_ref[rows, :] = act
            grad = act_ref[rows, :] * slope
            grad_ref[rows, :] = grad
            send_ref[c, :CK, :] = grad.astype(BF16)
            left.append(grad)
        stores.append(
            pltpu.make_async_copy(
                send_ref.at[pl.ds(g * LANE_CH, LANE_CH), pl.ds(0, CK), :],
                send_hbm.at[pl.ds(g * LANE_CH, LANE_CH), pl.ds(0, CK), :],
                out_sems.at[g],
            )
        )
        stores[-1].start()
        mine = pl.ds(g * LN, LN)
        stores.append(
            pltpu.make_async_copy(
                grad_ref.at[mine, :], grad_hbm.at[mine, :], out_sems.at[GROUPS + 1 + g]
            )
        )
        stores[-1].start()
        products = dot3(split(jnp.concatenate(left, 0)), (table_ref[4 * g], table_ref[4 * g + 1]))
        pr, pi = gather_group(products)
        sr_ref[every, :] = pr
        si_ref[every, :] = pi
    hr, hi = scan_states(sr_ref, si_ref, zr, zi, range(CK - 1, -1, -1))
    wait_small.store(3, 4)
    packed = packed_states(hr, hi)
    for d in range(RANKS):
        send_ref[d, CK:, :] = packed
    stores.append(
        pltpu.make_async_copy(
            send_ref.at[:, pl.ds(CK, CK), :], send_hbm.at[:, pl.ds(CK, CK), :],
            out_sems.at[GROUPS],
        )
    )
    stores[-1].start()
    for i in range(CK):
        flat_ref[:, i * LN : (i + 1) * LN] = activation_ref[pl.ds(i, CH, stride=CK), :].astype(BF16)
    mix_ref[...] = dot(flat_ref[...], cot_ref[:, :BLOCK], NT)
    wait_small.store(2)
    for copy in stores:
        copy.wait()


def second(me, group, parts, out, got, send, terms, wide, far, steps, sr, si):
    return staged(
        second_kernel,
        (me, group),
        (*parts, out, got, send),
        (terms, wide, far[0], far[1], steps[0], steps[1], sr, si),
        out_specs=[ANY] * 2 + [VMEM] * 3,
        out_shape=(
            jax.ShapeDtypeStruct((RANKS, SEND2, LN), BF16),
            jax.ShapeDtypeStruct((CH * CK, LN), F32),
            jax.ShapeDtypeStruct((CH, LN), F32),
            jax.ShapeDtypeStruct((CK * GROUPS, LN), F32),
            jax.ShapeDtypeStruct((CK * GROUPS, LN), F32),
        ),
        scratch_shapes=[
            pltpu.VMEM((LN, BLOCK + LN), BF16),
            pltpu.VMEM((CH, BLOCK), BF16),
            pltpu.VMEM((CH * CK, LN), F32),
            pltpu.VMEM((RANKS, CK, LN), BF16),
            pltpu.VMEM((CH, CK, LN), BF16),
            pltpu.VMEM((CH * CK, LN), F32),
            pltpu.VMEM((CH * CK, LN), F32),
            pltpu.VMEM((RANKS, SEND2, LN), BF16),
            pltpu.VMEM((CH * CK, LN), F32),
            pltpu.VMEM((4 * GROUPS, LN, 2 * LN), BF16),
            pltpu.SemaphoreType.DMA((7,)),
            pltpu.SemaphoreType.DMA((2 * GROUPS + 1,)),
        ],
        name="activation_and_states",
        eager=1,
        early=(2, 3, 4),
    )


def signal_kernel(
    wait_small, me_ref, got_hbm, send_hbm, cot_hbm, after_hbm, terms_ref, wide_ref, far_r, far_i,
    step_r, step_i, sr_in, si_in, out_ref, sr_ref, si_ref, rows_ref, got_ref, send_ref, cot_ref, sems,
):
    loads = started(
        sems,
        (got_hbm.at[:, pl.ds(CK, CK), :], got_ref),
        (send_hbm, send_ref),
        (cot_hbm, cot_ref),
    )
    wait_small()
    me = me_ref[0]
    terms = terms_ref[0], terms_ref[1], terms_ref[2], terms_ref[3]
    decay, turn = terms[0], terms[1]
    doubles = doublings(decay, turn)
    one_r, one_i = power(decay, turn, 1.0)
    ur, ui = cmul(2.0 * terms[2], 2.0 * terms[3], one_r, one_i)
    loads[0].wait()
    start = entering(lambda d: unpacked_states(got_ref[d]), far_r, far_i, lambda d: d - me - 1)
    add_entering(sr_ref, si_ref, sr_in, si_in, step_r, step_i, start, range(CK - 1, -1, -1))
    for copy in loads[1:]:
        copy.wait()
    for g in range(GROUPS):
        every = pl.ds(g, CK, stride=GROUPS)
        fr, fi = falling(decay, turn, doubles, g)
        wr, wi = cmul(fr, fi, ur[g : g + 1], ui[g : g + 1])
        inter = spread_group(sr_ref[every, :], si_ref[every, :], split(jnp.concatenate([wr, wi], 1)))
        taps = group_taps(terms, rising(decay, turn, doubles, g), g)
        for k in range(LANE_CH):
            c = g * LANE_CH + k
            grad = send_ref[c * CK : (c + 1) * CK, :]
            rows_ref[c * CK : (c + 1) * CK, :] = (
                dot3(split(grad), split(toeplitz(taps[k : k + 1])), NT)
                + inter[k * CK : (k + 1) * CK]
                + wide_ref[1, c : c + 1, :] * grad
            )
    for i in range(CK):
        cols = slice(i * LN, (i + 1) * LN)
        out_ref[:, cols] = (
            cot_ref[:, cols].astype(F32) + rows_ref[pl.ds(i, CH, stride=CK), :]
        ).astype(BF16)


def signal_grad(me, got, send, terms, wide, far, steps, sr, si, cotangent, after):
    return staged(
        signal_kernel,
        (me,),
        (got, send, cotangent, after),
        (terms, wide, far[0], far[1], steps[0], steps[1], sr, si),
        out_specs=[VMEM],
        out_shape=(
            jax.ShapeDtypeStruct((CH, BLOCK), BF16),
        ),
        scratch_shapes=[
            pltpu.VMEM((CK * GROUPS, LN), F32),
            pltpu.VMEM((CK * GROUPS, LN), F32),
            pltpu.VMEM((CH * CK, LN), F32),
            pltpu.VMEM((RANKS, CK, LN), BF16),
            pltpu.VMEM((CH * CK, LN), F32),
            pltpu.VMEM((CH, BLOCK), BF16),
            pltpu.SemaphoreType.DMA((3,)),
        ],
        name="signal_gradient",
        limit=62.5,
    )


def dft_tables():
    full_len = RANKS * BLOCK
    row = np.arange(ROWS)
    time_row = (row % RANKS) * (BLOCK // COLS) + row // RANKS
    first_ids = np.arange(ROWS)
    column = np.arange(COLS)
    angle1 = (
        2.0 * np.pi * (((4 * first_ids[:, None] + 1) * time_row[None, :]) % (4 * ROWS)) / (4 * ROWS)
    )
    angle_t = 2.0 * np.pi * ((4 * first_ids[:, None] + 1) * column[None, :]) / (4 * full_len)
    lane = np.arange(LN)
    angle2 = 2.0 * np.pi * ((lane[:, None] * lane[None, :]) % LN) / LN
    angle_p = 2.0 * np.pi * np.arange(PER)[:, None] * lane[None, :] / COLS

    def halves(values):
        values = values.astype(np.float32)
        high = values.astype(BF16)
        return high, (values - high.astype(np.float32)).astype(BF16)

    stage1 = np.concatenate([np.cos(angle1), -np.sin(angle1)], 0)
    cos2, sin2 = np.cos(angle2), np.sin(angle2)
    stage2 = np.concatenate(
        [np.concatenate([cos2, -sin2], 1), np.concatenate([sin2, cos2], 1)], 0
    )
    twiddle = np.stack([np.cos(angle_t), np.sin(angle_t)]).astype(np.float32)
    steps = np.concatenate([np.cos(angle_p), np.sin(angle_p)], 0).astype(np.float32)
    return halves(stage1), halves(stage1.T / full_len), halves(stage2), twiddle, steps


def gather_rows(ref, stride, base):
    return jnp.concatenate(
        [
            jnp.concatenate(
                [
                    ref[pl.ds(base + piece * PER + q, RANKS, stride=stride), :]
                    for q in range(PER)
                ],
                1,
            )
            for piece in range(BLOCK // COLS)
        ],
        0,
    )


def butterfly(parts, sign):
    (r0, i0), (r1, i1), (r2, i2), (r3, i3) = parts
    sr, si, dr, di = r0 + r2, i0 + i2, r0 - r2, i0 - i2
    tr, ti, er, ei = r1 + r3, i1 + i3, r1 - r3, i1 - i3
    if sign > 0:
        er, ei = -er, -ei
    return (sr + tr, si + ti), (dr + ei, di - er), (sr - tr, si - ti), (dr - ei, di + er)


def forward_dft(rows, exact, d1h, d1l, d2h, d2l, twiddle, steps, wait1, wait2):
    xh, xl = split(rows)
    wait1()
    if exact:
        a = dot(jnp.concatenate([d1h[...], d1l[...]], 1), jnp.concatenate([xh, xh], 0))
    else:
        a = dot3((d1h[...], d1l[...]), (xh, xl))
    wait2()
    parts = []
    for q in range(PER):
        cols = slice(q * LN, (q + 1) * LN)
        parts.append(cmul(a[:ROWS, cols], a[ROWS:, cols], twiddle[0, :, cols], -twiddle[1, :, cols]))
    out = []
    for p, (ur, ui) in enumerate(butterfly(parts, -1)):
        if p:
            ur, ui = cmul(ur, ui, steps[p : p + 1, :], -steps[PER + p : PER + p + 1, :])
        out.append(jnp.concatenate([ur, ui], 1))
    return dot3(split(jnp.concatenate(out, 0)), (d2h[...], d2l[...]))


def inverse_dft(spec, d1th, d1tl, d2h, d2l, twiddle, steps):
    v = dot3(split(spec), (d2h[...], d2l[...]), NT)
    parts = []
    for p in range(PER):
        vr, vi = v[p * ROWS : (p + 1) * ROWS, :LN], v[p * ROWS : (p + 1) * ROWS, LN:]
        if p:
            vr, vi = cmul(vr, vi, steps[p : p + 1, :], steps[PER + p : PER + p + 1, :])
        parts.append((vr, vi))
    real, imag = [], []
    for q, (br, bi) in enumerate(butterfly(parts, 1)):
        cols = slice(q * LN, (q + 1) * LN)
        br, bi = cmul(br, bi, twiddle[0, :, cols], twiddle[1, :, cols])
        real.append(br)
        imag.append(bi)
    bh, bl = split(
        jnp.concatenate([jnp.concatenate(real, 1), jnp.concatenate(imag, 1)], 0)
    )
    return dot3((d1th[...], d1tl[...]), (bh, bl))


def lane_block(row):
    return lax.broadcasted_iota(jnp.int32, row.shape, 1) // MODES


def repeated(row):
    row = jnp.where(lane_block(row) == 0, row, 0.0)
    total = row
    for m in range(1, LANE_CH):
        total = total + pltpu.roll(row, m * MODES, 1)
    return total


def by_block(rows):
    result = rows[0]
    for m in range(1, LANE_CH):
        result = jnp.where(lane_block(result) == m, rows[m], result)
    return result


def spectrum_kernel(
    wait_small, me_ref, got_hbm, d1h_hbm, d1l_hbm, twiddle_hbm, d2h_hbm, d2l_hbm, after_hbm,
    steps_ref, wide_ref, terms_ref, spec_ref, column_ref, turn_ref,
    got_ref, d1h, d1l, twiddle, d2h, d2l, rows_ref, sems,
):
    loads = started(
        sems,
        (got_hbm.at[:, pl.ds(0, CK), :], got_ref),
        (d1h_hbm, d1h), (d1l_hbm, d1l), (twiddle_hbm, twiddle), (d2h_hbm, d2h), (d2l_hbm, d2l),
    )
    wait_small()
    me = me_ref[0]
    embed = wide_ref[0, pl.ds(me, 1), :]
    loads[0].wait()
    for d in range(RANKS):
        rows_ref[d * CK : (d + 1) * CK, :] = got_ref[d].astype(F32) + embed
    rows = gather_rows(rows_ref, CK, 0)
    spec_ref[...] = forward_dft(
        rows, False, d1h, d1l, d2h, d2l, twiddle, steps_ref, waiting(loads[1:3]),
        waiting(loads[3:6]),
    )

    at, shift = me // LANE_CH, (me % LANE_CH) * MODES

    def own(k):
        row = jnp.broadcast_to(terms_ref[k, pl.ds(at, 1), :], (8, LN))
        return repeated(pltpu.roll(row, (LN - shift) % LN, 1)[:1])

    d, th = own(0), own(1)
    steps = lax.broadcasted_iota(jnp.int32, (8, LN), 0).astype(F32)
    cr, ci = power(d, th, steps)
    for k in (8, 16, 32, 64, 128, 256):
        zr, zi = far_power(d, th, float(k) / BLOCK)
        nr, ni = cmul(cr, ci, zr, zi)
        cr, ci = jnp.concatenate([cr, nr], 0), jnp.concatenate([ci, ni], 0)
    col = lax.broadcasted_iota(jnp.int32, (COLS, LN), 0).astype(F32)
    block = lane_block(col)
    table = jnp.where(block % 2 == 0, cr, ci)
    column_ref[...] = jnp.where(block < 2, table, table * col)
    ranks = lax.broadcasted_iota(jnp.int32, (RANKS, LN), 0).astype(F32)
    br, bi = far_power(d, th, ranks)
    for piece in range(BLOCK // COLS):
        zr, zi = far_power(d, th, float(piece * COLS) / BLOCK)
        nr, ni = cmul(br, bi, zr, zi) if piece else (br, bi)
        turn_ref[0, piece * RANKS : (piece + 1) * RANKS, :] = nr
        turn_ref[1, piece * RANKS : (piece + 1) * RANKS, :] = ni


def spectrum(me, got, after, wide, terms, tables):
    (d1h, d1l), unused, (d2h, d2l), twiddle, steps = tables
    return staged(
        spectrum_kernel,
        (me,),
        (got, d1h, d1l, twiddle, d2h, d2l, after),
        (steps, wide, terms),
        out_specs=[VMEM] * 3,
        out_shape=(
            jax.ShapeDtypeStruct((PER * ROWS, 2 * LN), F32),
            jax.ShapeDtypeStruct((COLS, LN), F32),
            jax.ShapeDtypeStruct((2, ROWS, LN), F32),
        ),
        scratch_shapes=[
            pltpu.VMEM((RANKS, CK, LN), BF16),
            pltpu.VMEM((2 * ROWS, ROWS), BF16),
            pltpu.VMEM((2 * ROWS, ROWS), BF16),
            pltpu.VMEM((2, ROWS, COLS), F32),
            pltpu.VMEM((2 * LN, 2 * LN), BF16),
            pltpu.VMEM((2 * LN, 2 * LN), BF16),
            pltpu.VMEM((RANKS * CK, LN), F32),
            pltpu.SemaphoreType.DMA((6,)),
        ],
        name="input_spectrum",
    )


def correlate_kernel(
    wait_small, got_hbm, d1h_hbm, d1l_hbm, twiddle_hbm, d2h_hbm, d2l_hbm, spec_hbm, d1th_hbm, d1tl_hbm,
    column_hbm, turn_hbm, steps_ref, m0, m1, m2, m3, send_hbm,
    got_ref, d1h, d1l, twiddle, d2h, d2l, spec_ref, d1th, d1tl, column_ref, turn_ref,
    rows_ref, send_ref, sems, out_sems,
):
    loads = started(
        sems,
        (got_hbm.at[:, pl.ds(0, CK), :], got_ref),
        (d1h_hbm, d1h), (d1l_hbm, d1l), (twiddle_hbm, twiddle), (d2h_hbm, d2h), (d2l_hbm, d2l),
        (spec_hbm, spec_ref), (d1th_hbm, d1th), (d1tl_hbm, d1tl), (column_hbm, column_ref),
        (turn_hbm, turn_ref),
    )
    wait_small()
    mixes = by_block([m[...] for m in (m0, m1, m2, m3)]).astype(BF16)
    for d in range(RANKS):
        send_ref[d, CK : 2 * CK, :] = mixes
    middle = pl.ds(CK, CK)
    stores = started(out_sems, (send_ref.at[:, middle, :], send_hbm.at[:, middle, :]))
    loads[0].wait()
    for d in range(RANKS):
        rows_ref[d * CK : (d + 1) * CK, :] = got_ref[d].astype(F32)
    g_rows = gather_rows(rows_ref, CK, 0)
    g_spec = forward_dft(
        g_rows, True, d1h, d1l, d2h, d2l, twiddle, steps_ref, waiting(loads[1:3]),
        waiting(loads[3:6]),
    )
    waiting(loads[6:7])()
    gr, gi = g_spec[:, :LN], g_spec[:, LN:]
    xr, xi = spec_ref[:, :LN], spec_ref[:, LN:]
    both = jnp.concatenate([xr * gr + xi * gi, xr * gi - xi * gr], 1)
    waiting(loads[7:])()
    kernel_rows = inverse_dft(both, d1th, d1tl, d2h, d2l, twiddle, steps_ref)
    for piece in range(BLOCK // COLS):
        for q in range(PER):
            rows_ref[pl.ds(piece * PER + q, RANKS, stride=CK), :] = kernel_rows[
                piece * RANKS : (piece + 1) * RANKS, q * LN : (q + 1) * LN
            ]
    for d in range(RANKS):
        send_ref[d, :CK, :] = rows_ref[d * CK : (d + 1) * CK, :].astype(BF16)
        if d % 8 == 7:
            part = pl.ds(d - 7, 8), pl.ds(0, CK)
            stores.append(
                pltpu.make_async_copy(
                    send_ref.at[part], send_hbm.at[part], out_sems.at[2 + d // 8]
                )
            )
            stores[-1].start()
    column = split(column_ref[...])
    inner = dot3(split(kernel_rows), column)
    g_inner = dot2(g_rows.astype(BF16), column)
    rr, ri = turn_ref[0], turn_ref[1]
    ids = lax.broadcasted_iota(jnp.int32, (ROWS, LN), 0)
    starts = ((ids % RANKS) * BLOCK + (ids // RANKS) * COLS).astype(F32)

    def total(values):
        return jnp.sum(values, 0, keepdims=True)

    by_r, by_i = rr * inner, ri * inner
    u, v = total(by_r), total(by_i)
    su, sv = total(starts * by_r), total(starts * by_i)
    gu, gv = total(rr * g_inner), total(ri * g_inner)

    lanes = lax.broadcasted_iota(jnp.int32, (1, LN), 1)
    scalars = jnp.where(lanes == 0, kernel_rows[0:1, 0:1], 0.0) + jnp.where(
        lanes == 1, jnp.sum(total(g_rows), 1, keepdims=True), 0.0
    )
    small = jnp.concatenate([u, v, su, sv, gu, gv, scalars, jnp.zeros((1, LN), F32)], 0)
    high, low = split(jnp.concatenate([small, small], 0))
    upper = lax.broadcasted_iota(jnp.int32, (16, LN), 0) < 8
    packed = jnp.where(upper, high.astype(F32), low.astype(F32)).astype(BF16)
    for d in range(RANKS):
        send_ref[d, 2 * CK :, :] = packed
    stores.append(
        pltpu.make_async_copy(
            send_ref.at[:, pl.ds(2 * CK, 16), :], send_hbm.at[:, pl.ds(2 * CK, 16), :],
            out_sems.at[1],
        )
    )
    stores[-1].start()
    for copy in stores:
        copy.wait()


def correlate(got, spec, tables, column, turns, mixes):
    (d1h, d1l), (d1th, d1tl), (d2h, d2l), twiddle, steps = tables
    return staged(
        correlate_kernel,
        (),
        (got, d1h, d1l, twiddle, d2h, d2l, spec, d1th, d1tl, column, turns),
        (steps, *mixes),
        out_specs=[ANY],
        out_shape=(
            jax.ShapeDtypeStruct((RANKS, SEND3, LN), BF16),
        ),
        scratch_shapes=[
            pltpu.VMEM((RANKS, CK, LN), BF16),
            pltpu.VMEM((2 * ROWS, ROWS), BF16),
            pltpu.VMEM((2 * ROWS, ROWS), BF16),
            pltpu.VMEM((2, ROWS, COLS), F32),
            pltpu.VMEM((2 * LN, 2 * LN), BF16),
            pltpu.VMEM((2 * LN, 2 * LN), BF16),
            pltpu.VMEM((PER * ROWS, 2 * LN), F32),
            pltpu.VMEM((ROWS, 2 * ROWS), BF16),
            pltpu.VMEM((ROWS, 2 * ROWS), BF16),
            pltpu.VMEM((COLS, LN), F32),
            pltpu.VMEM((2, ROWS, LN), F32),
            pltpu.VMEM((RANKS * CK, LN), F32),
            pltpu.VMEM((RANKS, SEND3, LN), BF16),
            pltpu.SemaphoreType.DMA((11,)),
            pltpu.SemaphoreType.DMA((6,)),
        ],
        name="correlation",
    )


def outputs_kernel(
    wait_small, step_ref, group_ref, got_ref, pull_ref, wide_ref, kernel_ref, damping_ref, frequency_ref, re_ref, im_ref,
    size_ref, skip_ref, mix_ref, table_ref, rows_ref, turned_ref,
):
    mixes = jnp.zeros((CH, LN), F32)
    for c in range(CH):
        rows_ref[c * CK : (c + 1) * CK, :] = got_ref[c, :CK, :].astype(F32)
        mixes = mixes + got_ref[c, CK : 2 * CK, :].astype(F32)
    for i in range(CK):
        kernel_ref[:, i * LN : (i + 1) * LN] = rows_ref[pl.ds(i, CH, stride=CK), :]
    for c in range(CH):
        small = got_ref[c, 2 * CK :, :].astype(F32)
        rows_ref[c * 8 : (c + 1) * 8, :] = small[:8] + small[8:]
    wait_small()
    u, v, su, sv, gu, gv, scalars = (rows_ref[pl.ds(k, CH, stride=8), :] for k in range(7))

    def block(row, k):
        moved = pltpu.roll(row, (LN - k * MODES) % LN, 1) if k else row
        return jnp.where(lane_block(row) == 0, moved, 0.0)

    sums = (
        block(u, 0) - block(v, 1),
        block(u, 1) + block(v, 0),
        block(u, 2) - block(v, 3) + block(su, 0) - block(sv, 1),
        block(u, 3) + block(v, 2) + block(su, 1) + block(sv, 0),
    )
    grads = jnp.zeros((CH, LN), F32)
    size = jnp.zeros((CH, LN), F32)
    for k, value in enumerate(sums):
        grads = grads + pull_ref[k] * repeated(value)
        size = size + pull_ref[4 + k] * value
    for k, ref in enumerate((damping_ref, frequency_ref, re_ref, im_ref)):
        ref[...] = grads[:, k * MODES : (k + 1) * MODES]
    g_sum = scalars[:, 1:2]
    back = (
        pull_ref[8] * g_sum
        + pull_ref[9] * (block(gu, 0) - block(gv, 1))
        + pull_ref[10] * (block(gu, 1) + block(gv, 0))
    )
    back_sum = jnp.sum(back, 1, keepdims=True) + wide_ref[1][:, :1] * g_sum
    lanes = lax.broadcasted_iota(jnp.int32, (CH, LN), 1)
    scalars = jnp.where(lanes == 0, jnp.sum(size, 1, keepdims=True), scalars[:, 0:1])
    turned = jnp.concatenate([scalars, jnp.zeros((LN - CH, LN), F32)], 0).T
    size_ref[...] = turned[0:1, :CH]
    skip_ref[...] = turned[1:2, :CH]
    picked = lax.broadcasted_iota(jnp.int32, table_ref.shape, 1) == step_ref[0]
    table_ref[...] = jnp.where(picked, back_sum, 0.0)
    turned_ref[...] = jnp.concatenate([mixes, jnp.zeros((LN - CH, LN), F32)], 0).T
    mix_ref[...] = jnp.concatenate(
        [
            turned_ref[pl.ds(pl.multiple_of((group_ref[0] ^ c) * CH, CH), CH), :][:, :CH]
            for c in range(LN // CH)
        ],
        1,
    )


def outputs(step, group, got, pull, levels, table_len):
    wide = jax.ShapeDtypeStruct((CH, MODES), F32)
    row = jax.ShapeDtypeStruct((1, CH), F32)
    return staged(
        outputs_kernel,
        (step, group),
        (got,),
        (pull, levels),
        out_specs=[VMEM] * 9,
        out_shape=(
            jax.ShapeDtypeStruct((CH, BLOCK), F32),
            wide, wide, wide, wide, row, row,
            jax.ShapeDtypeStruct((CH, LN), F32),
            jax.ShapeDtypeStruct((CH, table_len), F32),
        ),
        scratch_shapes=[pltpu.VMEM((CH * CK, LN), F32), pltpu.VMEM((LN, LN), F32)],
        name="outputs",
        plain_spec=VMEM,
        limit=8,
    )


def exchange(values):
    return lax.all_to_all(values, "tm", split_axis=0, concat_axis=0, tiled=True)


def shards(
    signal,
    cotangent,
    log_step,
    damping,
    frequency,
    coef_re,
    coef_im,
    skip_gain,
    mix_weight,
    embed_table,
    diffusion_step,
):
    me = lax.axis_index("tm").reshape(1)
    group = lax.axis_index("chan").reshape(1)
    tables = dft_tables()

    def swap(values, mask):
        return lax.ppermute(values, "chan", [(i, i ^ mask) for i in range(4)])

    send1, own, sr, si, terms, wide = first(
        diffusion_step, signal, cotangent, mix_weight, log_step[None], (damping, frequency, coef_re, coef_im),
        skip_gain[None], embed_table.T,
    )
    got1 = exchange(send1)
    own, across = lax.optimization_barrier((own, swap(own, 2)))
    parts = (own, swap(own, 1), across, swap(across, 1))
    raw = (log_step[None], damping, frequency, coef_re, coef_im)
    out, far_r, far_i, step_r, step_i, pull = within(send1, terms, wide, raw)
    far = (far_r, far_i)
    steps = (step_r, step_i)
    send2, grad, mix, br, bi = second(
        me, group, parts, out, got1, send1, terms, wide, far, steps, sr, si
    )
    got2 = exchange(send2)
    mixes = [mix] + [swap(mix, m) for m in range(1, 4)]
    spec, column, turns = spectrum(me, got1, mix, wide, terms, tables)
    (send3,) = correlate(got2, spec, tables, column, turns, mixes)
    got3 = exchange(send3)
    (grad_signal,) = signal_grad(
        me, got2, grad, terms, wide, far, steps, br, bi, cotangent, send3
    )
    kernel, g_damping, g_frequency, g_re, g_im, g_size, g_skip, g_mix, g_table = outputs(
        diffusion_step, group, got3, pull, wide, embed_table.shape[0]
    )
    return (
        grad_signal,
        kernel,
        g_size[0],
        g_damping,
        g_frequency,
        g_re,
        g_im,
        g_skip[0],
        g_mix,
        g_table.T,
    )


def solution(mesh):
    placed = (
        P("chan", "tm"),
        P("chan", "tm"),
        P("chan"),
        P("chan", None),
        P("chan", None),
        P("chan", None),
        P("chan", None),
        P("chan"),
        P("chan", None),
        P(None, "chan"),
        P(),
    )
    return jax.shard_map(
        shards,
        mesh=mesh,
        in_specs=placed,
        out_specs=(
            P("chan", "tm"),
            P("chan", "tm"),
            P("chan"),
            P("chan", None),
            P("chan", None),
            P("chan", None),
            P("chan", None),
            P("chan"),
            P("chan", None),
            P(None, "chan"),
        ),
        check_vma=False,
    )
```

```python
import functools

import jax
import jax.numpy as jnp
import numpy as np
from jax import lax
from jax.experimental import pallas as pl
from jax.experimental.pallas import tpu as pltpu
from jax.sharding import PartitionSpec as P

HIGHEST = lax.Precision.HIGHEST
F32 = jnp.float32
BF16 = jnp.bfloat16

CH = 32
MODES = 32
BLOCK = 4096
LN = 128
CK = BLOCK // LN
LANE_CH = LN // MODES
GROUPS = CH // LANE_CH
RANKS = 32
COLS = 512
PER = COLS // LN
ROWS = RANKS * BLOCK // COLS
PIECES = BLOCK // COLS
PLACE = [i % PER * PIECES + i // PER for i in range(CK)]
SEND1 = 64
SEND2 = 64
SEND3 = 80
NT = (((1,), (1,)), ((), ()))
NN = (((1,), (0,)), ((), ()))
GRANT = 63.75
SMEM = pl.BlockSpec(memory_space=pltpu.SMEM)
VMEM = pl.BlockSpec(memory_space=pltpu.VMEM)
ANY = pl.BlockSpec(memory_space=pl.ANY)
HBM = pl.BlockSpec(memory_space=pltpu.HBM)


def expm1_small(x):
    r = 1.0
    for k in (7.0, 6.0, 5.0, 4.0, 3.0, 2.0):
        r = 1.0 + x * r * (1.0 / k)
    return x * r


def mode_terms(step_size, damping, frequency, coef_re, coef_im):
    decay_rate = step_size * damping
    turn_rate = step_size * frequency
    half_sine = jnp.sin(0.5 * turn_rate)
    grow_real = expm1_small(-decay_rate) * jnp.cos(turn_rate) - 2.0 * half_sine * half_sine
    grow_imag = jnp.exp(-decay_rate) * jnp.sin(turn_rate)
    inverse = 1.0 / (damping * damping + frequency * frequency)
    hold_real = (frequency * grow_imag - damping * grow_real) * inverse
    hold_imag = -(frequency * grow_real + damping * grow_imag) * inverse
    weight_real = coef_re * hold_real - coef_im * hold_imag
    weight_imag = coef_re * hold_imag + coef_im * hold_real
    return (decay_rate, turn_rate, weight_real, weight_imag)


def cmul(ar, ai, br, bi):
    return ar * br - ai * bi, ar * bi + ai * br


def split(values):
    high = values.astype(BF16)
    return high, (values - high.astype(F32)).astype(BF16)


def dot(left, right, dims=NN):
    return lax.dot_general(left, right, dims, preferred_element_type=F32)


def dot3(left, right, dims=NN):
    (lh, ll), (rh, rl) = left, right
    (axis,), (other,) = dims[0]
    return dot(
        jnp.concatenate([lh, ll, lh], axis), jnp.concatenate([rh, rh, rl], other), dims
    )


def dot2(left, right, dims=NN):
    (axis,), (other,) = dims[0]
    return dot(jnp.concatenate([left, left], axis), jnp.concatenate(right, other), dims)


def started(sems, *pairs):
    copies = [pltpu.make_async_copy(a, b, sems.at[k]) for k, (a, b) in enumerate(pairs)]
    for copy in copies:
        copy.start()
    return copies


def waiting(copies):
    def wait(first=0, last=None):
        for copy in copies[first:last]:
            copy.wait()

    return wait


def staged(
    kernel, scalars, plain, small, *, out_specs, out_shape, scratch_shapes, name,
    plain_spec=HBM, limit=GRANT, eager=None, early=(),
):
    heads, outs = len(scalars) + len(plain), len(out_shape)

    def body(*refs):
        given, rest = refs[:heads], refs[heads:]
        sources, rest = rest[: len(small)], rest[len(small) :]
        results, rest = list(rest[:outs]), rest[outs:]
        held, sems, rest = rest[: len(small)], rest[len(small)], rest[len(small) + 1 :]
        written, out_sems, rest = rest[: len(early)], rest[len(early)], rest[len(early) + 1 :]
        copies = [
            pltpu.make_async_copy(a, b, sems.at[k]) for k, (a, b) in enumerate(zip(sources, held))
        ]
        leaving = {
            k: pltpu.make_async_copy(written[n], results[k], out_sems.at[n])
            for n, k in enumerate(early)
        }
        for n, k in enumerate(early):
            results[k] = written[n]
        gone = set()

        def start(first=0, last=None):
            for copy in copies[first:last]:
                copy.start()

        def store(*which):
            for k in which:
                leaving[k].start()
                gone.add(k)

        wait = waiting(copies)
        wait.start, wait.store = start, store
        start(0, eager)
        kernel(wait, *given, *held, *results, *rest)
        store(*[k for k in early if k not in gone])
        for copy in leaving.values():
            copy.wait()

    return pl.pallas_call(
        body,
        in_specs=[SMEM] * len(scalars) + [plain_spec] * len(plain) + [HBM] * len(small),
        out_specs=[HBM if k in early else spec for k, spec in enumerate(out_specs)],
        out_shape=out_shape,
        scratch_shapes=[pltpu.VMEM(a.shape, a.dtype) for a in small]
        + [pltpu.SemaphoreType.DMA((len(small),))]
        + [pltpu.VMEM(out_shape[k].shape, out_shape[k].dtype) for k in early]
        + [pltpu.SemaphoreType.DMA((max(len(early), 1),))]
        + scratch_shapes,
        compiler_params=pltpu.CompilerParams(vmem_limit_bytes=int(limit * 1024 * 1024)),
        name=name,
    )(*scalars, *plain, *small)


def sin_cos(x):
    y = x * x
    s = 1.0
    for k in (210.0, 156.0, 110.0, 72.0, 42.0, 20.0, 6.0):
        s = 1.0 - y * s * (1.0 / k)
    c = 1.0
    for k in (240.0, 182.0, 132.0, 90.0, 56.0, 30.0, 12.0, 2.0):
        c = 1.0 - y * c * (1.0 / k)
    return x * s, c


def power(decay, turn, steps):
    size = jnp.exp(-decay * steps)
    s, c = sin_cos(turn * steps)
    return size * c, size * s


def doublings(decay, turn):
    return [power(decay, turn, float(k)) for k in (8, 16, 32, 64)]


def rising(decay, turn, doubles, g):
    rows = lax.broadcasted_iota(jnp.int32, (8, LN), 0).astype(F32)
    tr, ti = power(decay[g : g + 1], turn[g : g + 1], rows)
    for zr, zi in doubles:
        nr, ni = cmul(tr, ti, zr[g : g + 1], zi[g : g + 1])
        tr, ti = jnp.concatenate([tr, nr], 0), jnp.concatenate([ti, ni], 0)
    return tr, ti


def falling(decay, turn, doubles, g):
    rows = 7.0 - lax.broadcasted_iota(jnp.int32, (8, LN), 0).astype(F32)
    tr, ti = power(decay[g : g + 1], turn[g : g + 1], rows)
    for zr, zi in doubles:
        nr, ni = cmul(tr, ti, zr[g : g + 1], zi[g : g + 1])
        tr, ti = jnp.concatenate([nr, tr], 0), jnp.concatenate([ni, ti], 0)
    return tr, ti


def lane_channel(shape):
    return lax.broadcasted_iota(jnp.int32, shape, 1) // MODES


def gather_group(products):
    owner = lane_channel((CK, LN))
    real, imag = products[:, :LN], products[:, LN:]
    out_r, out_i = real[:CK], imag[:CK]
    for k in range(1, LANE_CH):
        mine = owner == k
        out_r = jnp.where(mine, real[k * CK : (k + 1) * CK], out_r)
        out_i = jnp.where(mine, imag[k * CK : (k + 1) * CK], out_i)
    return out_r, out_i


def spread_group(state_r, state_i, table):
    owner = lane_channel((CK, LN))
    zero = jnp.zeros((CK, LN), F32)
    left = jnp.concatenate(
        [
            jnp.concatenate(
                [jnp.where(owner == k, state_r, zero), jnp.where(owner == k, -state_i, zero)], 1
            )
            for k in range(LANE_CH)
        ],
        0,
    )
    return dot3(split(left), table, NT)


def scan_states(sr_ref, si_ref, power_r, power_i, order):
    hr = jnp.zeros((GROUPS, LN), F32)
    hi = jnp.zeros((GROUPS, LN), F32)
    for i in order:
        rows = pl.ds(PLACE[i] * GROUPS, GROUPS)
        own_r, own_i = sr_ref[rows, :], si_ref[rows, :]
        sr_ref[rows, :] = hr
        si_ref[rows, :] = hi
        nr, ni = cmul(power_r, power_i, hr, hi)
        hr, hi = nr + own_r, ni + own_i
    return hr, hi


def add_entering(sr_ref, si_ref, sr_in, si_in, step_r, step_i, start, order):
    for k, i in enumerate(order):
        rows = pl.ds(PLACE[i] * GROUPS, GROUPS)
        nr, ni = cmul(step_r[k], step_i[k], *start) if k else start
        sr_ref[rows, :] = sr_in[rows, :] + nr
        si_ref[rows, :] = si_in[rows, :] + ni


def toeplitz(taps_row):
    rows = jnp.broadcast_to(taps_row, (LN, LN))
    turned = pltpu.roll(rows, 0, 1, stride=1, stride_axis=0)
    lag = lax.broadcasted_iota(jnp.int32, (LN, LN), 1) - lax.broadcasted_iota(
        jnp.int32, (LN, LN), 0
    )
    return jnp.where(lag >= 0, turned, 0.0)


def group_taps(terms, table, g):
    real = 2.0 * (terms[2][g : g + 1] * table[0] - terms[3][g : g + 1] * table[1])
    owner = (
        lane_channel((8, LN)) == lax.broadcasted_iota(jnp.int32, (8, LN), 0)
    ).astype(BF16)
    high, low = split(real)
    return dot2(owner, (high, low), NT)


def packed_lanes(ref):
    return jnp.concatenate([ref[pl.ds(k, GROUPS, stride=LANE_CH), :] for k in range(LANE_CH)], 1)


def as_column(row):
    shape = (CH, CH)
    same = lax.broadcasted_iota(jnp.int32, shape, 0) == lax.broadcasted_iota(jnp.int32, shape, 1)
    return jnp.sum(jnp.where(same, row, 0.0), 1, keepdims=True)


def first_kernel(
    wait_small, step_ref, signal_hbm, cot_hbm, mix_hbm, size_ref, damping_ref, frequency_ref, re_ref, im_ref,
    skip_ref, table_ref, send_hbm, own_hbm, sr_ref, si_ref, terms_ref, wide_ref,
    signal_ref, own_ref, send_ref, rows_ref, pack_ref, sems, out_sems,
):
    loads = started(
        sems,
        (signal_hbm, signal_ref),
        (cot_hbm, own_ref.at[:, pl.ds(0, BLOCK)]),
        (mix_hbm, own_ref.at[:, pl.ds(BLOCK, LN)]),
    )
    wait_small()
    picked = lax.broadcasted_iota(jnp.int32, table_ref.shape, 1) == step_ref[0]
    embed = jnp.sum(jnp.where(picked, table_ref[...], 0.0), 1, keepdims=True)
    wide_ref[0] = jnp.broadcast_to(embed, (CH, LN))
    wide_ref[1] = jnp.broadcast_to(as_column(skip_ref[...]), (CH, LN))
    pack_ref[...] = jnp.broadcast_to(embed, (CH, MODES))
    embed_lanes = packed_lanes(pack_ref)
    pack_ref[...] = jnp.broadcast_to(as_column(jnp.exp(size_ref[...])), (CH, MODES))
    raw = [packed_lanes(r) for r in (pack_ref, damping_ref, frequency_ref, re_ref, im_ref)]
    terms = mode_terms(*raw)
    for k in range(4):
        terms_ref[k] = terms[k]
    wait_small.store(4, 5)
    decay, turn = terms[0], terms[1]
    doubles = doublings(decay, turn)
    loads[0].wait()
    for i in range(CK):
        rows_ref[pl.ds(PLACE[i], CH, stride=CK), :] = signal_ref[
            :, i * LN : (i + 1) * LN
        ].astype(F32)
    for c in range(CH):
        send_ref[c, :CK, :] = rows_ref[c * CK : (c + 1) * CK, :].astype(BF16)
    loads[1].wait()
    loads[2].wait()
    stores = started(
        out_sems,
        (send_ref.at[:, pl.ds(0, CK), :], send_hbm.at[:, pl.ds(0, CK), :]),
        (own_ref, own_hbm),
    )
    for g in range(GROUPS):
        x = rows_ref[g * LN : (g + 1) * LN, :].astype(BF16)
        fr, fi = falling(decay, turn, doubles, g)
        table = jnp.concatenate([fr, fi], 1)
        th, tl = split(table)
        pr, pi = gather_group(dot2(x, (th, tl)))
        level = embed_lanes[g : g + 1]
        sr_ref[pl.ds(g, CK, stride=GROUPS), :] = pr + level * jnp.sum(fr, 0, keepdims=True)
        si_ref[pl.ds(g, CK, stride=GROUPS), :] = pi + level * jnp.sum(fi, 0, keepdims=True)
    zr, zi = power(decay, turn, float(LN))
    hr, hi = scan_states(sr_ref, si_ref, zr, zi, range(CK))
    wait_small.store(2, 3)
    packed = packed_states(hr, hi)
    for d in range(RANKS):
        send_ref[d, CK:, :] = packed
    last = pltpu.make_async_copy(
        send_ref.at[:, pl.ds(CK, CK), :], send_hbm.at[:, pl.ds(CK, CK), :], out_sems.at[2]
    )
    last.start()
    for copy in stores + [last]:
        copy.wait()


def packed_states(hr, hi):
    high, low = split(jnp.concatenate([hr, hi], 0))
    return jnp.concatenate([high, low], 0)


def unpacked_states(packed):
    packed = packed.astype(F32)
    values = packed[: 2 * GROUPS] + packed[2 * GROUPS :]
    return values[:GROUPS], values[GROUPS:]


def first(step, signal, cotangent, mix_weight, sizes, params, skip, table):
    return staged(
        first_kernel,
        (step,),
        (signal, cotangent, mix_weight),
        (sizes, *params, skip, table),
        out_specs=[ANY] * 2 + [VMEM] * 4,
        out_shape=(
            jax.ShapeDtypeStruct((RANKS, SEND1, LN), BF16),
            jax.ShapeDtypeStruct((CH, BLOCK + LN), BF16),
            jax.ShapeDtypeStruct((CK * GROUPS, LN), F32),
            jax.ShapeDtypeStruct((CK * GROUPS, LN), F32),
            jax.ShapeDtypeStruct((4, GROUPS, LN), F32),
            jax.ShapeDtypeStruct((2, CH, LN), F32),
        ),
        scratch_shapes=[
            pltpu.VMEM((CH, BLOCK), BF16),
            pltpu.VMEM((CH, BLOCK + LN), BF16),
            pltpu.VMEM((RANKS, SEND1, LN), BF16),
            pltpu.VMEM((CH * CK, LN), F32),
            pltpu.VMEM((CH, MODES), F32),
            pltpu.SemaphoreType.DMA((3,)),
            pltpu.SemaphoreType.DMA((3,)),
        ],
        name="block_states",
        early=(2, 3, 4, 5),
    )


def wide_sin_cos(x):
    turns = jnp.floor(x * np.float32(1.0 / (2.0 * np.pi)) + 0.5)
    x = (x - turns * np.float32(6.28125)) - turns * np.float32(2.0 * np.pi - 6.28125)
    s, c = sin_cos(0.5 * x)
    return 2.0 * s * c, 1.0 - 2.0 * s * s


def far_power(decay, turn, blocks):
    size = jnp.exp(-decay * (BLOCK * blocks))
    s, c = wide_sin_cos(turn * (BLOCK * blocks))
    return size * c, size * s


def pull_table(size_ref, damping_ref, frequency_ref, re_ref, im_ref, pull_ref):
    def tiled(values):
        return jnp.concatenate([values] * LANE_CH, 1)

    size = jnp.broadcast_to(as_column(jnp.exp(size_ref[...])), (CH, LN))
    raw = [size] + [tiled(r[...]) for r in (damping_ref, frequency_ref, re_ref, im_ref)]
    (d, th, mr, mi), pull = jax.vjp(mode_terms, *raw)
    zero = jnp.zeros((CH, LN), F32)
    pulled = [
        pull((zero, zero, zero + 2.0, zero)),
        pull((zero, zero, zero, zero - 2.0)),
        pull((-2.0 * mr, -2.0 * mi, zero, zero)),
        pull((2.0 * mi, -2.0 * mr, zero, zero)),
    ]
    inverse = 1.0 / (raw[1] * raw[1] + raw[2] * raw[2])
    qr, qi = cmul(raw[3], raw[4], raw[1] * inverse, raw[2] * inverse)
    one_r, one_i = power(d, th, 1.0)
    er, ei = cmul(qr, qi, one_r, one_i)
    first_lanes = lane_block(zero) == 0
    for k, p in enumerate(pulled):
        pull_ref[k] = by_block(p[1:])
        pull_ref[4 + k] = jnp.where(first_lanes, p[0] * raw[0], 0.0)
    for k, value in enumerate((2.0 * qr, -2.0 * er, 2.0 * ei)):
        pull_ref[8 + k] = jnp.where(first_lanes, value, 0.0)


def within_kernel(
    wait_small, x_hbm, terms_ref, wide_ref, size_ref, damping_ref, frequency_ref, re_ref, im_ref,
    out_ref, far_r, far_i, step_r, step_i, pull_ref, x_ref, sems,
):
    loads = started(sems, (x_hbm.at[:, pl.ds(0, CK), :], x_ref))
    wait_small()
    pull_table(size_ref, damping_ref, frequency_ref, re_ref, im_ref, pull_ref)
    terms = terms_ref[0], terms_ref[1], terms_ref[2], terms_ref[3]
    decay, turn = terms[0], terms[1]
    near = [far_power(decay, turn, float(b)) for b in range(4)]
    for a in range(RANKS // 4):
        base = far_power(decay, turn, float(4 * a))
        for b in range(4):
            pr, pi = cmul(base[0], base[1], near[b][0], near[b][1]) if a and b else (
                base if a else near[b]
            )
            far_r[4 * a + b] = pr
            far_i[4 * a + b] = pi
    near = [far_power(decay, turn, b * LN / BLOCK) for b in range(4)]
    for a in range(CK // 4):
        base = far_power(decay, turn, 4 * a * LN / BLOCK)
        for b in range(4):
            step_r[4 * a + b], step_i[4 * a + b] = cmul(*base, *near[b])
    doubles = doublings(decay, turn)
    loads[0].wait()
    for g in range(GROUPS):
        taps = group_taps(terms, rising(decay, turn, doubles, g), g)
        for k in range(LANE_CH):
            c = g * LANE_CH + k
            matrix = toeplitz(taps[k : k + 1])
            high, low = split(matrix)
            x = x_ref[c]
            level = wide_ref[0, c : c + 1, :]
            out_ref[c * CK : (c + 1) * CK, :] = (
                dot2(x, (high, low)) + level * jnp.sum(matrix, 0, keepdims=True)
            )


def within(send, terms, wide, raw):
    return staged(
        within_kernel,
        (),
        (send,),
        (terms, wide, *raw),
        out_specs=[VMEM] * 6,
        out_shape=(
            jax.ShapeDtypeStruct((CH * CK, LN), F32),
            jax.ShapeDtypeStruct((RANKS, GROUPS, LN), F32),
            jax.ShapeDtypeStruct((RANKS, GROUPS, LN), F32),
            jax.ShapeDtypeStruct((CK, GROUPS, LN), F32),
            jax.ShapeDtypeStruct((CK, GROUPS, LN), F32),
            jax.ShapeDtypeStruct((11, CH, LN), F32),
        ),
        scratch_shapes=[pltpu.VMEM((CH, CK, LN), BF16), pltpu.SemaphoreType.DMA((1,))],
        name="within_chunks",
    )


def mixed_back(group, cot_ref, act_ref):
    mine = lax.broadcasted_iota(jnp.int32, (CH, LN), 1) == group * CH + lax.broadcasted_iota(
        jnp.int32, (CH, LN), 0
    )
    weights = dot(mine.astype(BF16), cot_ref[:, BLOCK:], NT).astype(BF16)
    for i in range(CK):
        act_ref[pl.ds(PLACE[i], CH, stride=CK), :] = dot(
            weights, cot_ref[:, i * LN : (i + 1) * LN]
        )


def gelu_both(x):
    scale = np.float32(np.sqrt(2.0 / np.pi))
    square = x * x
    t = jnp.tanh(scale * (x + 0.044715 * (square * x)))
    half = 0.5 * (1.0 + t)
    slope = half + 0.5 * x * (1.0 - t * t) * (scale * (1.0 + (3.0 * 0.044715) * square))
    return x * half, slope


def entering(states, table_r, table_i, distance):
    hr = jnp.zeros((GROUPS, LN), F32)
    hi = jnp.zeros((GROUPS, LN), F32)
    for d in range(RANKS):
        steps = distance(d)
        sr, si = states(d)
        at = jnp.maximum(steps, 0)
        nr, ni = cmul(table_r[at], table_i[at], sr, si)
        hr = jnp.where(steps >= 0, hr + nr, hr)
        hi = jnp.where(steps >= 0, hi + ni, hi)
    return hr, hi


def second_kernel(
    wait_small, me_ref, group_ref, c0h, c1h, c2h, c3h, out_hbm, got_hbm, x_hbm, terms_ref, wide_ref, far_r,
    far_i, step_r, step_i, sr_in, si_in, send_hbm, grad_hbm, mix_ref, sr_ref, si_ref,
    cot_ref, flat_ref, out_ref, got_ref, x_ref, act_ref, activation_ref, send_ref, grad_ref, table_ref, sems, out_sems,
):
    loads = started(
        sems,
        *[(c, cot_ref.at[pl.ds(m * CH, CH), :]) for m, c in enumerate((c0h, c1h, c2h, c3h))],
        (got_hbm.at[:, pl.ds(CK, CK), :], got_ref),
        (x_hbm.at[:, pl.ds(0, CK), :], x_ref),
        (out_hbm, out_ref),
    )
    wait_small.start(1)
    wait_small(0, 1)
    me = me_ref[0]
    terms = terms_ref[0], terms_ref[1], terms_ref[2], terms_ref[3]
    decay, turn = terms[0], terms[1]
    doubles = doublings(decay, turn)
    zr, zi = power(decay, turn, float(LN))
    one_r, one_i = power(decay, turn, 1.0)
    ur, ui = cmul(2.0 * terms[2], 2.0 * terms[3], one_r, one_i)
    for g in range(GROUPS):
        er, ei = rising(decay, turn, doubles, g)
        wr, wi = cmul(er, ei, ur[g : g + 1], ui[g : g + 1])
        table_ref[4 * g], table_ref[4 * g + 1] = split(jnp.concatenate([er, ei], 1))
        table_ref[4 * g + 2], table_ref[4 * g + 3] = split(jnp.concatenate([wr, wi], 1))
    for copy in loads[:4]:
        copy.wait()
    mixed_back(group_ref[0], cot_ref, act_ref)
    wait_small(1)
    loads[4].wait()
    start = entering(lambda d: unpacked_states(got_ref[d]), far_r, far_i, lambda d: me - 1 - d)
    add_entering(sr_ref, si_ref, sr_in, si_in, step_r, step_i, start, range(CK))
    for copy in loads[5:]:
        copy.wait()
    stores = []
    for g in range(GROUPS):
        every = pl.ds(g, CK, stride=GROUPS)
        inter = spread_group(
            sr_ref[every, :], si_ref[every, :], (table_ref[4 * g + 2], table_ref[4 * g + 3])
        )
        left = []
        for k in range(LANE_CH):
            c = g * LANE_CH + k
            rows = slice(c * CK, (c + 1) * CK)
            x = x_ref[c].astype(F32) + wide_ref[0, c : c + 1, :]
            mixed = out_ref[rows, :] + inter[k * CK : (k + 1) * CK] + wide_ref[1, c : c + 1, :] * x
            act, slope = gelu_both(mixed)
            activation_ref[rows, :] = act
            grad = act_ref[rows, :] * slope
            grad_ref[rows, :] = grad
            send_ref[c, :CK, :] = grad.astype(BF16)
            left.append(grad)
        stores.append(
            pltpu.make_async_copy(
                send_ref.at[pl.ds(g * LANE_CH, LANE_CH), pl.ds(0, CK), :],
                send_hbm.at[pl.ds(g * LANE_CH, LANE_CH), pl.ds(0, CK), :],
                out_sems.at[g],
            )
        )
        stores[-1].start()
        mine = pl.ds(g * LN, LN)
        stores.append(
            pltpu.make_async_copy(
                grad_ref.at[mine, :], grad_hbm.at[mine, :], out_sems.at[GROUPS + 1 + g]
            )
        )
        stores[-1].start()
        products = dot3(split(jnp.concatenate(left, 0)), (table_ref[4 * g], table_ref[4 * g + 1]))
        pr, pi = gather_group(products)
        sr_ref[every, :] = pr
        si_ref[every, :] = pi
    hr, hi = scan_states(sr_ref, si_ref, zr, zi, range(CK - 1, -1, -1))
    wait_small.store(3, 4)
    packed = packed_states(hr, hi)
    for d in range(RANKS):
        send_ref[d, CK:, :] = packed
    stores.append(
        pltpu.make_async_copy(
            send_ref.at[:, pl.ds(CK, CK), :], send_hbm.at[:, pl.ds(CK, CK), :],
            out_sems.at[GROUPS],
        )
    )
    stores[-1].start()
    for i in range(CK):
        flat_ref[:, i * LN : (i + 1) * LN] = activation_ref[
            pl.ds(PLACE[i], CH, stride=CK), :
        ].astype(BF16)
    mix_ref[...] = dot(flat_ref[...], cot_ref[:, :BLOCK], NT)
    wait_small.store(2)
    for copy in stores:
        copy.wait()


def second(me, group, parts, out, got, send, terms, wide, far, steps, sr, si):
    return staged(
        second_kernel,
        (me, group),
        (*parts, out, got, send),
        (terms, wide, far[0], far[1], steps[0], steps[1], sr, si),
        out_specs=[ANY] * 2 + [VMEM] * 3,
        out_shape=(
            jax.ShapeDtypeStruct((RANKS, SEND2, LN), BF16),
            jax.ShapeDtypeStruct((CH * CK, LN), F32),
            jax.ShapeDtypeStruct((CH, LN), F32),
            jax.ShapeDtypeStruct((CK * GROUPS, LN), F32),
            jax.ShapeDtypeStruct((CK * GROUPS, LN), F32),
        ),
        scratch_shapes=[
            pltpu.VMEM((LN, BLOCK + LN), BF16),
            pltpu.VMEM((CH, BLOCK), BF16),
            pltpu.VMEM((CH * CK, LN), F32),
            pltpu.VMEM((RANKS, CK, LN), BF16),
            pltpu.VMEM((CH, CK, LN), BF16),
            pltpu.VMEM((CH * CK, LN), F32),
            pltpu.VMEM((CH * CK, LN), F32),
            pltpu.VMEM((RANKS, SEND2, LN), BF16),
            pltpu.VMEM((CH * CK, LN), F32),
            pltpu.VMEM((4 * GROUPS, LN, 2 * LN), BF16),
            pltpu.SemaphoreType.DMA((7,)),
            pltpu.SemaphoreType.DMA((2 * GROUPS + 1,)),
        ],
        name="activation_and_states",
        eager=1,
        early=(2, 3, 4),
    )


def signal_kernel(
    wait_small, me_ref, got_hbm, send_hbm, cot_hbm, after_hbm, terms_ref, wide_ref, far_r, far_i,
    step_r, step_i, sr_in, si_in, out_ref, sr_ref, si_ref, rows_ref, got_ref, send_ref, cot_ref, sems,
):
    loads = started(
        sems,
        (got_hbm.at[:, pl.ds(CK, CK), :], got_ref),
        (send_hbm, send_ref),
        (cot_hbm, cot_ref),
    )
    wait_small()
    me = me_ref[0]
    terms = terms_ref[0], terms_ref[1], terms_ref[2], terms_ref[3]
    decay, turn = terms[0], terms[1]
    doubles = doublings(decay, turn)
    one_r, one_i = power(decay, turn, 1.0)
    ur, ui = cmul(2.0 * terms[2], 2.0 * terms[3], one_r, one_i)
    loads[0].wait()
    start = entering(lambda d: unpacked_states(got_ref[d]), far_r, far_i, lambda d: d - me - 1)
    add_entering(sr_ref, si_ref, sr_in, si_in, step_r, step_i, start, range(CK - 1, -1, -1))
    for copy in loads[1:]:
        copy.wait()
    for g in range(GROUPS):
        every = pl.ds(g, CK, stride=GROUPS)
        fr, fi = falling(decay, turn, doubles, g)
        wr, wi = cmul(fr, fi, ur[g : g + 1], ui[g : g + 1])
        inter = spread_group(sr_ref[every, :], si_ref[every, :], split(jnp.concatenate([wr, wi], 1)))
        taps = group_taps(terms, rising(decay, turn, doubles, g), g)
        for k in range(LANE_CH):
            c = g * LANE_CH + k
            grad = send_ref[c * CK : (c + 1) * CK, :]
            rows_ref[c * CK : (c + 1) * CK, :] = (
                dot3(split(grad), split(toeplitz(taps[k : k + 1])), NT)
                + inter[k * CK : (k + 1) * CK]
                + wide_ref[1, c : c + 1, :] * grad
            )
    for i in range(CK):
        cols = slice(i * LN, (i + 1) * LN)
        out_ref[:, cols] = (
            cot_ref[:, cols].astype(F32) + rows_ref[pl.ds(PLACE[i], CH, stride=CK), :]
        ).astype(BF16)


def signal_grad(me, got, send, terms, wide, far, steps, sr, si, cotangent, after):
    return staged(
        signal_kernel,
        (me,),
        (got, send, cotangent, after),
        (terms, wide, far[0], far[1], steps[0], steps[1], sr, si),
        out_specs=[VMEM],
        out_shape=(
            jax.ShapeDtypeStruct((CH, BLOCK), BF16),
        ),
        scratch_shapes=[
            pltpu.VMEM((CK * GROUPS, LN), F32),
            pltpu.VMEM((CK * GROUPS, LN), F32),
            pltpu.VMEM((CH * CK, LN), F32),
            pltpu.VMEM((RANKS, CK, LN), BF16),
            pltpu.VMEM((CH * CK, LN), F32),
            pltpu.VMEM((CH, BLOCK), BF16),
            pltpu.SemaphoreType.DMA((3,)),
        ],
        name="signal_gradient",
        limit=62.5,
    )


def dft_tables():
    full_len = RANKS * BLOCK
    row = np.arange(ROWS)
    first_ids = np.arange(ROWS)
    column = np.arange(COLS)
    angle1 = (
        2.0 * np.pi * (((4 * first_ids[:, None] + 1) * row[None, :]) % (4 * ROWS)) / (4 * ROWS)
    )
    angle_t = 2.0 * np.pi * ((4 * first_ids[:, None] + 1) * column[None, :]) / (4 * full_len)
    lane = np.arange(LN)
    angle2 = 2.0 * np.pi * ((lane[:, None] * lane[None, :]) % LN) / LN
    angle_p = 2.0 * np.pi * np.arange(PER)[:, None] * lane[None, :] / COLS

    def halves(values):
        values = values.astype(np.float32)
        high = values.astype(BF16)
        return high, (values - high.astype(np.float32)).astype(BF16)

    stage1 = np.concatenate([np.cos(angle1), -np.sin(angle1)], 0)
    cos2, sin2 = np.cos(angle2), np.sin(angle2)
    stage2 = np.concatenate(
        [np.concatenate([cos2, -sin2], 1), np.concatenate([sin2, cos2], 1)], 0
    )
    twiddle = np.stack([np.cos(angle_t), np.sin(angle_t)]).astype(np.float32)
    steps = np.concatenate([np.cos(angle_p), np.sin(angle_p)], 0).astype(np.float32)
    return halves(stage1), halves(stage1.T / full_len), halves(stage2), twiddle, steps


def gather_rows(ref):
    result = []
    for d in range(RANKS):
        block = ref[d].astype(F32)
        result.append(
            jnp.concatenate([block[q * PIECES : (q + 1) * PIECES] for q in range(PER)], 1)
        )
    return jnp.concatenate(result, 0)


def butterfly(parts, sign):
    (r0, i0), (r1, i1), (r2, i2), (r3, i3) = parts
    sr, si, dr, di = r0 + r2, i0 + i2, r0 - r2, i0 - i2
    tr, ti, er, ei = r1 + r3, i1 + i3, r1 - r3, i1 - i3
    if sign > 0:
        er, ei = -er, -ei
    return (sr + tr, si + ti), (dr + ei, di - er), (sr - tr, si - ti), (dr - ei, di + er)


def forward_dft(rows, exact, d1h, d1l, d2h, d2l, twiddle, steps, wait1, wait2):
    xh, xl = split(rows)
    wait1()
    if exact:
        a = dot(jnp.concatenate([d1h[...], d1l[...]], 1), jnp.concatenate([xh, xh], 0))
    else:
        a = dot3((d1h[...], d1l[...]), (xh, xl))
    wait2()
    parts = []
    for q in range(PER):
        cols = slice(q * LN, (q + 1) * LN)
        parts.append(cmul(a[:ROWS, cols], a[ROWS:, cols], twiddle[0, :, cols], -twiddle[1, :, cols]))
    out = []
    for p, (ur, ui) in enumerate(butterfly(parts, -1)):
        if p:
            ur, ui = cmul(ur, ui, steps[p : p + 1, :], -steps[PER + p : PER + p + 1, :])
        out.append(jnp.concatenate([ur, ui], 1))
    return dot3(split(jnp.concatenate(out, 0)), (d2h[...], d2l[...]))


def inverse_dft(spec, d1th, d1tl, d2h, d2l, twiddle, steps):
    v = dot3(split(spec), (d2h[...], d2l[...]), NT)
    parts = []
    for p in range(PER):
        vr, vi = v[p * ROWS : (p + 1) * ROWS, :LN], v[p * ROWS : (p + 1) * ROWS, LN:]
        if p:
            vr, vi = cmul(vr, vi, steps[p : p + 1, :], steps[PER + p : PER + p + 1, :])
        parts.append((vr, vi))
    real, imag = [], []
    for q, (br, bi) in enumerate(butterfly(parts, 1)):
        cols = slice(q * LN, (q + 1) * LN)
        br, bi = cmul(br, bi, twiddle[0, :, cols], twiddle[1, :, cols])
        real.append(br)
        imag.append(bi)
    bh, bl = split(
        jnp.concatenate([jnp.concatenate(real, 1), jnp.concatenate(imag, 1)], 0)
    )
    return dot3((d1th[...], d1tl[...]), (bh, bl))


def lane_block(row):
    return lax.broadcasted_iota(jnp.int32, row.shape, 1) // MODES


def repeated(row):
    row = jnp.where(lane_block(row) == 0, row, 0.0)
    total = row
    for m in range(1, LANE_CH):
        total = total + pltpu.roll(row, m * MODES, 1)
    return total


def by_block(rows):
    result = rows[0]
    for m in range(1, LANE_CH):
        result = jnp.where(lane_block(result) == m, rows[m], result)
    return result


def spectrum_kernel(
    wait_small, me_ref, got_hbm, d1h_hbm, d1l_hbm, twiddle_hbm, d2h_hbm, d2l_hbm, after_hbm,
    steps_ref, wide_ref, terms_ref, spec_ref, column_ref, turn_ref,
    got_ref, d1h, d1l, twiddle, d2h, d2l, sems,
):
    loads = started(
        sems,
        (got_hbm.at[:, pl.ds(0, CK), :], got_ref),
        (d1h_hbm, d1h), (d1l_hbm, d1l), (twiddle_hbm, twiddle), (d2h_hbm, d2h), (d2l_hbm, d2l),
    )
    wait_small()
    me = me_ref[0]
    embed = wide_ref[0, pl.ds(me, 1), :]
    loads[0].wait()
    rows = gather_rows(got_ref) + jnp.concatenate([embed] * PER, 1)
    spec_ref[...] = forward_dft(
        rows, False, d1h, d1l, d2h, d2l, twiddle, steps_ref, waiting(loads[1:3]),
        waiting(loads[3:6]),
    )

    at, shift = me // LANE_CH, (me % LANE_CH) * MODES

    def own(k):
        row = jnp.broadcast_to(terms_ref[k, pl.ds(at, 1), :], (8, LN))
        return repeated(pltpu.roll(row, (LN - shift) % LN, 1)[:1])

    d, th = own(0), own(1)
    steps = lax.broadcasted_iota(jnp.int32, (8, LN), 0).astype(F32)
    cr, ci = power(d, th, steps)
    for k in (8, 16, 32, 64, 128, 256):
        zr, zi = far_power(d, th, float(k) / BLOCK)
        nr, ni = cmul(cr, ci, zr, zi)
        cr, ci = jnp.concatenate([cr, nr], 0), jnp.concatenate([ci, ni], 0)
    col = lax.broadcasted_iota(jnp.int32, (COLS, LN), 0).astype(F32)
    block = lane_block(col)
    table = jnp.where(block % 2 == 0, cr, ci)
    column_ref[...] = jnp.where(block < 2, table, table * col)
    ranks = lax.broadcasted_iota(jnp.int32, (RANKS, LN), 0).astype(F32)
    br, bi = far_power(d, th, ranks)
    pieces = lax.broadcasted_iota(jnp.int32, (PIECES, LN), 0).astype(F32) * (COLS / BLOCK)
    pr, pi = far_power(d, th, pieces)
    for k in range(RANKS):
        rows = slice(k * PIECES, (k + 1) * PIECES)
        turn_ref[0, rows, :], turn_ref[1, rows, :] = cmul(
            pr, pi, br[k : k + 1], bi[k : k + 1]
        )


def spectrum(me, got, after, wide, terms, tables):
    (d1h, d1l), unused, (d2h, d2l), twiddle, steps = tables
    return staged(
        spectrum_kernel,
        (me,),
        (got, d1h, d1l, twiddle, d2h, d2l, after),
        (steps, wide, terms),
        out_specs=[VMEM] * 3,
        out_shape=(
            jax.ShapeDtypeStruct((PER * ROWS, 2 * LN), F32),
            jax.ShapeDtypeStruct((COLS, LN), F32),
            jax.ShapeDtypeStruct((2, ROWS, LN), F32),
        ),
        scratch_shapes=[
            pltpu.VMEM((RANKS, CK, LN), BF16),
            pltpu.VMEM((2 * ROWS, ROWS), BF16),
            pltpu.VMEM((2 * ROWS, ROWS), BF16),
            pltpu.VMEM((2, ROWS, COLS), F32),
            pltpu.VMEM((2 * LN, 2 * LN), BF16),
            pltpu.VMEM((2 * LN, 2 * LN), BF16),
            pltpu.SemaphoreType.DMA((6,)),
        ],
        name="input_spectrum",
    )


def correlate_kernel(
    wait_small, got_hbm, d1h_hbm, d1l_hbm, twiddle_hbm, d2h_hbm, d2l_hbm, spec_hbm, d1th_hbm, d1tl_hbm,
    column_hbm, turn_hbm, steps_ref, m0, m1, m2, m3, send_hbm,
    got_ref, d1h, d1l, twiddle, d2h, d2l, spec_ref, d1th, d1tl, column_ref, turn_ref,
    send_ref, sems, out_sems,
):
    loads = started(
        sems,
        (got_hbm.at[:, pl.ds(0, CK), :], got_ref),
        (d1h_hbm, d1h), (d1l_hbm, d1l), (twiddle_hbm, twiddle), (d2h_hbm, d2h), (d2l_hbm, d2l),
        (spec_hbm, spec_ref), (d1th_hbm, d1th), (d1tl_hbm, d1tl), (column_hbm, column_ref),
        (turn_hbm, turn_ref),
    )
    wait_small()
    mixes = by_block([m[...] for m in (m0, m1, m2, m3)]).astype(BF16)
    for d in range(RANKS):
        send_ref[d, CK : 2 * CK, :] = mixes
    middle = pl.ds(CK, CK)
    stores = started(out_sems, (send_ref.at[:, middle, :], send_hbm.at[:, middle, :]))
    loads[0].wait()
    g_rows = gather_rows(got_ref)
    g_spec = forward_dft(
        g_rows, True, d1h, d1l, d2h, d2l, twiddle, steps_ref, waiting(loads[1:3]),
        waiting(loads[3:6]),
    )
    waiting(loads[6:7])()
    gr, gi = g_spec[:, :LN], g_spec[:, LN:]
    xr, xi = spec_ref[:, :LN], spec_ref[:, LN:]
    both = jnp.concatenate([xr * gr + xi * gi, xr * gi - xi * gr], 1)
    waiting(loads[7:])()
    kernel_rows = inverse_dft(both, d1th, d1tl, d2h, d2l, twiddle, steps_ref)
    for d in range(RANKS):
        piece = kernel_rows[d * PIECES : (d + 1) * PIECES]
        send_ref[d, :CK, :] = jnp.concatenate(
            [piece[:, q * LN : (q + 1) * LN] for q in range(PER)], 0
        ).astype(BF16)
        if d % 8 == 7:
            part = pl.ds(d - 7, 8), pl.ds(0, CK)
            stores.append(
                pltpu.make_async_copy(
                    send_ref.at[part], send_hbm.at[part], out_sems.at[2 + d // 8]
                )
            )
            stores[-1].start()
    column = split(column_ref[...])
    inner = dot3(split(kernel_rows), column)
    g_inner = dot2(g_rows.astype(BF16), column)
    rr, ri = turn_ref[0], turn_ref[1]
    ids = lax.broadcasted_iota(jnp.int32, (ROWS, LN), 0)
    starts = (ids * COLS).astype(F32)

    def total(values):
        return jnp.sum(values, 0, keepdims=True)

    by_r, by_i = rr * inner, ri * inner
    u, v = total(by_r), total(by_i)
    su, sv = total(starts * by_r), total(starts * by_i)
    gu, gv = total(rr * g_inner), total(ri * g_inner)

    lanes = lax.broadcasted_iota(jnp.int32, (1, LN), 1)
    scalars = jnp.where(lanes == 0, kernel_rows[0:1, 0:1], 0.0) + jnp.where(
        lanes == 1, jnp.sum(total(g_rows), 1, keepdims=True), 0.0
    )
    small = jnp.concatenate([u, v, su, sv, gu, gv, scalars, jnp.zeros((1, LN), F32)], 0)
    high, low = split(jnp.concatenate([small, small], 0))
    upper = lax.broadcasted_iota(jnp.int32, (16, LN), 0) < 8
    packed = jnp.where(upper, high.astype(F32), low.astype(F32)).astype(BF16)
    for d in range(RANKS):
        send_ref[d, 2 * CK :, :] = packed
    stores.append(
        pltpu.make_async_copy(
            send_ref.at[:, pl.ds(2 * CK, 16), :], send_hbm.at[:, pl.ds(2 * CK, 16), :],
            out_sems.at[1],
        )
    )
    stores[-1].start()
    for copy in stores:
        copy.wait()


def correlate(got, spec, tables, column, turns, mixes):
    (d1h, d1l), (d1th, d1tl), (d2h, d2l), twiddle, steps = tables
    return staged(
        correlate_kernel,
        (),
        (got, d1h, d1l, twiddle, d2h, d2l, spec, d1th, d1tl, column, turns),
        (steps, *mixes),
        out_specs=[ANY],
        out_shape=(
            jax.ShapeDtypeStruct((RANKS, SEND3, LN), BF16),
        ),
        scratch_shapes=[
            pltpu.VMEM((RANKS, CK, LN), BF16),
            pltpu.VMEM((2 * ROWS, ROWS), BF16),
            pltpu.VMEM((2 * ROWS, ROWS), BF16),
            pltpu.VMEM((2, ROWS, COLS), F32),
            pltpu.VMEM((2 * LN, 2 * LN), BF16),
            pltpu.VMEM((2 * LN, 2 * LN), BF16),
            pltpu.VMEM((PER * ROWS, 2 * LN), F32),
            pltpu.VMEM((ROWS, 2 * ROWS), BF16),
            pltpu.VMEM((ROWS, 2 * ROWS), BF16),
            pltpu.VMEM((COLS, LN), F32),
            pltpu.VMEM((2, ROWS, LN), F32),
            pltpu.VMEM((RANKS, SEND3, LN), BF16),
            pltpu.SemaphoreType.DMA((11,)),
            pltpu.SemaphoreType.DMA((6,)),
        ],
        name="correlation",
    )


def outputs_kernel(
    wait_small, step_ref, group_ref, got_ref, pull_ref, wide_ref, kernel_ref, damping_ref, frequency_ref, re_ref, im_ref,
    size_ref, skip_ref, mix_ref, table_ref, rows_ref, turned_ref,
):
    mixes = jnp.zeros((CH, LN), F32)
    for c in range(CH):
        rows_ref[c * CK : (c + 1) * CK, :] = got_ref[c, :CK, :].astype(F32)
        mixes = mixes + got_ref[c, CK : 2 * CK, :].astype(F32)
    for i in range(CK):
        kernel_ref[:, i * LN : (i + 1) * LN] = rows_ref[pl.ds(PLACE[i], CH, stride=CK), :]
    for c in range(CH):
        small = got_ref[c, 2 * CK :, :].astype(F32)
        rows_ref[c * 8 : (c + 1) * 8, :] = small[:8] + small[8:]
    wait_small()
    u, v, su, sv, gu, gv, scalars = (rows_ref[pl.ds(k, CH, stride=8), :] for k in range(7))

    def block(row, k):
        moved = pltpu.roll(row, (LN - k * MODES) % LN, 1) if k else row
        return jnp.where(lane_block(row) == 0, moved, 0.0)

    sums = (
        block(u, 0) - block(v, 1),
        block(u, 1) + block(v, 0),
        block(u, 2) - block(v, 3) + block(su, 0) - block(sv, 1),
        block(u, 3) + block(v, 2) + block(su, 1) + block(sv, 0),
    )
    grads = jnp.zeros((CH, LN), F32)
    size = jnp.zeros((CH, LN), F32)
    for k, value in enumerate(sums):
        grads = grads + pull_ref[k] * repeated(value)
        size = size + pull_ref[4 + k] * value
    for k, ref in enumerate((damping_ref, frequency_ref, re_ref, im_ref)):
        ref[...] = grads[:, k * MODES : (k + 1) * MODES]
    g_sum = scalars[:, 1:2]
    back = (
        pull_ref[8] * g_sum
        + pull_ref[9] * (block(gu, 0) - block(gv, 1))
        + pull_ref[10] * (block(gu, 1) + block(gv, 0))
    )
    back_sum = jnp.sum(back, 1, keepdims=True) + wide_ref[1][:, :1] * g_sum
    lanes = lax.broadcasted_iota(jnp.int32, (CH, LN), 1)
    scalars = jnp.where(lanes == 0, jnp.sum(size, 1, keepdims=True), scalars[:, 0:1])
    turned = jnp.concatenate([scalars, jnp.zeros((LN - CH, LN), F32)], 0).T
    size_ref[...] = turned[0:1, :CH]
    skip_ref[...] = turned[1:2, :CH]
    picked = lax.broadcasted_iota(jnp.int32, table_ref.shape, 1) == step_ref[0]
    table_ref[...] = jnp.where(picked, back_sum, 0.0)
    turned_ref[...] = jnp.concatenate([mixes, jnp.zeros((LN - CH, LN), F32)], 0).T
    mix_ref[...] = jnp.concatenate(
        [
            turned_ref[pl.ds(pl.multiple_of((group_ref[0] ^ c) * CH, CH), CH), :][:, :CH]
            for c in range(LN // CH)
        ],
        1,
    )


def outputs(step, group, got, pull, levels, table_len):
    wide = jax.ShapeDtypeStruct((CH, MODES), F32)
    row = jax.ShapeDtypeStruct((1, CH), F32)
    return staged(
        outputs_kernel,
        (step, group),
        (got,),
        (pull, levels),
        out_specs=[VMEM] * 9,
        out_shape=(
            jax.ShapeDtypeStruct((CH, BLOCK), F32),
            wide, wide, wide, wide, row, row,
            jax.ShapeDtypeStruct((CH, LN), F32),
            jax.ShapeDtypeStruct((CH, table_len), F32),
        ),
        scratch_shapes=[pltpu.VMEM((CH * CK, LN), F32), pltpu.VMEM((LN, LN), F32)],
        name="outputs",
        plain_spec=VMEM,
        limit=8,
    )


def exchange(values):
    return lax.all_to_all(values, "tm", split_axis=0, concat_axis=0, tiled=True)


def shards(
    signal,
    cotangent,
    log_step,
    damping,
    frequency,
    coef_re,
    coef_im,
    skip_gain,
    mix_weight,
    embed_table,
    diffusion_step,
):
    me = lax.axis_index("tm").reshape(1)
    group = lax.axis_index("chan").reshape(1)
    tables = dft_tables()

    def swap(values, mask):
        return lax.ppermute(values, "chan", [(i, i ^ mask) for i in range(4)])

    send1, own, sr, si, terms, wide = first(
        diffusion_step, signal, cotangent, mix_weight, log_step[None], (damping, frequency, coef_re, coef_im),
        skip_gain[None], embed_table.T,
    )
    got1 = exchange(send1)
    own, across = lax.optimization_barrier((own, swap(own, 2)))
    parts = (own, swap(own, 1), across, swap(across, 1))
    raw = (log_step[None], damping, frequency, coef_re, coef_im)
    out, far_r, far_i, step_r, step_i, pull = within(send1, terms, wide, raw)
    far = (far_r, far_i)
    steps = (step_r, step_i)
    send2, grad, mix, br, bi = second(
        me, group, parts, out, got1, send1, terms, wide, far, steps, sr, si
    )
    got2 = exchange(send2)
    mixes = [mix] + [swap(mix, m) for m in range(1, 4)]
    spec, column, turns = spectrum(me, got1, mix, wide, terms, tables)
    (send3,) = correlate(got2, spec, tables, column, turns, mixes)
    got3 = exchange(send3)
    (grad_signal,) = signal_grad(
        me, got2, grad, terms, wide, far, steps, br, bi, cotangent, send3
    )
    kernel, g_damping, g_frequency, g_re, g_im, g_size, g_skip, g_mix, g_table = outputs(
        diffusion_step, group, got3, pull, wide, embed_table.shape[0]
    )
    return (
        grad_signal,
        kernel,
        g_size[0],
        g_damping,
        g_frequency,
        g_re,
        g_im,
        g_skip[0],
        g_mix,
        g_table.T,
    )


def solution(mesh):
    placed = (
        P("chan", "tm"),
        P("chan", "tm"),
        P("chan"),
        P("chan", None),
        P("chan", None),
        P("chan", None),
        P("chan", None),
        P("chan"),
        P("chan", None),
        P(None, "chan"),
        P(),
    )
    return jax.shard_map(
        shards,
        mesh=mesh,
        in_specs=placed,
        out_specs=(
            P("chan", "tm"),
            P("chan", "tm"),
            P("chan"),
            P("chan", None),
            P("chan", None),
            P("chan", None),
            P("chan", None),
            P("chan"),
            P("chan", None),
            P(None, "chan"),
        ),
        check_vma=False,
    )
```

```python
import functools

import jax
import jax.numpy as jnp
import numpy as np
from jax import lax
from jax.experimental import pallas as pl
from jax.experimental.pallas import tpu as pltpu
from jax.sharding import PartitionSpec as P

HIGHEST = lax.Precision.HIGHEST
F32 = jnp.float32
BF16 = jnp.bfloat16

CH = 32
MODES = 32
BLOCK = 4096
LN = 128
CK = BLOCK // LN
LANE_CH = LN // MODES
GROUPS = CH // LANE_CH
RANKS = 32
COLS = 512
PER = COLS // LN
ROWS = RANKS * BLOCK // COLS
PIECES = BLOCK // COLS
PLACE = [i % PER * PIECES + i // PER for i in range(CK)]
SEND1 = 64
SEND2 = 64
SEND3 = 80
NT = (((1,), (1,)), ((), ()))
NN = (((1,), (0,)), ((), ()))
GRANT = 63.75
SMEM = pl.BlockSpec(memory_space=pltpu.SMEM)
VMEM = pl.BlockSpec(memory_space=pltpu.VMEM)
ANY = pl.BlockSpec(memory_space=pl.ANY)
HBM = pl.BlockSpec(memory_space=pltpu.HBM)


def expm1_small(x):
    r = 1.0
    for k in (7.0, 6.0, 5.0, 4.0, 3.0, 2.0):
        r = 1.0 + x * r * (1.0 / k)
    return x * r


def mode_terms(step_size, damping, frequency, coef_re, coef_im):
    decay_rate = step_size * damping
    turn_rate = step_size * frequency
    half_sine = jnp.sin(0.5 * turn_rate)
    grow_real = expm1_small(-decay_rate) * jnp.cos(turn_rate) - 2.0 * half_sine * half_sine
    grow_imag = jnp.exp(-decay_rate) * jnp.sin(turn_rate)
    inverse = 1.0 / (damping * damping + frequency * frequency)
    hold_real = (frequency * grow_imag - damping * grow_real) * inverse
    hold_imag = -(frequency * grow_real + damping * grow_imag) * inverse
    weight_real = coef_re * hold_real - coef_im * hold_imag
    weight_imag = coef_re * hold_imag + coef_im * hold_real
    return (decay_rate, turn_rate, weight_real, weight_imag)


def cmul(ar, ai, br, bi):
    return ar * br - ai * bi, ar * bi + ai * br


def split(values):
    high = values.astype(BF16)
    return high, (values - high.astype(F32)).astype(BF16)


def dot(left, right, dims=NN):
    return lax.dot_general(left, right, dims, preferred_element_type=F32)


def dot3(left, right, dims=NN):
    (lh, ll), (rh, rl) = left, right
    (axis,), (other,) = dims[0]
    return dot(
        jnp.concatenate([lh, ll, lh], axis), jnp.concatenate([rh, rh, rl], other), dims
    )


def dot2(left, right, dims=NN):
    (axis,), (other,) = dims[0]
    return dot(jnp.concatenate([left, left], axis), jnp.concatenate(right, other), dims)


def started(sems, *pairs, between=None, ahead=1):
    copies = [pltpu.make_async_copy(a, b, sems.at[k]) for k, (a, b) in enumerate(pairs)]
    for k, copy in enumerate(copies):
        if between is not None and k == ahead:
            between()
        copy.start()
    return copies


def waiting(copies):
    def wait(first=0, last=None):
        for copy in copies[first:last]:
            copy.wait()

    return wait


def staged(
    kernel, scalars, plain, small, *, out_specs, out_shape, scratch_shapes, name,
    plain_spec=HBM, limit=GRANT, eager=None, early=(),
):
    heads, outs = len(scalars) + len(plain), len(out_shape)

    def body(*refs):
        given, rest = refs[:heads], refs[heads:]
        sources, rest = rest[: len(small)], rest[len(small) :]
        results, rest = list(rest[:outs]), rest[outs:]
        held, sems, rest = rest[: len(small)], rest[len(small)], rest[len(small) + 1 :]
        written, out_sems, rest = rest[: len(early)], rest[len(early)], rest[len(early) + 1 :]
        copies = [
            pltpu.make_async_copy(a, b, sems.at[k]) for k, (a, b) in enumerate(zip(sources, held))
        ]
        leaving = {
            k: pltpu.make_async_copy(written[n], results[k], out_sems.at[n])
            for n, k in enumerate(early)
        }
        for n, k in enumerate(early):
            results[k] = written[n]
        gone = set()

        def start(first=0, last=None):
            for copy in copies[first:last]:
                copy.start()

        def store(*which):
            for k in which:
                leaving[k].start()
                gone.add(k)

        wait = waiting(copies)
        wait.start, wait.store = start, store
        start(0, eager)
        kernel(wait, *given, *held, *results, *rest)
        store(*[k for k in early if k not in gone])
        for copy in leaving.values():
            copy.wait()

    return pl.pallas_call(
        body,
        in_specs=[SMEM] * len(scalars) + [plain_spec] * len(plain) + [HBM] * len(small),
        out_specs=[HBM if k in early else spec for k, spec in enumerate(out_specs)],
        out_shape=out_shape,
        scratch_shapes=[pltpu.VMEM(a.shape, a.dtype) for a in small]
        + [pltpu.SemaphoreType.DMA((len(small),))]
        + [pltpu.VMEM(out_shape[k].shape, out_shape[k].dtype) for k in early]
        + [pltpu.SemaphoreType.DMA((max(len(early), 1),))]
        + scratch_shapes,
        compiler_params=pltpu.CompilerParams(vmem_limit_bytes=int(limit * 1024 * 1024)),
        name=name,
    )(*scalars, *plain, *small)


def sin_cos(x):
    y = x * x
    s = 1.0
    for k in (210.0, 156.0, 110.0, 72.0, 42.0, 20.0, 6.0):
        s = 1.0 - y * s * (1.0 / k)
    c = 1.0
    for k in (240.0, 182.0, 132.0, 90.0, 56.0, 30.0, 12.0, 2.0):
        c = 1.0 - y * c * (1.0 / k)
    return x * s, c


def power(decay, turn, steps):
    size = jnp.exp(-decay * steps)
    s, c = sin_cos(turn * steps)
    return size * c, size * s


def doublings(decay, turn):
    return [power(decay, turn, float(k)) for k in (8, 16, 32, 64)]


def rising(decay, turn, doubles, g):
    rows = lax.broadcasted_iota(jnp.int32, (8, LN), 0).astype(F32)
    tr, ti = power(decay[g : g + 1], turn[g : g + 1], rows)
    for zr, zi in doubles:
        nr, ni = cmul(tr, ti, zr[g : g + 1], zi[g : g + 1])
        tr, ti = jnp.concatenate([tr, nr], 0), jnp.concatenate([ti, ni], 0)
    return tr, ti


def falling(decay, turn, doubles, g):
    rows = 7.0 - lax.broadcasted_iota(jnp.int32, (8, LN), 0).astype(F32)
    tr, ti = power(decay[g : g + 1], turn[g : g + 1], rows)
    for zr, zi in doubles:
        nr, ni = cmul(tr, ti, zr[g : g + 1], zi[g : g + 1])
        tr, ti = jnp.concatenate([nr, tr], 0), jnp.concatenate([ni, ti], 0)
    return tr, ti


def lane_channel(shape):
    return lax.broadcasted_iota(jnp.int32, shape, 1) // MODES


def gather_group(products):
    owner = lane_channel((CK, LN))
    real, imag = products[:, :LN], products[:, LN:]
    out_r, out_i = real[:CK], imag[:CK]
    for k in range(1, LANE_CH):
        mine = owner == k
        out_r = jnp.where(mine, real[k * CK : (k + 1) * CK], out_r)
        out_i = jnp.where(mine, imag[k * CK : (k + 1) * CK], out_i)
    return out_r, out_i


def spread_group(state_r, state_i, table):
    owner = lane_channel((CK, LN))
    zero = jnp.zeros((CK, LN), F32)
    left = jnp.concatenate(
        [
            jnp.concatenate(
                [jnp.where(owner == k, state_r, zero), jnp.where(owner == k, -state_i, zero)], 1
            )
            for k in range(LANE_CH)
        ],
        0,
    )
    return dot3(split(left), table, NT)


def scan_states(sr_ref, si_ref, power_r, power_i, order):
    hr = jnp.zeros((GROUPS, LN), F32)
    hi = jnp.zeros((GROUPS, LN), F32)
    for i in order:
        rows = pl.ds(PLACE[i] * GROUPS, GROUPS)
        own_r, own_i = sr_ref[rows, :], si_ref[rows, :]
        sr_ref[rows, :] = hr
        si_ref[rows, :] = hi
        nr, ni = cmul(power_r, power_i, hr, hi)
        hr, hi = nr + own_r, ni + own_i
    return hr, hi


def add_entering(sr_ref, si_ref, sr_in, si_in, step_r, step_i, start, order):
    for k, i in enumerate(order):
        rows = pl.ds(PLACE[i] * GROUPS, GROUPS)
        nr, ni = cmul(step_r[k], step_i[k], *start) if k else start
        sr_ref[rows, :] = sr_in[rows, :] + nr
        si_ref[rows, :] = si_in[rows, :] + ni


def toeplitz(taps_row):
    rows = jnp.broadcast_to(taps_row, (LN, LN))
    turned = pltpu.roll(rows, 0, 1, stride=1, stride_axis=0)
    lag = lax.broadcasted_iota(jnp.int32, (LN, LN), 1) - lax.broadcasted_iota(
        jnp.int32, (LN, LN), 0
    )
    return jnp.where(lag >= 0, turned, 0.0)


def group_taps(terms, table, g):
    real = 2.0 * (terms[2][g : g + 1] * table[0] - terms[3][g : g + 1] * table[1])
    owner = (
        lane_channel((8, LN)) == lax.broadcasted_iota(jnp.int32, (8, LN), 0)
    ).astype(BF16)
    high, low = split(real)
    return dot2(owner, (high, low), NT)


def packed_lanes(ref):
    return jnp.concatenate([ref[pl.ds(k, GROUPS, stride=LANE_CH), :] for k in range(LANE_CH)], 1)


def as_column(row):
    shape = (CH, CH)
    same = lax.broadcasted_iota(jnp.int32, shape, 0) == lax.broadcasted_iota(jnp.int32, shape, 1)
    return jnp.sum(jnp.where(same, row, 0.0), 1, keepdims=True)


def first_kernel(
    wait_small, step_ref, signal_hbm, cot_hbm, mix_hbm, size_ref, damping_ref, frequency_ref, re_ref, im_ref,
    skip_ref, table_ref, send_hbm, own_hbm, sr_ref, si_ref, terms_ref, wide_ref,
    signal_ref, own_ref, send_ref, rows_ref, pack_ref, sems, out_sems,
):
    loads = started(
        sems,
        (signal_hbm, signal_ref),
        (cot_hbm, own_ref.at[:, pl.ds(0, BLOCK)]),
        (mix_hbm, own_ref.at[:, pl.ds(BLOCK, LN)]),
        between=wait_small.start,
    )
    wait_small()
    picked = lax.broadcasted_iota(jnp.int32, table_ref.shape, 1) == step_ref[0]
    embed = jnp.sum(jnp.where(picked, table_ref[...], 0.0), 1, keepdims=True)
    wide_ref[0] = jnp.broadcast_to(embed, (CH, LN))
    wide_ref[1] = jnp.broadcast_to(as_column(skip_ref[...]), (CH, LN))
    pack_ref[...] = jnp.broadcast_to(embed, (CH, MODES))
    embed_lanes = packed_lanes(pack_ref)
    pack_ref[...] = jnp.broadcast_to(as_column(jnp.exp(size_ref[...])), (CH, MODES))
    raw = [packed_lanes(r) for r in (pack_ref, damping_ref, frequency_ref, re_ref, im_ref)]
    terms = mode_terms(*raw)
    for k in range(4):
        terms_ref[k] = terms[k]
    wait_small.store(4, 5)
    decay, turn = terms[0], terms[1]
    doubles = doublings(decay, turn)
    loads[0].wait()
    for i in range(CK):
        rows_ref[pl.ds(PLACE[i], CH, stride=CK), :] = signal_ref[
            :, i * LN : (i + 1) * LN
        ].astype(F32)
    for c in range(CH):
        send_ref[c, :CK, :] = rows_ref[c * CK : (c + 1) * CK, :].astype(BF16)
    loads[1].wait()
    loads[2].wait()
    stores = started(
        out_sems,
        (send_ref.at[:, pl.ds(0, CK), :], send_hbm.at[:, pl.ds(0, CK), :]),
        (own_ref, own_hbm),
    )
    for g in range(GROUPS):
        x = rows_ref[g * LN : (g + 1) * LN, :].astype(BF16)
        fr, fi = falling(decay, turn, doubles, g)
        table = jnp.concatenate([fr, fi], 1)
        th, tl = split(table)
        pr, pi = gather_group(dot2(x, (th, tl)))
        level = embed_lanes[g : g + 1]
        sr_ref[pl.ds(g, CK, stride=GROUPS), :] = pr + level * jnp.sum(fr, 0, keepdims=True)
        si_ref[pl.ds(g, CK, stride=GROUPS), :] = pi + level * jnp.sum(fi, 0, keepdims=True)
    zr, zi = power(decay, turn, float(LN))
    hr, hi = scan_states(sr_ref, si_ref, zr, zi, range(CK))
    wait_small.store(2, 3)
    packed = packed_states(hr, hi)
    for d in range(RANKS):
        send_ref[d, CK:, :] = packed
    last = pltpu.make_async_copy(
        send_ref.at[:, pl.ds(CK, CK), :], send_hbm.at[:, pl.ds(CK, CK), :], out_sems.at[2]
    )
    last.start()
    for copy in stores + [last]:
        copy.wait()


def packed_states(hr, hi):
    high, low = split(jnp.concatenate([hr, hi], 0))
    return jnp.concatenate([high, low], 0)


def unpacked_states(packed):
    packed = packed.astype(F32)
    values = packed[: 2 * GROUPS] + packed[2 * GROUPS :]
    return values[:GROUPS], values[GROUPS:]


def first(step, signal, cotangent, mix_weight, sizes, params, skip, table):
    return staged(
        first_kernel,
        (step,),
        (signal, cotangent, mix_weight),
        (sizes, *params, skip, table),
        out_specs=[ANY] * 2 + [VMEM] * 4,
        out_shape=(
            jax.ShapeDtypeStruct((RANKS, SEND1, LN), BF16),
            jax.ShapeDtypeStruct((CH, BLOCK + LN), BF16),
            jax.ShapeDtypeStruct((CK * GROUPS, LN), F32),
            jax.ShapeDtypeStruct((CK * GROUPS, LN), F32),
            jax.ShapeDtypeStruct((4, GROUPS, LN), F32),
            jax.ShapeDtypeStruct((2, CH, LN), F32),
        ),
        scratch_shapes=[
            pltpu.VMEM((CH, BLOCK), BF16),
            pltpu.VMEM((CH, BLOCK + LN), BF16),
            pltpu.VMEM((RANKS, SEND1, LN), BF16),
            pltpu.VMEM((CH * CK, LN), F32),
            pltpu.VMEM((CH, MODES), F32),
            pltpu.SemaphoreType.DMA((3,)),
            pltpu.SemaphoreType.DMA((3,)),
        ],
        name="block_states",
        eager=0,
        early=(2, 3, 4, 5),
    )


def wide_sin_cos(x):
    turns = jnp.floor(x * np.float32(1.0 / (2.0 * np.pi)) + 0.5)
    x = (x - turns * np.float32(6.28125)) - turns * np.float32(2.0 * np.pi - 6.28125)
    s, c = sin_cos(0.5 * x)
    return 2.0 * s * c, 1.0 - 2.0 * s * s


def far_power(decay, turn, blocks):
    size = jnp.exp(-decay * (BLOCK * blocks))
    s, c = wide_sin_cos(turn * (BLOCK * blocks))
    return size * c, size * s


def pull_table(size_ref, damping_ref, frequency_ref, re_ref, im_ref, pull_ref):
    def tiled(values):
        return jnp.concatenate([values] * LANE_CH, 1)

    size = jnp.broadcast_to(as_column(jnp.exp(size_ref[...])), (CH, LN))
    raw = [size] + [tiled(r[...]) for r in (damping_ref, frequency_ref, re_ref, im_ref)]
    (d, th, mr, mi), pull = jax.vjp(mode_terms, *raw)
    zero = jnp.zeros((CH, LN), F32)
    pulled = [
        pull((zero, zero, zero + 2.0, zero)),
        pull((zero, zero, zero, zero - 2.0)),
        pull((-2.0 * mr, -2.0 * mi, zero, zero)),
        pull((2.0 * mi, -2.0 * mr, zero, zero)),
    ]
    inverse = 1.0 / (raw[1] * raw[1] + raw[2] * raw[2])
    qr, qi = cmul(raw[3], raw[4], raw[1] * inverse, raw[2] * inverse)
    one_r, one_i = power(d, th, 1.0)
    er, ei = cmul(qr, qi, one_r, one_i)
    first_lanes = lane_block(zero) == 0
    for k, p in enumerate(pulled):
        pull_ref[k] = by_block(p[1:])
        pull_ref[4 + k] = jnp.where(first_lanes, p[0] * raw[0], 0.0)
    for k, value in enumerate((2.0 * qr, -2.0 * er, 2.0 * ei)):
        pull_ref[8 + k] = jnp.where(first_lanes, value, 0.0)


def within_kernel(
    wait_small, x_hbm, terms_ref, wide_ref, size_ref, damping_ref, frequency_ref, re_ref, im_ref,
    out_ref, far_r, far_i, step_r, step_i, pull_ref, x_ref, sems,
):
    loads = started(sems, (x_hbm.at[:, pl.ds(0, CK), :], x_ref))
    wait_small()
    pull_table(size_ref, damping_ref, frequency_ref, re_ref, im_ref, pull_ref)
    terms = terms_ref[0], terms_ref[1], terms_ref[2], terms_ref[3]
    decay, turn = terms[0], terms[1]
    near = [far_power(decay, turn, float(b)) for b in range(4)]
    for a in range(RANKS // 4):
        base = far_power(decay, turn, float(4 * a))
        for b in range(4):
            pr, pi = cmul(base[0], base[1], near[b][0], near[b][1]) if a and b else (
                base if a else near[b]
            )
            far_r[4 * a + b] = pr
            far_i[4 * a + b] = pi
    near = [far_power(decay, turn, b * LN / BLOCK) for b in range(4)]
    for a in range(CK // 4):
        base = far_power(decay, turn, 4 * a * LN / BLOCK)
        for b in range(4):
            step_r[4 * a + b], step_i[4 * a + b] = cmul(*base, *near[b])
    doubles = doublings(decay, turn)
    loads[0].wait()
    for g in range(GROUPS):
        taps = group_taps(terms, rising(decay, turn, doubles, g), g)
        for k in range(LANE_CH):
            c = g * LANE_CH + k
            matrix = toeplitz(taps[k : k + 1])
            high, low = split(matrix)
            x = x_ref[c]
            level = wide_ref[0, c : c + 1, :]
            out_ref[c * CK : (c + 1) * CK, :] = (
                dot2(x, (high, low)) + level * jnp.sum(matrix, 0, keepdims=True)
            )


def within(send, terms, wide, raw):
    return staged(
        within_kernel,
        (),
        (send,),
        (terms, wide, *raw),
        out_specs=[VMEM] * 6,
        out_shape=(
            jax.ShapeDtypeStruct((CH * CK, LN), F32),
            jax.ShapeDtypeStruct((RANKS, GROUPS, LN), F32),
            jax.ShapeDtypeStruct((RANKS, GROUPS, LN), F32),
            jax.ShapeDtypeStruct((CK, GROUPS, LN), F32),
            jax.ShapeDtypeStruct((CK, GROUPS, LN), F32),
            jax.ShapeDtypeStruct((11, CH, LN), F32),
        ),
        scratch_shapes=[pltpu.VMEM((CH, CK, LN), BF16), pltpu.SemaphoreType.DMA((1,))],
        name="within_chunks",
    )


def mixed_back(group, cot_ref, act_ref):
    mine = lax.broadcasted_iota(jnp.int32, (CH, LN), 1) == group * CH + lax.broadcasted_iota(
        jnp.int32, (CH, LN), 0
    )
    weights = dot(mine.astype(BF16), cot_ref[:, BLOCK:], NT).astype(BF16)
    for i in range(CK):
        act_ref[pl.ds(PLACE[i], CH, stride=CK), :] = dot(
            weights, cot_ref[:, i * LN : (i + 1) * LN]
        )


def gelu_both(x):
    scale = np.float32(np.sqrt(2.0 / np.pi))
    square = x * x
    t = jnp.tanh(scale * (x + 0.044715 * (square * x)))
    half = 0.5 * (1.0 + t)
    slope = half + 0.5 * x * (1.0 - t * t) * (scale * (1.0 + (3.0 * 0.044715) * square))
    return x * half, slope


def entering(states, table_r, table_i, distance):
    hr = jnp.zeros((GROUPS, LN), F32)
    hi = jnp.zeros((GROUPS, LN), F32)
    for d in range(RANKS):
        steps = distance(d)
        sr, si = states(d)
        at = jnp.maximum(steps, 0)
        nr, ni = cmul(table_r[at], table_i[at], sr, si)
        hr = jnp.where(steps >= 0, hr + nr, hr)
        hi = jnp.where(steps >= 0, hi + ni, hi)
    return hr, hi


def second_kernel(
    wait_small, me_ref, group_ref, c0h, c1h, c2h, c3h, out_hbm, got_hbm, x_hbm, terms_ref, wide_ref, far_r,
    far_i, step_r, step_i, sr_in, si_in, send_hbm, grad_hbm, mix_ref, sr_ref, si_ref,
    cot_ref, flat_ref, out_ref, got_ref, x_ref, act_ref, activation_ref, send_ref, grad_ref, table_ref, sems, out_sems,
):
    loads = started(
        sems,
        *[(c, cot_ref.at[pl.ds(m * CH, CH), :]) for m, c in enumerate((c0h, c1h, c2h, c3h))],
        (got_hbm.at[:, pl.ds(CK, CK), :], got_ref),
        (x_hbm.at[:, pl.ds(0, CK), :], x_ref),
        (out_hbm, out_ref),
        between=lambda: wait_small.start(1),
        ahead=5,
    )
    wait_small(0, 1)
    me = me_ref[0]
    terms = terms_ref[0], terms_ref[1], terms_ref[2], terms_ref[3]
    decay, turn = terms[0], terms[1]
    doubles = doublings(decay, turn)
    zr, zi = power(decay, turn, float(LN))
    one_r, one_i = power(decay, turn, 1.0)
    ur, ui = cmul(2.0 * terms[2], 2.0 * terms[3], one_r, one_i)
    for g in range(GROUPS):
        er, ei = rising(decay, turn, doubles, g)
        wr, wi = cmul(er, ei, ur[g : g + 1], ui[g : g + 1])
        table_ref[4 * g], table_ref[4 * g + 1] = split(jnp.concatenate([er, ei], 1))
        table_ref[4 * g + 2], table_ref[4 * g + 3] = split(jnp.concatenate([wr, wi], 1))
    for copy in loads[:4]:
        copy.wait()
    mixed_back(group_ref[0], cot_ref, act_ref)
    wait_small(1)
    loads[4].wait()
    start = entering(lambda d: unpacked_states(got_ref[d]), far_r, far_i, lambda d: me - 1 - d)
    add_entering(sr_ref, si_ref, sr_in, si_in, step_r, step_i, start, range(CK))
    for copy in loads[5:]:
        copy.wait()
    stores = []
    for g in range(GROUPS):
        every = pl.ds(g, CK, stride=GROUPS)
        inter = spread_group(
            sr_ref[every, :], si_ref[every, :], (table_ref[4 * g + 2], table_ref[4 * g + 3])
        )
        left = []
        for k in range(LANE_CH):
            c = g * LANE_CH + k
            rows = slice(c * CK, (c + 1) * CK)
            x = x_ref[c].astype(F32) + wide_ref[0, c : c + 1, :]
            mixed = out_ref[rows, :] + inter[k * CK : (k + 1) * CK] + wide_ref[1, c : c + 1, :] * x
            act, slope = gelu_both(mixed)
            activation_ref[rows, :] = act
            grad = act_ref[rows, :] * slope
            grad_ref[rows, :] = grad
            send_ref[c, :CK, :] = grad.astype(BF16)
            left.append(grad)
        stores.append(
            pltpu.make_async_copy(
                send_ref.at[pl.ds(g * LANE_CH, LANE_CH), pl.ds(0, CK), :],
                send_hbm.at[pl.ds(g * LANE_CH, LANE_CH), pl.ds(0, CK), :],
                out_sems.at[g],
            )
        )
        stores[-1].start()
        mine = pl.ds(g * LN, LN)
        stores.append(
            pltpu.make_async_copy(
                grad_ref.at[mine, :], grad_hbm.at[mine, :], out_sems.at[GROUPS + 1 + g]
            )
        )
        stores[-1].start()
        products = dot3(split(jnp.concatenate(left, 0)), (table_ref[4 * g], table_ref[4 * g + 1]))
        pr, pi = gather_group(products)
        sr_ref[every, :] = pr
        si_ref[every, :] = pi
    hr, hi = scan_states(sr_ref, si_ref, zr, zi, range(CK - 1, -1, -1))
    wait_small.store(3, 4)
    packed = packed_states(hr, hi)
    for d in range(RANKS):
        send_ref[d, CK:, :] = packed
    stores.append(
        pltpu.make_async_copy(
            send_ref.at[:, pl.ds(CK, CK), :], send_hbm.at[:, pl.ds(CK, CK), :],
            out_sems.at[GROUPS],
        )
    )
    stores[-1].start()
    for i in range(CK):
        flat_ref[:, i * LN : (i + 1) * LN] = activation_ref[
            pl.ds(PLACE[i], CH, stride=CK), :
        ].astype(BF16)
    mix_ref[...] = dot(flat_ref[...], cot_ref[:, :BLOCK], NT)
    wait_small.store(2)
    for copy in stores:
        copy.wait()


def second(me, group, parts, out, got, send, terms, wide, far, steps, sr, si):
    return staged(
        second_kernel,
        (me, group),
        (*parts, out, got, send),
        (terms, wide, far[0], far[1], steps[0], steps[1], sr, si),
        out_specs=[ANY] * 2 + [VMEM] * 3,
        out_shape=(
            jax.ShapeDtypeStruct((RANKS, SEND2, LN), BF16),
            jax.ShapeDtypeStruct((CH * CK, LN), F32),
            jax.ShapeDtypeStruct((CH, LN), F32),
            jax.ShapeDtypeStruct((CK * GROUPS, LN), F32),
            jax.ShapeDtypeStruct((CK * GROUPS, LN), F32),
        ),
        scratch_shapes=[
            pltpu.VMEM((LN, BLOCK + LN), BF16),
            pltpu.VMEM((CH, BLOCK), BF16),
            pltpu.VMEM((CH * CK, LN), F32),
            pltpu.VMEM((RANKS, CK, LN), BF16),
            pltpu.VMEM((CH, CK, LN), BF16),
            pltpu.VMEM((CH * CK, LN), F32),
            pltpu.VMEM((CH * CK, LN), F32),
            pltpu.VMEM((RANKS, SEND2, LN), BF16),
            pltpu.VMEM((CH * CK, LN), F32),
            pltpu.VMEM((4 * GROUPS, LN, 2 * LN), BF16),
            pltpu.SemaphoreType.DMA((7,)),
            pltpu.SemaphoreType.DMA((2 * GROUPS + 1,)),
        ],
        name="activation_and_states",
        eager=1,
        early=(2, 3, 4),
    )


def signal_kernel(
    wait_small, me_ref, got_hbm, send_hbm, cot_hbm, after_hbm, terms_ref, wide_ref, far_r, far_i,
    step_r, step_i, sr_in, si_in, out_ref, sr_ref, si_ref, rows_ref, got_ref, send_ref, cot_ref, sems,
):
    loads = started(
        sems,
        (got_hbm.at[:, pl.ds(CK, CK), :], got_ref),
        (send_hbm, send_ref),
        (cot_hbm, cot_ref),
    )
    wait_small()
    me = me_ref[0]
    terms = terms_ref[0], terms_ref[1], terms_ref[2], terms_ref[3]
    decay, turn = terms[0], terms[1]
    doubles = doublings(decay, turn)
    one_r, one_i = power(decay, turn, 1.0)
    ur, ui = cmul(2.0 * terms[2], 2.0 * terms[3], one_r, one_i)
    loads[0].wait()
    start = entering(lambda d: unpacked_states(got_ref[d]), far_r, far_i, lambda d: d - me - 1)
    add_entering(sr_ref, si_ref, sr_in, si_in, step_r, step_i, start, range(CK - 1, -1, -1))
    for copy in loads[1:]:
        copy.wait()
    for g in range(GROUPS):
        every = pl.ds(g, CK, stride=GROUPS)
        fr, fi = falling(decay, turn, doubles, g)
        wr, wi = cmul(fr, fi, ur[g : g + 1], ui[g : g + 1])
        inter = spread_group(sr_ref[every, :], si_ref[every, :], split(jnp.concatenate([wr, wi], 1)))
        taps = group_taps(terms, rising(decay, turn, doubles, g), g)
        for k in range(LANE_CH):
            c = g * LANE_CH + k
            grad = send_ref[c * CK : (c + 1) * CK, :]
            rows_ref[c * CK : (c + 1) * CK, :] = (
                dot3(split(grad), split(toeplitz(taps[k : k + 1])), NT)
                + inter[k * CK : (k + 1) * CK]
                + wide_ref[1, c : c + 1, :] * grad
            )
    for i in range(CK):
        cols = slice(i * LN, (i + 1) * LN)
        out_ref[:, cols] = (
            cot_ref[:, cols].astype(F32) + rows_ref[pl.ds(PLACE[i], CH, stride=CK), :]
        ).astype(BF16)


def signal_grad(me, got, send, terms, wide, far, steps, sr, si, cotangent, after):
    return staged(
        signal_kernel,
        (me,),
        (got, send, cotangent, after),
        (terms, wide, far[0], far[1], steps[0], steps[1], sr, si),
        out_specs=[VMEM],
        out_shape=(
            jax.ShapeDtypeStruct((CH, BLOCK), BF16),
        ),
        scratch_shapes=[
            pltpu.VMEM((CK * GROUPS, LN), F32),
            pltpu.VMEM((CK * GROUPS, LN), F32),
            pltpu.VMEM((CH * CK, LN), F32),
            pltpu.VMEM((RANKS, CK, LN), BF16),
            pltpu.VMEM((CH * CK, LN), F32),
            pltpu.VMEM((CH, BLOCK), BF16),
            pltpu.SemaphoreType.DMA((3,)),
        ],
        name="signal_gradient",
        limit=62.5,
    )


def dft_tables():
    full_len = RANKS * BLOCK
    row = np.arange(ROWS)
    first_ids = np.arange(ROWS)
    column = np.arange(COLS)
    angle1 = (
        2.0 * np.pi * (((4 * first_ids[:, None] + 1) * row[None, :]) % (4 * ROWS)) / (4 * ROWS)
    )
    angle_t = 2.0 * np.pi * ((4 * first_ids[:, None] + 1) * column[None, :]) / (4 * full_len)
    lane = np.arange(LN)
    angle2 = 2.0 * np.pi * ((lane[:, None] * lane[None, :]) % LN) / LN
    angle_p = 2.0 * np.pi * np.arange(PER)[:, None] * lane[None, :] / COLS

    def halves(values):
        values = values.astype(np.float32)
        high = values.astype(BF16)
        return high, (values - high.astype(np.float32)).astype(BF16)

    stage1 = np.concatenate([np.cos(angle1), -np.sin(angle1)], 0)
    cos2, sin2 = np.cos(angle2), np.sin(angle2)
    stage2 = np.concatenate(
        [np.concatenate([cos2, -sin2], 1), np.concatenate([sin2, cos2], 1)], 0
    )
    twiddle = np.stack([np.cos(angle_t), np.sin(angle_t)]).astype(np.float32)
    steps = np.concatenate([np.cos(angle_p), np.sin(angle_p)], 0).astype(np.float32)
    return halves(stage1), halves(stage1.T / full_len), halves(stage2), twiddle, steps


def gather_rows(ref):
    result = []
    for d in range(RANKS):
        block = ref[d].astype(F32)
        result.append(
            jnp.concatenate([block[q * PIECES : (q + 1) * PIECES] for q in range(PER)], 1)
        )
    return jnp.concatenate(result, 0)


def butterfly(parts, sign):
    (r0, i0), (r1, i1), (r2, i2), (r3, i3) = parts
    sr, si, dr, di = r0 + r2, i0 + i2, r0 - r2, i0 - i2
    tr, ti, er, ei = r1 + r3, i1 + i3, r1 - r3, i1 - i3
    if sign > 0:
        er, ei = -er, -ei
    return (sr + tr, si + ti), (dr + ei, di - er), (sr - tr, si - ti), (dr - ei, di + er)


def forward_dft(rows, exact, d1h, d1l, d2h, d2l, twiddle, steps, wait1, wait2):
    xh, xl = split(rows)
    wait1()
    if exact:
        a = dot(jnp.concatenate([d1h[...], d1l[...]], 1), jnp.concatenate([xh, xh], 0))
    else:
        a = dot3((d1h[...], d1l[...]), (xh, xl))
    wait2()
    parts = []
    for q in range(PER):
        cols = slice(q * LN, (q + 1) * LN)
        parts.append(cmul(a[:ROWS, cols], a[ROWS:, cols], twiddle[0, :, cols], -twiddle[1, :, cols]))
    out = []
    for p, (ur, ui) in enumerate(butterfly(parts, -1)):
        if p:
            ur, ui = cmul(ur, ui, steps[p : p + 1, :], -steps[PER + p : PER + p + 1, :])
        out.append(jnp.concatenate([ur, ui], 1))
    return dot3(split(jnp.concatenate(out, 0)), (d2h[...], d2l[...]))


def inverse_dft(spec, d1th, d1tl, d2h, d2l, twiddle, steps):
    v = dot3(split(spec), (d2h[...], d2l[...]), NT)
    parts = []
    for p in range(PER):
        vr, vi = v[p * ROWS : (p + 1) * ROWS, :LN], v[p * ROWS : (p + 1) * ROWS, LN:]
        if p:
            vr, vi = cmul(vr, vi, steps[p : p + 1, :], steps[PER + p : PER + p + 1, :])
        parts.append((vr, vi))
    real, imag = [], []
    for q, (br, bi) in enumerate(butterfly(parts, 1)):
        cols = slice(q * LN, (q + 1) * LN)
        br, bi = cmul(br, bi, twiddle[0, :, cols], twiddle[1, :, cols])
        real.append(br)
        imag.append(bi)
    bh, bl = split(
        jnp.concatenate([jnp.concatenate(real, 1), jnp.concatenate(imag, 1)], 0)
    )
    return dot3((d1th[...], d1tl[...]), (bh, bl))


def lane_block(row):
    return lax.broadcasted_iota(jnp.int32, row.shape, 1) // MODES


def repeated(row):
    row = jnp.where(lane_block(row) == 0, row, 0.0)
    total = row
    for m in range(1, LANE_CH):
        total = total + pltpu.roll(row, m * MODES, 1)
    return total


def by_block(rows):
    result = rows[0]
    for m in range(1, LANE_CH):
        result = jnp.where(lane_block(result) == m, rows[m], result)
    return result


def spectrum_kernel(
    wait_small, me_ref, got_hbm, d1h_hbm, d1l_hbm, twiddle_hbm, d2h_hbm, d2l_hbm, after_hbm,
    steps_ref, wide_ref, terms_ref, spec_ref, column_ref, turn_ref,
    got_ref, d1h, d1l, twiddle, d2h, d2l, sems,
):
    loads = started(
        sems,
        (got_hbm.at[:, pl.ds(0, CK), :], got_ref),
        (d1h_hbm, d1h), (d1l_hbm, d1l), (twiddle_hbm, twiddle), (d2h_hbm, d2h), (d2l_hbm, d2l),
    )
    wait_small()
    me = me_ref[0]
    embed = wide_ref[0, pl.ds(me, 1), :]
    loads[0].wait()
    rows = gather_rows(got_ref) + jnp.concatenate([embed] * PER, 1)
    spec_ref[...] = forward_dft(
        rows, False, d1h, d1l, d2h, d2l, twiddle, steps_ref, waiting(loads[1:3]),
        waiting(loads[3:6]),
    )

    at, shift = me // LANE_CH, (me % LANE_CH) * MODES

    def own(k):
        row = jnp.broadcast_to(terms_ref[k, pl.ds(at, 1), :], (8, LN))
        return repeated(pltpu.roll(row, (LN - shift) % LN, 1)[:1])

    d, th = own(0), own(1)
    steps = lax.broadcasted_iota(jnp.int32, (8, LN), 0).astype(F32)
    cr, ci = power(d, th, steps)
    for k in (8, 16, 32, 64, 128, 256):
        zr, zi = far_power(d, th, float(k) / BLOCK)
        nr, ni = cmul(cr, ci, zr, zi)
        cr, ci = jnp.concatenate([cr, nr], 0), jnp.concatenate([ci, ni], 0)
    col = lax.broadcasted_iota(jnp.int32, (COLS, LN), 0).astype(F32)
    block = lane_block(col)
    table = jnp.where(block % 2 == 0, cr, ci)
    column_ref[...] = jnp.where(block < 2, table, table * col)
    ranks = lax.broadcasted_iota(jnp.int32, (RANKS, LN), 0).astype(F32)
    br, bi = far_power(d, th, ranks)
    pieces = lax.broadcasted_iota(jnp.int32, (PIECES, LN), 0).astype(F32) * (COLS / BLOCK)
    pr, pi = far_power(d, th, pieces)
    for k in range(RANKS):
        rows = slice(k * PIECES, (k + 1) * PIECES)
        turn_ref[0, rows, :], turn_ref[1, rows, :] = cmul(
            pr, pi, br[k : k + 1], bi[k : k + 1]
        )


def spectrum(me, got, after, wide, terms, tables):
    (d1h, d1l), unused, (d2h, d2l), twiddle, steps = tables
    return staged(
        spectrum_kernel,
        (me,),
        (got, d1h, d1l, twiddle, d2h, d2l, after),
        (steps, wide, terms),
        out_specs=[VMEM] * 3,
        out_shape=(
            jax.ShapeDtypeStruct((PER * ROWS, 2 * LN), F32),
            jax.ShapeDtypeStruct((COLS, LN), F32),
            jax.ShapeDtypeStruct((2, ROWS, LN), F32),
        ),
        scratch_shapes=[
            pltpu.VMEM((RANKS, CK, LN), BF16),
            pltpu.VMEM((2 * ROWS, ROWS), BF16),
            pltpu.VMEM((2 * ROWS, ROWS), BF16),
            pltpu.VMEM((2, ROWS, COLS), F32),
            pltpu.VMEM((2 * LN, 2 * LN), BF16),
            pltpu.VMEM((2 * LN, 2 * LN), BF16),
            pltpu.SemaphoreType.DMA((6,)),
        ],
        name="input_spectrum",
    )


def correlate_kernel(
    wait_small, got_hbm, d1h_hbm, d1l_hbm, twiddle_hbm, d2h_hbm, d2l_hbm, spec_hbm, d1th_hbm, d1tl_hbm,
    column_hbm, turn_hbm, steps_ref, m0, m1, m2, m3, send_hbm,
    got_ref, d1h, d1l, twiddle, d2h, d2l, spec_ref, d1th, d1tl, column_ref, turn_ref,
    send_ref, sems, out_sems,
):
    loads = started(
        sems,
        (got_hbm.at[:, pl.ds(0, CK), :], got_ref),
        (d1h_hbm, d1h), (d1l_hbm, d1l), (twiddle_hbm, twiddle), (d2h_hbm, d2h), (d2l_hbm, d2l),
        (spec_hbm, spec_ref), (d1th_hbm, d1th), (d1tl_hbm, d1tl), (column_hbm, column_ref),
        (turn_hbm, turn_ref),
    )
    wait_small()
    mixes = by_block([m[...] for m in (m0, m1, m2, m3)]).astype(BF16)
    for d in range(RANKS):
        send_ref[d, CK : 2 * CK, :] = mixes
    middle = pl.ds(CK, CK)
    stores = started(out_sems, (send_ref.at[:, middle, :], send_hbm.at[:, middle, :]))
    loads[0].wait()
    g_rows = gather_rows(got_ref)
    g_spec = forward_dft(
        g_rows, True, d1h, d1l, d2h, d2l, twiddle, steps_ref, waiting(loads[1:3]),
        waiting(loads[3:6]),
    )
    waiting(loads[6:7])()
    gr, gi = g_spec[:, :LN], g_spec[:, LN:]
    xr, xi = spec_ref[:, :LN], spec_ref[:, LN:]
    both = jnp.concatenate([xr * gr + xi * gi, xr * gi - xi * gr], 1)
    waiting(loads[7:])()
    kernel_rows = inverse_dft(both, d1th, d1tl, d2h, d2l, twiddle, steps_ref)
    for d in range(RANKS):
        piece = kernel_rows[d * PIECES : (d + 1) * PIECES]
        send_ref[d, :CK, :] = jnp.concatenate(
            [piece[:, q * LN : (q + 1) * LN] for q in range(PER)], 0
        ).astype(BF16)
        if d % 8 == 7:
            part = pl.ds(d - 7, 8), pl.ds(0, CK)
            stores.append(
                pltpu.make_async_copy(
                    send_ref.at[part], send_hbm.at[part], out_sems.at[2 + d // 8]
                )
            )
            stores[-1].start()
    column = split(column_ref[...])
    inner = dot3(split(kernel_rows), column)
    g_inner = dot2(g_rows.astype(BF16), column)
    rr, ri = turn_ref[0], turn_ref[1]
    ids = lax.broadcasted_iota(jnp.int32, (ROWS, LN), 0)
    starts = (ids * COLS).astype(F32)

    def total(values):
        return jnp.sum(values, 0, keepdims=True)

    by_r, by_i = rr * inner, ri * inner
    u, v = total(by_r), total(by_i)
    su, sv = total(starts * by_r), total(starts * by_i)
    gu, gv = total(rr * g_inner), total(ri * g_inner)

    lanes = lax.broadcasted_iota(jnp.int32, (1, LN), 1)
    scalars = jnp.where(lanes == 0, kernel_rows[0:1, 0:1], 0.0) + jnp.where(
        lanes == 1, jnp.sum(total(g_rows), 1, keepdims=True), 0.0
    )
    small = jnp.concatenate([u, v, su, sv, gu, gv, scalars, jnp.zeros((1, LN), F32)], 0)
    high, low = split(jnp.concatenate([small, small], 0))
    upper = lax.broadcasted_iota(jnp.int32, (16, LN), 0) < 8
    packed = jnp.where(upper, high.astype(F32), low.astype(F32)).astype(BF16)
    for d in range(RANKS):
        send_ref[d, 2 * CK :, :] = packed
    stores.append(
        pltpu.make_async_copy(
            send_ref.at[:, pl.ds(2 * CK, 16), :], send_hbm.at[:, pl.ds(2 * CK, 16), :],
            out_sems.at[1],
        )
    )
    stores[-1].start()
    for copy in stores:
        copy.wait()


def correlate(got, spec, tables, column, turns, mixes):
    (d1h, d1l), (d1th, d1tl), (d2h, d2l), twiddle, steps = tables
    return staged(
        correlate_kernel,
        (),
        (got, d1h, d1l, twiddle, d2h, d2l, spec, d1th, d1tl, column, turns),
        (steps, *mixes),
        out_specs=[ANY],
        out_shape=(
            jax.ShapeDtypeStruct((RANKS, SEND3, LN), BF16),
        ),
        scratch_shapes=[
            pltpu.VMEM((RANKS, CK, LN), BF16),
            pltpu.VMEM((2 * ROWS, ROWS), BF16),
            pltpu.VMEM((2 * ROWS, ROWS), BF16),
            pltpu.VMEM((2, ROWS, COLS), F32),
            pltpu.VMEM((2 * LN, 2 * LN), BF16),
            pltpu.VMEM((2 * LN, 2 * LN), BF16),
            pltpu.VMEM((PER * ROWS, 2 * LN), F32),
            pltpu.VMEM((ROWS, 2 * ROWS), BF16),
            pltpu.VMEM((ROWS, 2 * ROWS), BF16),
            pltpu.VMEM((COLS, LN), F32),
            pltpu.VMEM((2, ROWS, LN), F32),
            pltpu.VMEM((RANKS, SEND3, LN), BF16),
            pltpu.SemaphoreType.DMA((11,)),
            pltpu.SemaphoreType.DMA((6,)),
        ],
        name="correlation",
    )


def outputs_kernel(
    wait_small, step_ref, group_ref, got_ref, pull_ref, wide_ref, kernel_ref, damping_ref, frequency_ref, re_ref, im_ref,
    size_ref, skip_ref, mix_ref, table_ref, rows_ref, turned_ref,
):
    mixes = jnp.zeros((CH, LN), F32)
    for c in range(CH):
        rows_ref[c * CK : (c + 1) * CK, :] = got_ref[c, :CK, :].astype(F32)
        mixes = mixes + got_ref[c, CK : 2 * CK, :].astype(F32)
    for i in range(CK):
        kernel_ref[:, i * LN : (i + 1) * LN] = rows_ref[pl.ds(PLACE[i], CH, stride=CK), :]
    for c in range(CH):
        small = got_ref[c, 2 * CK :, :].astype(F32)
        rows_ref[c * 8 : (c + 1) * 8, :] = small[:8] + small[8:]
    wait_small()
    u, v, su, sv, gu, gv, scalars = (rows_ref[pl.ds(k, CH, stride=8), :] for k in range(7))

    def block(row, k):
        moved = pltpu.roll(row, (LN - k * MODES) % LN, 1) if k else row
        return jnp.where(lane_block(row) == 0, moved, 0.0)

    sums = (
        block(u, 0) - block(v, 1),
        block(u, 1) + block(v, 0),
        block(u, 2) - block(v, 3) + block(su, 0) - block(sv, 1),
        block(u, 3) + block(v, 2) + block(su, 1) + block(sv, 0),
    )
    grads = jnp.zeros((CH, LN), F32)
    size = jnp.zeros((CH, LN), F32)
    for k, value in enumerate(sums):
        grads = grads + pull_ref[k] * repeated(value)
        size = size + pull_ref[4 + k] * value
    for k, ref in enumerate((damping_ref, frequency_ref, re_ref, im_ref)):
        ref[...] = grads[:, k * MODES : (k + 1) * MODES]
    g_sum = scalars[:, 1:2]
    back = (
        pull_ref[8] * g_sum
        + pull_ref[9] * (block(gu, 0) - block(gv, 1))
        + pull_ref[10] * (block(gu, 1) + block(gv, 0))
    )
    back_sum = jnp.sum(back, 1, keepdims=True) + wide_ref[1][:, :1] * g_sum
    lanes = lax.broadcasted_iota(jnp.int32, (CH, LN), 1)
    scalars = jnp.where(lanes == 0, jnp.sum(size, 1, keepdims=True), scalars[:, 0:1])
    turned = jnp.concatenate([scalars, jnp.zeros((LN - CH, LN), F32)], 0).T
    size_ref[...] = turned[0:1, :CH]
    skip_ref[...] = turned[1:2, :CH]
    picked = lax.broadcasted_iota(jnp.int32, table_ref.shape, 1) == step_ref[0]
    table_ref[...] = jnp.where(picked, back_sum, 0.0)
    turned_ref[...] = jnp.concatenate([mixes, jnp.zeros((LN - CH, LN), F32)], 0).T
    mix_ref[...] = jnp.concatenate(
        [
            turned_ref[pl.ds(pl.multiple_of((group_ref[0] ^ c) * CH, CH), CH), :][:, :CH]
            for c in range(LN // CH)
        ],
        1,
    )


def outputs(step, group, got, pull, levels, table_len):
    wide = jax.ShapeDtypeStruct((CH, MODES), F32)
    row = jax.ShapeDtypeStruct((1, CH), F32)
    return staged(
        outputs_kernel,
        (step, group),
        (got,),
        (pull, levels),
        out_specs=[VMEM] * 9,
        out_shape=(
            jax.ShapeDtypeStruct((CH, BLOCK), F32),
            wide, wide, wide, wide, row, row,
            jax.ShapeDtypeStruct((CH, LN), F32),
            jax.ShapeDtypeStruct((CH, table_len), F32),
        ),
        scratch_shapes=[pltpu.VMEM((CH * CK, LN), F32), pltpu.VMEM((LN, LN), F32)],
        name="outputs",
        plain_spec=VMEM,
        limit=8,
    )


def exchange(values):
    return lax.all_to_all(values, "tm", split_axis=0, concat_axis=0, tiled=True)


def shards(
    signal,
    cotangent,
    log_step,
    damping,
    frequency,
    coef_re,
    coef_im,
    skip_gain,
    mix_weight,
    embed_table,
    diffusion_step,
):
    me = lax.axis_index("tm").reshape(1)
    group = lax.axis_index("chan").reshape(1)
    tables = dft_tables()

    def swap(values, mask):
        return lax.ppermute(values, "chan", [(i, i ^ mask) for i in range(4)])

    send1, own, sr, si, terms, wide = first(
        diffusion_step, signal, cotangent, mix_weight, log_step[None], (damping, frequency, coef_re, coef_im),
        skip_gain[None], embed_table.T,
    )
    got1 = exchange(send1)
    own, across = lax.optimization_barrier((own, swap(own, 2)))
    parts = (own, swap(own, 1), across, swap(across, 1))
    raw = (log_step[None], damping, frequency, coef_re, coef_im)
    out, far_r, far_i, step_r, step_i, pull = within(send1, terms, wide, raw)
    far = (far_r, far_i)
    steps = (step_r, step_i)
    send2, grad, mix, br, bi = second(
        me, group, parts, out, got1, send1, terms, wide, far, steps, sr, si
    )
    got2 = exchange(send2)
    mixes = [mix] + [swap(mix, m) for m in range(1, 4)]
    spec, column, turns = spectrum(me, got1, mix, wide, terms, tables)
    (send3,) = correlate(got2, spec, tables, column, turns, mixes)
    got3 = exchange(send3)
    (grad_signal,) = signal_grad(
        me, got2, grad, terms, wide, far, steps, br, bi, cotangent, send3
    )
    kernel, g_damping, g_frequency, g_re, g_im, g_size, g_skip, g_mix, g_table = outputs(
        diffusion_step, group, got3, pull, wide, embed_table.shape[0]
    )
    return (
        grad_signal,
        kernel,
        g_size[0],
        g_damping,
        g_frequency,
        g_re,
        g_im,
        g_skip[0],
        g_mix,
        g_table.T,
    )


def solution(mesh):
    placed = (
        P("chan", "tm"),
        P("chan", "tm"),
        P("chan"),
        P("chan", None),
        P("chan", None),
        P("chan", None),
        P("chan", None),
        P("chan"),
        P("chan", None),
        P(None, "chan"),
        P(),
    )
    return jax.shard_map(
        shards,
        mesh=mesh,
        in_specs=placed,
        out_specs=(
            P("chan", "tm"),
            P("chan", "tm"),
            P("chan"),
            P("chan", None),
            P("chan", None),
            P("chan", None),
            P("chan", None),
            P("chan"),
            P("chan", None),
            P(None, "chan"),
        ),
        check_vma=False,
    )
```
